32 devices in a mesh: dp: 16 (over z, x, core), tensor: 2 (over y).
Axes of the slice: x: 2, y: 2, z: 4, core: 2. Of those that a mesh axis runs over, the one named last changes fastest.
Arguments:
- frames: bfloat16 [14336, 1024], P('dp'), may hold values from -6 to 6
- lengths: int32 [16], P('dp'), may hold values from 448 to 896, as said below
- span_starts: int32 [16, 58], P('dp'), may hold values from 0 to 886
- mask_embedding: bfloat16 [1024], replicated, may hold values from -6 to 6
- norm1_gain: bfloat16 [1024], replicated, may hold values from 0.5 to 1.5
- norm1_bias: bfloat16 [1024], replicated, may hold values from -1.796875 to 1.796875
- qkv_weight: bfloat16 [1024, 3, 1024], P(None, None, 'tensor'), may hold values from -0.25 to 0.25
- qv_bias: bfloat16 [2, 1024], P(None, 'tensor'), may hold values from -1.796875 to 1.796875
- out_weight: bfloat16 [1024, 1024], P('tensor'), may hold values from -0.75 to 0.75
- out_bias: bfloat16 [1024], replicated, may hold values from -1.796875 to 1.796875
- norm2_gain: bfloat16 [1024], replicated, may hold values from 0.5 to 1.5
- norm2_bias: bfloat16 [1024], replicated, may hold values from -1.796875 to 1.796875
- up_weight: bfloat16 [1024, 4096], P(None, 'tensor'), may hold values from -0.1875 to 0.1875
- up_bias: bfloat16 [4096], P('tensor'), may hold values from -1.796875 to 1.796875
- down_weight: bfloat16 [4096, 1024], P('tensor'), may hold values from -0.09375 to 0.09375
- down_bias: bfloat16 [1024], replicated, may hold values from -1.796875 to 1.796875
- head_weight: bfloat16 [1024, 32], replicated, may hold values from -0.1875 to 0.1875
- head_bias: bfloat16 [32], replicated, may hold values from -1.796875 to 1.796875
- logit_grad: bfloat16 [14336, 32], P('dp'), may hold values from -6 to 6
Outputs:
- logits: float32 [14336, 32], P('dp')
- frames_grad: float32 [14336, 1024], P('dp')
- mask_grad: float32 [1024], replicated
- norm1_gain_grad: float32 [1024], replicated
- norm1_bias_grad: float32 [1024], replicated
- qkv_grad: float32 [1024, 3, 1024], P(None, None, 'tensor')
- qv_bias_grad: float32 [2, 1024], P(None, 'tensor')
- out_grad: float32 [1024, 1024], P('tensor')
- out_bias_grad: float32 [1024], replicated
- norm2_gain_grad: float32 [1024], replicated
- norm2_bias_grad: float32 [1024], replicated
- up_grad: float32 [1024, 4096], P(None, 'tensor')
- up_bias_grad: float32 [4096], P('tensor')
- down_grad: float32 [4096, 1024], P('tensor')
- down_bias_grad: float32 [1024], replicated
- head_grad: float32 [1024, 32], replicated
- head_bias_grad: float32 [32], replicated
The draws below stay inside these ranges and needn't reach their ends.
Inputs may be any that keep to these rules, and one draw needn't show every extreme that they name: Frames 0 to lengths - 1 of an utterance are valid; some utterance has all 896 frames valid.
All inputs are finite; a program needn't handle non-finite values.
Results may differ from the reference program's by a relative error of at most 0.02.
Values may be sent and summed in bfloat16 or wider, within the bound.
A program may use at most 256 MiB of HBM per device.

```python
import jax
import jax.numpy as jnp
from jax import lax

D = 1024
HEADS = 16
FF = 4096
V = 32
HEAD_DIM = 64
LEN = 896
SPANS = 58
MASK_SPAN = 10
UTTERANCES = 16
TOKENS = 14336


def draw_lengths(key, part):
    key = jax.random.fold_in(key, 11)
    first_key, second_key = jax.random.split(key)
    drawn = jax.random.randint(first_key, (UTTERANCES,), LEN // 2, LEN + 1)
    chosen = jax.random.randint(second_key, (), 0, UTTERANCES)
    return jnp.where(jnp.arange(UTTERANCES) == chosen, LEN, drawn).astype(jnp.int32)


def set_ends(values, key, smallest, high):
    longest = values.shape.index(max(values.shape))
    spots = []
    for shift in (0, 1):
        where = [jax.random.randint(jax.random.fold_in(key, axis), (), 0, length) for axis, length in enumerate(values.shape)]
        where[longest] = (where[longest] + shift) % values.shape[longest]
        spots.append(tuple(where))
    return values.at[spots[0]].set(smallest).at[spots[1]].set(high)


def levels(rng, extent, cuts, low, largest):
    level, own = 1.0, jax.random.fold_in(rng, 6)
    for position, blocks in cuts:
        heights = jnp.exp(jax.random.uniform(jax.random.fold_in(own, position), (blocks,), jnp.float32, low / len(cuts), largest / len(cuts)))
        level = level * jnp.repeat(heights, extent[position] // blocks).reshape([-1 if axis == position else 1 for axis in range(len(extent))])
    return level


def bell_draw(key, shape, scale, limit, pieces=(), kind=jnp.bfloat16):
    array = scale * jax.random.normal(key, shape, jnp.float32)
    if pieces:
        array = array * levels(key, shape, pieces, -0.22, 0.18)
    return jnp.clip(array, -limit, limit).astype(kind)


def setup_inputs(seed: int = 0) -> dict:
    arg_keys = jax.random.split(jax.random.key(seed), 20)
    frames = bell_draw(arg_keys[0], (TOKENS, D), 1.0, 6.0, ((0, 16),))
    lengths = draw_lengths(jax.random.fold_in(arg_keys[19], 71), 0)
    span_starts = set_ends(jax.random.randint(arg_keys[2], (UTTERANCES, SPANS), 0, LEN - MASK_SPAN + 1), jax.random.fold_in(arg_keys[2], 1), 0, LEN - MASK_SPAN).astype(jnp.int32)
    mask_embedding = bell_draw(arg_keys[3], (D,), 1.0, 6.0)
    norm1_gain = jnp.clip(1.0 + 0.1 * jax.random.normal(arg_keys[4], (D,), jnp.float32), 0.5, 1.5).astype(jnp.bfloat16)
    norm1_bias = bell_draw(arg_keys[5], (D,), 0.3, 1.796875)
    qkv_weight = bell_draw(arg_keys[6], (D, 3, D), (D // 2) ** -0.5, 0.25, ((2, 2),))
    qv_bias = bell_draw(arg_keys[7], (2, D), 0.3, 1.796875, ((1, 2),))
    out_weight = bell_draw(arg_keys[8], (D, D), (D // 16) ** -0.5, 0.75, ((0, 2),))
    out_bias = bell_draw(arg_keys[9], (D,), 0.3, 1.796875)
    norm2_gain = jnp.clip(1.0 + 0.1 * jax.random.normal(arg_keys[10], (D,), jnp.float32), 0.5, 1.5).astype(jnp.bfloat16)
    norm2_bias = bell_draw(arg_keys[11], (D,), 0.3, 1.796875)
    up_weight = bell_draw(arg_keys[12], (D, FF), D ** -0.5, 0.1875, ((1, 2),))
    up_bias = bell_draw(arg_keys[13], (FF,), 0.3, 1.796875, ((0, 2),))
    down_weight = bell_draw(arg_keys[14], (FF, D), FF ** -0.5, 0.09375, ((0, 2),))
    down_bias = bell_draw(arg_keys[15], (D,), 0.3, 1.796875)
    head_weight = bell_draw(arg_keys[16], (D, V), D ** -0.5, 0.1875)
    head_bias = bell_draw(arg_keys[17], (V,), 0.3, 1.796875)
    logit_grad = bell_draw(arg_keys[18], (TOKENS, V), 1.0, 6.0, ((0, 16),))
    return dict(frames=frames, lengths=lengths, span_starts=span_starts, mask_embedding=mask_embedding, norm1_gain=norm1_gain, norm1_bias=norm1_bias, qkv_weight=qkv_weight, qv_bias=qv_bias, out_weight=out_weight, out_bias=out_bias, norm2_gain=norm2_gain, norm2_bias=norm2_bias, up_weight=up_weight, up_bias=up_bias, down_weight=down_weight, down_bias=down_bias, head_weight=head_weight, head_bias=head_bias, logit_grad=logit_grad)


EPS = 1e-05
NEG = -1e+30
PRECISE = lax.Precision.HIGHEST

@jax.custom_vjp
def low(v):
    return lax.optimization_barrier(v.astype(jnp.bfloat16)).astype(jnp.float32)

@jax.custom_vjp
def low_back(v):
    return v

def low_keep(v):
    return (low(v), None)

def low_pass(kept, grad):
    return (grad,)

def back_keep(v):
    return (v, None)

def back_low(kept, grad):
    return (low(grad),)
low.defvjp(low_keep, low_pass)
low_back.defvjp(back_keep, back_low)

def layer_norm(row_block, gain, shift):
    center = row_block - lax.optimization_barrier(jnp.mean(row_block, axis=-1, keepdims=True))
    spread = lax.optimization_barrier(jnp.mean(center * center, axis=-1, keepdims=True))
    return center * lax.rsqrt(spread + EPS) * gain + shift

def attend(packed):
    queries, key_rows, values, key_valid = packed
    factor = HEAD_DIM ** (-0.5)
    scores = jnp.einsum('qhd,khd->hqk', queries, key_rows, precision=PRECISE) * factor
    scores = low_back(scores)
    scores = jnp.where(key_valid[None, None, :], scores, NEG)
    prob_rows = jax.nn.softmax(scores, axis=-1)
    return jnp.einsum('hqk,khd->qhd', low(prob_rows), values, precision=PRECISE)

def reference(frames, lengths, span_starts, mask_embedding, norm1_gain, norm1_bias, qkv_weight, qv_bias, out_weight, out_bias, norm2_gain, norm2_bias, up_weight, up_bias, down_weight, down_bias, head_weight, head_bias, logit_grad):
    places = jnp.arange(LEN, dtype=jnp.int32)
    covered = (places[None, None, :] >= span_starts[:, :, None]) & (places[None, None, :] < span_starts[:, :, None] + MASK_SPAN)
    masked = jnp.any(covered, axis=1).reshape(TOKENS, 1)
    key_valid = places[None, :] < lengths[:, None]
    params = tuple((item.astype(jnp.float32) for item in (frames, mask_embedding, norm1_gain, norm1_bias, qkv_weight, qv_bias, out_weight, out_bias, norm2_gain, norm2_bias, up_weight, up_bias, down_weight, down_bias, head_weight, head_bias)))

    def forward(frame_rows, mask_row, gain_one, shift_one, qkv_matrix, qv_shift, out_matrix, out_shift, gain_two, shift_two, up_matrix, up_shift, down_matrix, down_shift, head_matrix, head_shift):
        filled = jnp.where(masked, mask_row[None, :], frame_rows)
        first_norm = low(layer_norm(filled, gain_one, shift_one))
        projected = jnp.dot(first_norm, qkv_matrix.reshape(D, 3 * D), precision=PRECISE)
        queries = low(low_back(projected[:, :D] + qv_shift[0]))
        key_rows = low(low_back(projected[:, D:2 * D]))
        values = low(low_back(projected[:, 2 * D:] + qv_shift[1]))
        shape_four = (UTTERANCES, LEN, HEADS, HEAD_DIM)
        mixture = lax.map(jax.checkpoint(attend), (queries.reshape(shape_four), key_rows.reshape(shape_four), values.reshape(shape_four), key_valid))
        mixture = low(low_back(mixture.reshape(TOKENS, D)))
        hidden = filled + low_back(jnp.dot(mixture, out_matrix, precision=PRECISE) + out_shift)
        second_norm = low(layer_norm(hidden, gain_two, shift_two))
        up_rows = low_back(jnp.dot(second_norm, up_matrix, precision=PRECISE) + up_shift)
        activ = low(jax.nn.gelu(up_rows, approximate=False))
        output = hidden + low_back(jnp.dot(activ, down_matrix, precision=PRECISE) + down_shift)
        return jnp.dot(low(output), head_matrix, precision=PRECISE) + head_shift
    logits, pullback = jax.vjp(forward, *params)
    grads = pullback(logit_grad.astype(jnp.float32))
    return (logits, grads[0], grads[1], grads[2], grads[3], grads[4], grads[5], grads[6], grads[7], grads[8], grads[9], grads[10], grads[11], grads[12], grads[13], grads[14], grads[15])
```

```python
from functools import partial

import jax
import jax.numpy as jnp
from jax import lax
from jax.sharding import PartitionSpec as P

HEAD_DIM = 64
MASK_SPAN = 10


EPS = 1e-05
NEG = -1e30


def norm_stats(row_block, gain, shift):
    center = row_block - jnp.mean(row_block, axis=-1, keepdims=True)
    spread = jnp.mean(center * center, axis=-1, keepdims=True)
    inverse = lax.rsqrt(spread + EPS)
    unit_rows = center * inverse
    return (unit_rows * gain + shift, unit_rows, inverse)


def norm_back(grad_rows, unit_rows, inverse, gain):
    grad_unit = grad_rows * gain
    first_mean = jnp.mean(grad_unit, axis=-1, keepdims=True)
    second_mean = jnp.mean(grad_unit * unit_rows, axis=-1, keepdims=True)
    return inverse * (grad_unit - first_mean - unit_rows * second_mean)


def masked_scores(queries, key_rows, key_valid):
    factor = HEAD_DIM ** (-0.5)
    scores = (
        jnp.einsum("qhd,khd->hqk", queries, key_rows, preferred_element_type=jnp.float32) * factor
    )
    return jnp.where(key_valid[None, None, :], scores, NEG)


def attend_forward(packed):
    queries, key_rows, values, key_valid = packed
    scores = masked_scores(queries, key_rows, key_valid)
    row_peak = jnp.max(scores, axis=-1, keepdims=True)
    exp_scores = jnp.exp(scores - row_peak)
    row_total = jnp.sum(exp_scores, axis=-1, keepdims=True)
    prob_rows = (exp_scores / row_total).astype(jnp.bfloat16)
    mixture = jnp.einsum("hqk,khd->qhd", prob_rows, values, preferred_element_type=jnp.float32)
    return (mixture, row_peak + jnp.log(row_total))


def attend_backward(packed):
    queries, key_rows, values, key_valid, log_total, grad_mixture = packed
    factor = HEAD_DIM ** (-0.5)
    scores = masked_scores(queries, key_rows, key_valid)
    prob_rows = jnp.exp(scores - log_total)
    grad_values = jnp.einsum(
        "hqk,qhd->khd",
        prob_rows.astype(jnp.bfloat16),
        grad_mixture,
        preferred_element_type=jnp.float32,
    )
    grad_probs = jnp.einsum(
        "qhd,khd->hqk", grad_mixture, values, preferred_element_type=jnp.float32
    )
    row_dot = jnp.sum(prob_rows * grad_probs, axis=-1, keepdims=True)
    grad_scores = (prob_rows * (grad_probs - row_dot)).astype(jnp.bfloat16)
    grad_queries = (
        jnp.einsum("hqk,khd->qhd", grad_scores, key_rows, preferred_element_type=jnp.float32)
        * factor
    )
    grad_keys = (
        jnp.einsum("hqk,qhd->khd", grad_scores, queries, preferred_element_type=jnp.float32)
        * factor
    )
    return (grad_queries, grad_keys, grad_values)


def local(
    frames,
    lengths,
    span_starts,
    mask_embedding,
    norm1_gain,
    norm1_bias,
    qkv_weight,
    qv_bias,
    out_weight,
    out_bias,
    norm2_gain,
    norm2_bias,
    up_weight,
    up_bias,
    down_weight,
    down_bias,
    head_weight,
    head_bias,
    logit_grad,
):
    utterances_here, span_count = span_starts.shape
    row_count, model_width = frames.shape
    frame_count = row_count // utterances_here
    local_width = qkv_weight.shape[2]
    heads_here = local_width // HEAD_DIM
    f32, bf16 = jnp.float32, jnp.bfloat16
    first_share = lax.axis_index("tensor") == 0

    def mm(spec, left, right):
        return jnp.einsum(spec, left, right, preferred_element_type=f32)

    def split(wide):
        high = wide.astype(bf16)
        return jnp.concatenate([high, (wide - high.astype(f32)).astype(bf16)], axis=-1)

    places = jnp.arange(frame_count, dtype=jnp.int32)
    covered = (places[None, None, :] >= span_starts[:, :, None]) & (
        places[None, None, :] < span_starts[:, :, None] + MASK_SPAN
    )
    masked = jnp.any(covered, axis=1).reshape(row_count, 1)
    key_valid = places[None, :] < lengths[:, None]
    gain_one = norm1_gain.astype(f32)
    gain_two = norm2_gain.astype(f32)
    filled = jnp.where(masked, mask_embedding.astype(f32)[None, :], frames.astype(f32))
    first_norm, first_unit, first_inverse = norm_stats(filled, gain_one, norm1_bias.astype(f32))
    first_low = first_norm.astype(bf16)
    weight_flat = qkv_weight.reshape(model_width, 3 * local_width)
    bias_full = jnp.stack(
        [qv_bias[0].astype(f32), jnp.zeros((local_width,), f32), qv_bias[1].astype(f32)]
    ).reshape(3 * local_width)
    projected = (mm("rd,dc->rc", first_low, weight_flat) + bias_full).astype(bf16)
    triple = projected.reshape(utterances_here, frame_count, 3, heads_here, HEAD_DIM)
    queries = triple[:, :, 0]
    key_rows = triple[:, :, 1]
    values = triple[:, :, 2]
    mixture, log_total = lax.map(attend_forward, (queries, key_rows, values, key_valid))
    mixture_low = mixture.astype(bf16).reshape(row_count, local_width)
    mixture_all = lax.all_gather(mixture_low, "tensor", axis=1, tiled=True)
    out_all = lax.all_gather(out_weight, "tensor", axis=0, tiled=True)
    hidden = filled + mm("rl,ld->rd", mixture_all, out_all) + out_bias.astype(f32)
    second_norm, second_unit, second_inverse = norm_stats(hidden, gain_two, norm2_bias.astype(f32))
    second_low = second_norm.astype(bf16)
    up_rows = mm("rd,df->rf", second_low, up_weight) + up_bias.astype(f32)
    activ, gelu_pull = jax.vjp(partial(jax.nn.gelu, approximate=False), up_rows)
    activ_low = activ.astype(bf16)
    down_head = split(mm("fd,dv->fv", down_weight, head_weight))
    characters = head_weight.shape[1]
    own_logits = mm("rf,fv->rv", activ_low, down_head)
    own_logits = own_logits[:, :characters] + own_logits[:, characters:]
    hidden_down = (hidden + down_bias.astype(f32)).astype(bf16)
    logits = (
        lax.psum(own_logits, "tensor")
        + mm("rd,dv->rv", hidden_down, head_weight)
        + head_bias.astype(f32)
    )
    twice = jnp.concatenate([logit_grad, logit_grad], axis=1)
    grad_activ = mm("rv,fv->rf", twice, down_head)
    grad_up = gelu_pull(grad_activ)[0].astype(bf16)
    activ_head = mm("rf,rv->fv", activ_low, logit_grad)
    hidden_head = mm("rd,rv->dv", hidden_down, logit_grad)
    head_bias_grad = jnp.sum(logit_grad.astype(f32), axis=0)
    up_grad = mm("rd,rf->df", second_low, grad_up)
    up_bias_grad = jnp.sum(grad_up.astype(f32), axis=0)
    grad_second = mm("rf,df->rd", grad_up, up_weight)
    norm2_gain_grad = jnp.sum(grad_second * second_unit, axis=0)
    norm2_bias_grad = jnp.sum(grad_second, axis=0)
    grad_output = mm("rv,dv->rd", logit_grad, head_weight)
    grad_hidden = norm_back(grad_second, second_unit, second_inverse, gain_two) + jnp.where(
        first_share, grad_output, 0.0
    )
    grad_attn = grad_hidden.astype(bf16)
    out_bias_grad = jnp.sum(grad_hidden, axis=0)
    grad_mixture = lax.psum_scatter(
        mm("rd,ld->rl", grad_attn, out_all).astype(bf16), "tensor", scatter_dimension=1, tiled=True
    )
    out_grad = lax.psum_scatter(
        mm("rl,rd->ld", mixture_all, grad_attn).astype(bf16),
        "tensor",
        scatter_dimension=0,
        tiled=True,
    )
    grad_mixture = grad_mixture.reshape(utterances_here, frame_count, heads_here, HEAD_DIM)
    grad_queries, grad_keys, grad_values = lax.map(
        attend_backward, (queries, key_rows, values, key_valid, log_total, grad_mixture)
    )
    grad_triple = (
        jnp.stack([grad_queries, grad_keys, grad_values], axis=2)
        .astype(bf16)
        .reshape(row_count, 3 * local_width)
    )
    qkv_grad = mm("rd,rc->dc", first_low, grad_triple).reshape(model_width, 3, local_width)
    column_sums = jnp.sum(grad_triple.astype(f32), axis=0).reshape(3, local_width)
    qv_bias_grad = jnp.stack([column_sums[0], column_sums[2]])
    grad_first = mm("rc,dc->rd", grad_triple, weight_flat)
    norm1_gain_grad = jnp.sum(grad_first * first_unit, axis=0)
    norm1_bias_grad = jnp.sum(grad_first, axis=0)
    grad_filled = grad_hidden + norm_back(grad_first, first_unit, first_inverse, gain_one)
    mask_grad = jnp.sum(jnp.where(masked, grad_filled, 0.0), axis=0)
    frames_grad = jnp.where(masked, 0.0, grad_filled).astype(bf16)
    frames_grad = lax.all_gather(
        lax.psum_scatter(frames_grad, "tensor", scatter_dimension=0, tiled=True),
        "tensor",
        axis=0,
        tiled=True,
    ).astype(f32)
    up_grad = lax.psum(up_grad.astype(bf16), "dp").astype(f32)
    out_grad = lax.psum(out_grad, "dp").astype(f32)
    qkv_grad = lax.psum(qkv_grad.astype(bf16), "dp").astype(f32)
    activ_head, up_bias_grad, qv_bias_grad, head_bias_grad, hidden_head = lax.psum(
        (activ_head, up_bias_grad, qv_bias_grad, head_bias_grad, hidden_head), "dp"
    )
    activ_split = split(activ_head)
    head_twice = jnp.concatenate([head_weight, head_weight], axis=1)
    down_grad = mm("fv,dv->fd", activ_split, head_twice)
    down_head_grad = mm("fd,fv->dv", down_weight, activ_split)
    down_head_grad = down_head_grad[:, :characters] + down_head_grad[:, characters:]
    down_bias_grad = jnp.dot(
        head_weight.astype(f32), head_bias_grad, precision=lax.Precision.HIGHEST
    )
    mask_grad, norm1_gain_grad, norm1_bias_grad, norm2_gain_grad, norm2_bias_grad, out_bias_grad = (
        lax.psum(
            (
                mask_grad,
                norm1_gain_grad,
                norm1_bias_grad,
                norm2_gain_grad,
                norm2_bias_grad,
                out_bias_grad,
            ),
            ("dp", "tensor"),
        )
    )
    head_grad = hidden_head + lax.psum(down_head_grad, "tensor")
    return (
        logits,
        frames_grad,
        mask_grad,
        norm1_gain_grad,
        norm1_bias_grad,
        qkv_grad,
        qv_bias_grad,
        out_grad,
        out_bias_grad,
        norm2_gain_grad,
        norm2_bias_grad,
        up_grad,
        up_bias_grad,
        down_grad,
        down_bias_grad,
        head_grad,
        head_bias_grad,
    )


def solution(mesh):
    placed = (
        P("dp", None),
        P("dp"),
        P("dp", None),
        P(),
        P(),
        P(),
        P(None, None, "tensor"),
        P(None, "tensor"),
        P("tensor", None),
        P(),
        P(),
        P(),
        P(None, "tensor"),
        P("tensor"),
        P("tensor", None),
        P(),
        P(),
        P(),
        P("dp", None),
    )
    return jax.shard_map(
        local,
        mesh=mesh,
        in_specs=placed,
        out_specs=(
            P("dp", None),
            P("dp", None),
            P(),
            P(),
            P(),
            P(None, None, "tensor"),
            P(None, "tensor"),
            P("tensor", None),
            P(),
            P(),
            P(),
            P(None, "tensor"),
            P("tensor"),
            P("tensor", None),
            P(),
            P(),
            P(),
        ),
        check_vma=False,
    )
```

```python
from functools import partial
from types import SimpleNamespace

import jax
import jax.numpy as jnp
from jax import lax
from jax.experimental import pallas as pl
from jax.experimental.pallas import tpu as pltpu
from jax.sharding import PartitionSpec as P

HEAD_DIM = 64
MASK_SPAN = 10


EPS = 1e-05
NEG = -1e30


def norm_stats(row_block, gain, shift):
    center = row_block - jnp.mean(row_block, axis=-1, keepdims=True)
    spread = jnp.mean(center * center, axis=-1, keepdims=True)
    inverse = lax.rsqrt(spread + EPS)
    unit_rows = center * inverse
    return (unit_rows * gain + shift, unit_rows, inverse)


def norm_back(grad_rows, unit_rows, inverse, gain):
    grad_unit = grad_rows * gain
    first_mean = jnp.mean(grad_unit, axis=-1, keepdims=True)
    second_mean = jnp.mean(grad_unit * unit_rows, axis=-1, keepdims=True)
    return inverse * (grad_unit - first_mean - unit_rows * second_mean)


def masked_scores(queries, key_rows, key_valid):
    factor = HEAD_DIM ** (-0.5)
    scores = (
        jnp.einsum("qhd,khd->hqk", queries, key_rows, preferred_element_type=jnp.float32) * factor
    )
    return jnp.where(key_valid[None, None, :], scores, NEG)


def attend_forward(packed):
    queries, key_rows, values, key_valid = packed
    scores = masked_scores(queries, key_rows, key_valid)
    row_peak = jnp.max(scores, axis=-1, keepdims=True)
    exp_scores = jnp.exp(scores - row_peak)
    row_total = jnp.sum(exp_scores, axis=-1, keepdims=True)
    prob_rows = (exp_scores / row_total).astype(jnp.bfloat16)
    mixture = jnp.einsum("hqk,khd->qhd", prob_rows, values, preferred_element_type=jnp.float32)
    return (mixture, row_peak + jnp.log(row_total))


def attend_backward(packed):
    queries, key_rows, values, key_valid, log_total, grad_mixture = packed
    factor = HEAD_DIM ** (-0.5)
    scores = masked_scores(queries, key_rows, key_valid)
    prob_rows = jnp.exp(scores - log_total)
    grad_values = jnp.einsum(
        "hqk,qhd->khd",
        prob_rows.astype(jnp.bfloat16),
        grad_mixture,
        preferred_element_type=jnp.float32,
    )
    grad_probs = jnp.einsum(
        "qhd,khd->hqk", grad_mixture, values, preferred_element_type=jnp.float32
    )
    row_dot = jnp.sum(prob_rows * grad_probs, axis=-1, keepdims=True)
    grad_scores = (prob_rows * (grad_probs - row_dot)).astype(jnp.bfloat16)
    grad_queries = (
        jnp.einsum("hqk,khd->qhd", grad_scores, key_rows, preferred_element_type=jnp.float32)
        * factor
    )
    grad_keys = (
        jnp.einsum("hqk,qhd->khd", grad_scores, queries, preferred_element_type=jnp.float32)
        * factor
    )
    return (grad_queries, grad_keys, grad_values)


def local(
    frames,
    lengths,
    span_starts,
    mask_embedding,
    norm1_gain,
    norm1_bias,
    qkv_weight,
    qv_bias,
    out_weight,
    out_bias,
    norm2_gain,
    norm2_bias,
    up_weight,
    up_bias,
    down_weight,
    down_bias,
    head_weight,
    head_bias,
    logit_grad,
):
    utterances_here, span_count = span_starts.shape
    row_count, model_width = frames.shape
    frame_count = row_count // utterances_here
    local_width = qkv_weight.shape[2]
    heads_here = local_width // HEAD_DIM
    f32, bf16 = jnp.float32, jnp.bfloat16
    first_share = lax.axis_index("tensor") == 0

    def mm(spec, left, right):
        return jnp.einsum(spec, left, right, preferred_element_type=f32)

    def split(wide):
        high = wide.astype(bf16)
        return jnp.concatenate([high, (wide - high.astype(f32)).astype(bf16)], axis=-1)

    places = jnp.arange(frame_count, dtype=jnp.int32)
    covered = (places[None, None, :] >= span_starts[:, :, None]) & (
        places[None, None, :] < span_starts[:, :, None] + MASK_SPAN
    )
    masked = jnp.any(covered, axis=1).reshape(row_count, 1)
    key_valid = places[None, :] < lengths[:, None]
    gain_one = norm1_gain.astype(f32)
    gain_two = norm2_gain.astype(f32)
    filled = jnp.where(masked, mask_embedding.astype(f32)[None, :], frames.astype(f32))
    first_norm, first_unit, first_inverse = norm_stats(filled, gain_one, norm1_bias.astype(f32))
    first_low = first_norm.astype(bf16)
    weight_flat = qkv_weight.reshape(model_width, 3 * local_width)
    bias_full = jnp.stack(
        [qv_bias[0].astype(f32), jnp.zeros((local_width,), f32), qv_bias[1].astype(f32)]
    ).reshape(3 * local_width)
    projected = (mm("rd,dc->rc", first_low, weight_flat) + bias_full).astype(bf16)
    triple = projected.reshape(utterances_here, frame_count, 3, heads_here, HEAD_DIM)
    queries = triple[:, :, 0]
    key_rows = triple[:, :, 1]
    values = triple[:, :, 2]
    mixture, log_total = lax.map(attend_forward, (queries, key_rows, values, key_valid))
    mixture_low = mixture.astype(bf16).reshape(row_count, local_width)
    mixture_all = lax.all_gather(mixture_low, "tensor", axis=1, tiled=True)
    out_all = lax.all_gather(out_weight, "tensor", axis=0, tiled=True)
    hidden = filled + mm("rl,ld->rd", mixture_all, out_all) + out_bias.astype(f32)
    second_norm, second_unit, second_inverse = norm_stats(hidden, gain_two, norm2_bias.astype(f32))
    second_low = second_norm.astype(bf16)
    up_rows = mm("rd,df->rf", second_low, up_weight) + up_bias.astype(f32)
    activ, gelu_pull = jax.vjp(partial(jax.nn.gelu, approximate=False), up_rows)
    activ_low = activ.astype(bf16)
    down_head = split(mm("fd,dv->fv", down_weight, head_weight))
    characters = head_weight.shape[1]
    own_logits = mm("rf,fv->rv", activ_low, down_head)
    own_logits = own_logits[:, :characters] + own_logits[:, characters:]
    hidden_down = (hidden + down_bias.astype(f32)).astype(bf16)
    logits = (
        lax.psum(own_logits, "tensor")
        + mm("rd,dv->rv", hidden_down, head_weight)
        + head_bias.astype(f32)
    )
    twice = jnp.concatenate([logit_grad, logit_grad], axis=1)
    grad_activ = mm("rv,fv->rf", twice, down_head)
    grad_up = gelu_pull(grad_activ)[0].astype(bf16)
    activ_head = mm("rf,rv->fv", activ_low, logit_grad)
    hidden_head = mm("rd,rv->dv", hidden_down, logit_grad)
    head_bias_grad = jnp.sum(logit_grad.astype(f32), axis=0)
    up_grad = mm("rd,rf->df", second_low, grad_up)
    up_bias_grad = jnp.sum(grad_up.astype(f32), axis=0)
    grad_second = mm("rf,df->rd", grad_up, up_weight)
    norm2_gain_grad = jnp.sum(grad_second * second_unit, axis=0)
    norm2_bias_grad = jnp.sum(grad_second, axis=0)
    grad_output = mm("rv,dv->rd", logit_grad, head_weight)
    grad_hidden = norm_back(grad_second, second_unit, second_inverse, gain_two) + jnp.where(
        first_share, grad_output, 0.0
    )
    grad_attn = grad_hidden.astype(bf16)
    out_bias_grad = jnp.sum(grad_hidden, axis=0)
    grad_mixture = lax.psum_scatter(
        mm("rd,ld->rl", grad_attn, out_all).astype(bf16), "tensor", scatter_dimension=1, tiled=True
    )
    out_grad = lax.psum_scatter(
        mm("rl,rd->ld", mixture_all, grad_attn).astype(bf16),
        "tensor",
        scatter_dimension=0,
        tiled=True,
    )
    grad_mixture = grad_mixture.reshape(utterances_here, frame_count, heads_here, HEAD_DIM)
    grad_queries, grad_keys, grad_values = lax.map(
        attend_backward, (queries, key_rows, values, key_valid, log_total, grad_mixture)
    )
    grad_triple = (
        jnp.stack([grad_queries, grad_keys, grad_values], axis=2)
        .astype(bf16)
        .reshape(row_count, 3 * local_width)
    )
    qkv_grad = mm("rd,rc->dc", first_low, grad_triple).reshape(model_width, 3, local_width)
    column_sums = jnp.sum(grad_triple.astype(f32), axis=0).reshape(3, local_width)
    qv_bias_grad = jnp.stack([column_sums[0], column_sums[2]])
    grad_first = mm("rc,dc->rd", grad_triple, weight_flat)
    norm1_gain_grad = jnp.sum(grad_first * first_unit, axis=0)
    norm1_bias_grad = jnp.sum(grad_first, axis=0)
    grad_filled = grad_hidden + norm_back(grad_first, first_unit, first_inverse, gain_one)
    mask_grad = jnp.sum(jnp.where(masked, grad_filled, 0.0), axis=0)
    frames_grad = jnp.where(masked, 0.0, grad_filled).astype(bf16)
    frames_grad = lax.all_gather(
        lax.psum_scatter(frames_grad, "tensor", scatter_dimension=0, tiled=True),
        "tensor",
        axis=0,
        tiled=True,
    ).astype(f32)
    up_grad = lax.psum(up_grad.astype(bf16), "dp").astype(f32)
    out_grad = lax.psum(out_grad, "dp").astype(f32)
    qkv_grad = lax.psum(qkv_grad.astype(bf16), "dp").astype(f32)
    activ_head, up_bias_grad, qv_bias_grad, head_bias_grad, hidden_head = lax.psum(
        (activ_head, up_bias_grad, qv_bias_grad, head_bias_grad, hidden_head), "dp"
    )
    activ_split = split(activ_head)
    head_twice = jnp.concatenate([head_weight, head_weight], axis=1)
    down_grad = mm("fv,dv->fd", activ_split, head_twice)
    down_head_grad = mm("fd,fv->dv", down_weight, activ_split)
    down_head_grad = down_head_grad[:, :characters] + down_head_grad[:, characters:]
    down_bias_grad = jnp.dot(
        head_weight.astype(f32), head_bias_grad, precision=lax.Precision.HIGHEST
    )
    mask_grad, norm1_gain_grad, norm1_bias_grad, norm2_gain_grad, norm2_bias_grad, out_bias_grad = (
        lax.psum(
            (
                mask_grad,
                norm1_gain_grad,
                norm1_bias_grad,
                norm2_gain_grad,
                norm2_bias_grad,
                out_bias_grad,
            ),
            ("dp", "tensor"),
        )
    )
    head_grad = hidden_head + lax.psum(down_head_grad, "tensor")
    return (
        logits,
        frames_grad,
        mask_grad,
        norm1_gain_grad,
        norm1_bias_grad,
        qkv_grad,
        qv_bias_grad,
        out_grad,
        out_bias_grad,
        norm2_gain_grad,
        norm2_bias_grad,
        up_grad,
        up_bias_grad,
        down_grad,
        down_bias_grad,
        head_grad,
        head_bias_grad,
    )


f32, bf16 = jnp.float32, jnp.bfloat16
WIDTH = 1024
LOCAL = 512
FFL = 2048
ROWS = 896
CHARS = 32
CHUNK = 224
KEYS = 224
QROWS = 224


def dot(left, right):
    return lax.dot_general(left, right, (((1,), (0,)), ((), ())), preferred_element_type=f32)


def dot_nt(left, right):
    return lax.dot_general(left, right, (((1,), (1,)), ((), ())), preferred_element_type=f32)


def dot_tn(left, right):
    return lax.dot_general(left, right, (((0,), (0,)), ((), ())), preferred_element_type=f32)


def aligned(start, size):
    return pl.ds(pl.multiple_of(start, size), size)


def col_sum(block):
    rows, width = block.shape
    return jnp.sum(jnp.sum(block.reshape(rows // 8, 8, width), axis=0), axis=0, keepdims=True)


def gelu_parts(block):
    bell = jnp.exp(block * block * -0.5)
    cdf = 0.5 + 0.5 * lax.erf(block * (0.5**0.5))
    return block * cdf, cdf + block * bell * 0.3989422804014327


INPUTS = (
    ("frames", None),
    ("lengths", "smem"),
    ("starts", "vmem"),
    ("vectors", "vmem"),
    ("qkv_w", None),
    ("out_w", None),
    ("up_w", None),
    ("down_w", None),
    ("head_w", "vmem"),
    ("head_b", "vmem"),
    ("logit_grad", "vmem"),
)
OUTPUTS = (
    ("logits", (ROWS, CHARS), f32, "vmem"),
    ("frames_grad", (ROWS, WIDTH), bf16, None),
    ("up_o", (WIDTH, FFL), bf16, None),
    ("out_o", (768, WIDTH), bf16, None),
    ("qkv_o", (WIDTH, 3 * LOCAL), bf16, None),
    ("tiny_o", (16, WIDTH), f32, "vmem"),
)
SCRATCH = (
    ("x", (ROWS, WIDTH), bf16),
    ("wqkv", (3, WIDTH, LOCAL), bf16),
    ("first", (ROWS, WIDTH), bf16),
    ("first_t", (WIDTH, ROWS), bf16),
    ("qkv", (3, ROWS, LOCAL), bf16),
    ("mix", (ROWS, WIDTH), bf16),
    ("ow", (WIDTH, WIDTH), bf16),
    ("upw", (WIDTH, FFL), bf16),
    ("big", (2 * WIDTH, WIDTH), bf16),
    ("lse", (4, ROWS, 128), f32),
    ("dh", (FFL, 128), bf16),
    ("hw2", (WIDTH, 128), bf16),
    ("hw1", (WIDTH, 128), bf16),
    ("gd", (ROWS, 128), bf16),
    ("lp", (ROWS, 128), f32),
    ("lpt", (CHARS, ROWS), f32),
    ("lpr", (CHARS, ROWS), f32),
    ("second", (ROWS, WIDTH), bf16),
    ("unit", (CHUNK, WIDTH), f32),
    ("gu", (ROWS, FFL), bf16),
    ("pb", (ROWS, WIDTH), bf16),
    ("pm_own", (ROWS, LOCAL), f32),
    ("pm_send", (ROWS, LOCAL), bf16),
    ("pm_recv", (ROWS, LOCAL), bf16),
    ("nt", (CHARS, FFL), f32),
    ("hh", (CHARS, WIDTH), f32),
    ("ub", (8, FFL), f32),
    ("cs", (16, WIDTH), f32),
    ("gqt", (128, ROWS), f32),
    ("turn", (WIDTH, ROWS), bf16),
    ("og", (768, WIDTH), bf16),
    ("og_send", (560, WIDTH), bf16),
    ("og_recv", (560, WIDTH), bf16),
    ("f_recv", (ROWS, WIDTH), bf16),
    ("ty", (2, 16, WIDTH), f32),
    ("tc", (16, WIDTH), f32),
    ("tx", (16, WIDTH), f32),
    ("tz", (4, 16, WIDTH), f32),
)
PARTS = (
    ("u0", "big", 1024, 1024, 0, 0, "up_o", 0),
    ("u1", "big", 1024, 1024, 1024, 0, "up_o", 1024),
    ("o", "og", 768, 1024, 0, 0, "out_o", 0),
    ("q0", "upw", 1024, 768, 0, 0, "qkv_o", 0),
    ("q1", "upw", 1024, 768, 0, 768, "qkv_o", 768),
)


class Sum:
    def __init__(self, k, part, base):
        name, src, rows, width, row0, col0, out, ocol0 = part
        self.k, self.rows, self.width = k, rows, width
        self.src, self.row0, self.col0 = getattr(k, src), row0, col0
        self.out, self.ocol0 = getattr(k, out), ocol0
        self.rc, self.rx, self.rz = (getattr(k, name + s) for s in ("_rc", "_rx", "_rz"))
        self.base = base
        self.half, self.quarter, self.piece = rows // 2, rows // 4, rows // 16
        self.b1 = k.c * self.half
        self.b2 = self.b1 + k.x_ * self.quarter
        self.b3 = self.b2 + k.z * self.piece

    def at(self, start, size):
        return self.src.at[aligned(self.row0 + start, size), pl.ds(self.col0, self.width)]

    def out_at(self, start, size):
        return self.out.at[aligned(start, size), pl.ds(self.ocol0, self.width)]

    def add(self, start, size, others):
        step = size if size <= 64 else 64

        def body(i, carry):
            rows = aligned(self.row0 + start + i * step, step)
            cols = pl.ds(self.col0, self.width)
            total = self.src[rows, cols].astype(f32)
            for other in others:
                total += other[aligned(i * step, step), :].astype(f32)
            self.src[rows, cols] = total.astype(bf16)
            return carry

        lax.fori_loop(0, size // step, body, 0)

    def core(self):
        k = self.k
        self.h_core = k.copy(self.base, self.at((1 - k.c) * self.half, self.half), self.rc, k.core_peer)
        self.h_core.start()

    def x(self):
        k = self.k
        self.h_core.wait()
        self.add(self.b1, self.half, [self.rc])
        self.h_x = k.copy(
            self.base + 1,
            self.at(self.b1 + (1 - k.x_) * self.quarter, self.quarter),
            self.rx,
            k.x_peer,
        )
        self.h_x.start()

    def spread(self):
        k = self.k
        self.h_x.wait()
        self.add(self.b2, self.quarter, [self.rx])
        self.h_z = []
        for s in range(1, 4):
            there = lax.rem(k.z + s, 4)
            handle = k.copy(
                self.base + 1 + s,
                self.at(self.b2 + there * self.piece, self.piece),
                self.rz.at[s - 1],
                k.z_peer(s),
            )
            handle.start()
            self.h_z.append(handle)

    def gather(self):
        k = self.k
        for handle in self.h_z:
            handle.wait()
        self.add(self.b3, self.piece, [self.rz.at[s] for s in range(3)])
        mine = self.out_at(self.b3, self.piece)
        self.h_own = pltpu.make_async_copy(self.at(self.b3, self.piece), mine, k.sem.at[self.base + 10])
        self.h_own.start()
        self.h_zg = []
        for s in range(1, 4):
            handle = k.copy(self.base + 4 + s, self.at(self.b3, self.piece), mine, k.z_peer(s))
            handle.start()
            self.h_zg.append(handle)

    def x_back(self):
        k = self.k
        self.h_own.wait()
        for handle in self.h_zg:
            handle.wait()
        block = self.out_at(self.b2, self.quarter)
        self.h_xg = k.copy(self.base + 8, block, block, k.x_peer)
        self.h_xg.start()

    def core_back(self):
        k = self.k
        self.h_xg.wait()
        block = self.out_at(self.b1, self.half)
        self.h_cg = k.copy(self.base + 9, block, block, k.core_peer)
        self.h_cg.start()

    def end(self):
        self.h_cg.wait()


SEM_LOCAL, SEM_OW, SEM_MIX, SEM_PM, SEM_OG, SEM_F, SEM_TINY, SEM_SUM = 0, 16, 20, 24, 28, 32, 36, 44
SEM_COUNT = SEM_SUM + 11 * len(PARTS)


def rest_shapes():
    shapes = []
    for name, _, rows, width, *_ in PARTS:
        shapes += [
            (name + "_rc", (rows // 2, width), bf16),
            (name + "_rx", (rows // 4, width), bf16),
            (name + "_rz", (3, rows // 16, width), bf16),
        ]
    return tuple(shapes)


def fused(names, *refs):
    k = SimpleNamespace(**dict(zip(names, refs)))
    place = lax.axis_index("dp")
    k.t = lax.axis_index("tensor")
    k.z, k.x_, k.c = place // 4, lax.rem(place // 2, 2), lax.rem(place, 2)
    k.core_peer = {"dp": place + 1 - 2 * k.c}
    k.x_peer = {"dp": place + 2 - 4 * k.x_}
    k.y_peer = {"tensor": 1 - k.t}
    k.z_peer = lambda s: {"dp": lax.rem(k.z + s, 4) * 4 + k.x_ * 2 + k.c}

    def copy(number, src, dst, device):
        return pltpu.make_async_remote_copy(
            src_ref=src,
            dst_ref=dst,
            send_sem=k.sem.at[number],
            recv_sem=k.rsem.at[number],
            device_id=device,
            device_id_type=pl.DeviceIdType.MESH,
        )

    k.copy = copy
    loads = {}
    mine = aligned(k.t * LOCAL, LOCAL)
    for number, (name, src, dst) in enumerate(
        (
            ("x", k.frames, k.x),
            ("wqkv", k.qkv_w, k.wqkv),
            ("ow", k.out_w, k.ow.at[mine, :]),
            ("big", k.down_w, k.big),
            ("upw", k.up_w, k.upw),
        )
    ):
        loads[name] = pltpu.make_async_copy(src, dst, k.sem.at[SEM_LOCAL + number])
        loads[name].start()
    barrier = pltpu.get_barrier_semaphore()
    peers = [k.core_peer, k.x_peer, k.y_peer, k.z_peer(1), k.z_peer(2), k.z_peer(3)]
    for peer in peers:
        pl.semaphore_signal(barrier, inc=1, device_id=peer, device_id_type=pl.DeviceIdType.MESH)
    pl.semaphore_wait(barrier, len(peers))

    emb, gain1, bias1, out_bias, gain2, bias2, down_bias = (
        k.vectors[i : i + 1, :] for i in range(7)
    )
    lane = lax.broadcasted_iota(jnp.int32, (1, 128), 1)
    first_share = jnp.where(k.t == 0, 1.0, 0.0).astype(f32)

    def filled_rows(start, size):
        ids = lax.broadcasted_iota(jnp.int32, (size, k.starts.shape[1]), 0) + start
        begin = k.starts[...]
        inside = jnp.where((ids >= begin) & (ids < begin + MASK_SPAN), 1.0, 0.0)
        column = jnp.max(inside, axis=1, keepdims=True)
        flag = jnp.broadcast_to(column, (size, WIDTH)) > 0.5
        return jnp.where(flag, emb, k.x[aligned(start, size), :].astype(f32)), flag

    loads["ow"].wait()
    own_half = k.ow.at[aligned(k.t * LOCAL + k.c * 256, 256), :]
    ow_y = k.copy(SEM_OW, own_half, own_half, k.y_peer)
    ow_y.start()

    loads["x"].wait()

    def ln1(i, carry):
        filled, _ = filled_rows(i * 128, 128)
        norm, _, _ = norm_stats(filled, gain1, bias1)
        k.first[aligned(i * 128, 128), :] = norm.astype(bf16)
        return carry

    lax.fori_loop(0, ROWS // 128, ln1, 0)
    loads["wqkv"].wait()
    for m in range(3):
        bias = None if m == 1 else k.vectors[7 + m // 2 : 8 + m // 2, 0:LOCAL]

        def project(i, carry, m=m, bias=bias):
            rows = aligned(i * CHUNK, CHUNK)
            value = dot(k.first[rows, :], k.wqkv[m])
            k.qkv[m, rows, :] = (value if bias is None else value + bias).astype(bf16)
            return carry

        lax.fori_loop(0, ROWS // CHUNK, project, 0)
    ow_y.wait()
    got = k.ow.at[aligned((1 - k.t) * LOCAL + k.c * 256, 256), :]
    ow_core = k.copy(SEM_OW + 1, got, got, k.core_peer)
    ow_core.start()

    key_bias = jnp.where(
        lax.broadcasted_iota(jnp.int32, (ROWS, 1), 0) < k.lengths[0], 0.0, NEG
    ).astype(f32)

    def pair_cols(p):
        return aligned(p * 128, 128)

    def mix_copy(p):
        strip = k.mix.at[:, aligned(k.t * LOCAL + p * 128, 128)]
        return k.copy(SEM_MIX + p, strip, strip, k.y_peer)

    def forward_pair(p, carry):
        cols = pair_cols(p)
        q_pair = k.qkv[0, :, cols].astype(f32) * HEAD_DIM ** (-0.5)
        k_pair = k.qkv[1, :, cols].astype(f32)
        v_pair = k.qkv[2, :, cols].astype(f32)
        for start in range(0, ROWS, QROWS):
            parts = []
            stats = []
            for h in range(2):
                half = (lane < 64) if h == 0 else (lane >= 64)
                extra = 64 if h == 0 else 0
                spot = lane == extra
                q_h = jnp.where(half, q_pair[start : start + QROWS], jnp.where(spot, 1.0, 0.0))
                k_h = jnp.where(half, k_pair, jnp.where(spot, key_bias, 0.0))
                v_h = jnp.where(half, v_pair, jnp.where(spot, 1.0, 0.0))
                scores = dot_nt(q_h.astype(bf16), k_h.astype(bf16))
                peak = jnp.max(scores, axis=1, keepdims=True)
                weights = jnp.exp(scores - peak).astype(bf16)
                both = dot(weights, v_h.astype(bf16))
                total = both[:, extra : extra + 1]
                parts.append(both / total)
                stats.append(peak + jnp.log(total))
            k.mix[start : start + QROWS, aligned(k.t * LOCAL + p * 128, 128)] = jnp.where(
                lane < 64, parts[0], parts[1]
            ).astype(bf16)
            k.lse[p, start : start + QROWS, :] = jnp.where(lane < 64, stats[0], stats[1])
        mix_copy(p).start()
        return carry

    lax.fori_loop(0, 4, forward_pair, 0)

    def turn_rows(src, dst):
        def body(i, carry):
            cols = aligned(i * 128, 128)
            dst[cols, :] = src[:, cols].T
            return carry

        lax.fori_loop(0, WIDTH // 128, body, 0)

    turn_rows(k.first, k.first_t)
    pick = lax.broadcasted_iota(jnp.int32, (CHARS, 128), 0)
    spot = lax.broadcasted_iota(jnp.int32, (CHARS, 128), 1)
    once = jnp.where(pick == spot, 1.0, 0.0).astype(bf16)
    twice = jnp.where((pick == spot) | (pick + CHARS == spot), 1.0, 0.0).astype(bf16)
    k.hw1[...] = dot(k.head_w[...], once).astype(bf16)
    k.hw2[...] = dot(k.head_w[...], twice).astype(bf16)
    k.gd[...] = dot(k.logit_grad[...], twice).astype(bf16)
    loads["big"].wait()

    def fold(i, carry):
        rows = aligned(i * 512, 512)
        value = dot(k.big[rows, :], k.hw2[...])
        high = value.astype(bf16).astype(f32)
        k.dh[rows, :] = jnp.where(lane < CHARS, high, value - high).astype(bf16)
        return carry

    lax.fori_loop(0, 4, fold, 0)
    k.nt[...] = jnp.zeros_like(k.nt)
    k.hh[...] = jnp.zeros_like(k.hh)
    k.ub[...] = jnp.zeros_like(k.ub)
    k.cs[...] = jnp.zeros_like(k.cs)
    ow_core.wait()
    loads["upw"].wait()

    def mix_wait(p, carry):
        mix_copy(p).wait()
        return carry

    lax.fori_loop(0, 4, mix_wait, 0)

    def pm_copy(i):
        rows = aligned(i * CHUNK, CHUNK)
        return k.copy(SEM_PM + i, k.pm_send.at[rows, :], k.pm_recv.at[rows, :], k.y_peer)

    def feed(i, carry):
        start = i * CHUNK
        rows = aligned(start, CHUNK)
        filled, _ = filled_rows(start, CHUNK)
        hidden = filled + dot(k.mix[rows, :], k.ow[...]) + out_bias
        second, unit, inverse = norm_stats(hidden, gain2, bias2)
        low = second.astype(bf16)
        k.second[rows, :] = low
        k.unit[...] = unit
        down = (hidden + down_bias).astype(bf16)
        grad = k.gd[rows, :]
        part = dot(down, k.hw1[...])
        k.hh[...] += dot_tn(grad, down)[:CHARS] * first_share
        head = part * 0.5
        for j in range(4):
            cols = pl.ds(j * 512, 512)
            up = dot(low, k.upw[:, cols]) + k.vectors[9 + j // 2 : 10 + j // 2, pl.ds((j % 2) * 512, 512)]
            act, slope = gelu_parts(up)
            act = act.astype(bf16)
            head += dot(act, k.dh[cols, :])
            k.nt[:, cols] += dot_tn(grad, act)[:CHARS]
            grad_up = (dot_nt(grad, k.dh[cols, :]) * slope).astype(bf16)
            k.gu[rows, cols] = grad_up
            k.ub[0:1, cols] += col_sum(grad_up.astype(f32))
        k.lp[rows, :] = head
        grad_second = dot_nt(k.gu[rows, :], k.upw[...])
        unit = k.unit[...]
        k.cs[3:4, :] += col_sum(grad_second * unit)
        k.cs[4:5, :] += col_sum(grad_second)
        spread = norm_back(grad_second, unit, inverse, gain2)
        spread += dot_nt(grad, k.hw1[...]) * first_share
        k.cs[5:6, :] += col_sum(spread)
        low = spread.astype(bf16)
        k.pb[rows, :] = low
        other = aligned((1 - k.t) * LOCAL, LOCAL)
        k.pm_send[rows, :] = dot_nt(low, k.ow[other, :]).astype(bf16)
        pm_copy(i).start()
        k.pm_own[rows, :] = dot_nt(low, k.ow[mine, :])
        return carry

    lax.fori_loop(0, ROWS // CHUNK, feed, 0)

    turned = k.nt[...]
    high = turned.astype(bf16)
    rest = (turned - high.astype(f32)).astype(bf16)
    hh = k.hh[...]
    for j in range(2):
        cols = pl.ds(j * 1024, 1024)
        hh += dot(high[:, j * 1024 : (j + 1) * 1024], k.big[cols, :])
        hh += dot(rest[:, j * 1024 : (j + 1) * 1024], k.big[cols, :])
    k.hh[...] = hh

    sums = {part[0]: Sum(k, part, SEM_SUM + 11 * n) for n, part in enumerate(PARTS)}
    turn_rows(k.second, k.turn)
    for j in range(2):

        def up_block(i, carry, j=j):
            cols = aligned(i * 256, 256)
            k.big[pl.ds(j * 1024, 1024), cols] = dot(
                k.turn[...], k.gu[:, aligned(j * 1024 + i * 256, 256)]
            ).astype(bf16)
            return carry

        lax.fori_loop(0, 4, up_block, 0)
        sums[f"u{j}"].core()
    turn_rows(k.mix, k.turn)

    def out_block(i, carry):
        cols = aligned(i * 256, 256)
        other = aligned((1 - k.t) * LOCAL, LOCAL)
        k.og_send[0:512, cols] = dot(k.turn[other, :], k.pb[:, cols]).astype(bf16)
        k.og[0:512, cols] = dot(k.turn[mine, :], k.pb[:, cols]).astype(bf16)
        return carry

    lax.fori_loop(0, 4, out_block, 0)
    k.og_send[512:544, :] = k.hh[...].astype(bf16)
    k.og_send[544:560, :] = k.cs[...].astype(bf16)
    og_copy = k.copy(SEM_OG, k.og_send, k.og_recv, k.y_peer)
    og_copy.start()
    k.lpt[...] = (k.lp[...] + pltpu.roll(k.lp[...], 96, 1)).T[:CHARS]
    lp_copy = k.copy(SEM_OG + 1, k.lpt, k.lpr, k.y_peer)
    lp_copy.start()

    def pm_wait(i, carry):
        pm_copy(i).wait()
        return carry

    lax.fori_loop(0, ROWS // CHUNK, pm_wait, 0)

    def backward_pair(p):
        cols = pair_cols(p)
        mixed = k.mix[:, aligned(k.t * LOCAL + p * 128, 128)].astype(f32)
        grad_pair = (k.pm_own[:, cols] + k.pm_recv[:, cols].astype(f32)).astype(bf16).astype(f32)
        q_pair = k.qkv[0, :, cols].astype(f32) * HEAD_DIM ** (-0.5)
        k_pair = k.qkv[1, :, cols].astype(f32)
        v_pair = k.qkv[2, :, cols].astype(f32)
        lse = k.lse[p]
        q_s, k_s, v_s, g_s = [], [], [], []
        for h in range(2):
            half = (lane < 64) if h == 0 else (lane >= 64)
            e = 64 if h == 0 else 0
            shift = -lse[:, 0:1] if h == 0 else -lse[:, 64:65]
            one = shift.astype(bf16).astype(f32)
            two = (shift - one).astype(bf16).astype(f32)
            three = shift - one - two
            tail = jnp.where(
                lane == e, 1.0, jnp.where(lane == e + 1, one, jnp.where(lane == e + 2, two, jnp.where(lane == e + 3, three, 0.0)))
            )
            q_s.append(jnp.where(half, q_pair, tail).astype(bf16))
            tail = jnp.where(lane == e, key_bias, jnp.where((lane > e) & (lane < e + 4), 1.0, 0.0))
            k_s.append(jnp.where(half, k_pair, tail).astype(bf16))
            tail = jnp.where((lane >= e) & (lane < e + 2), 1.0, 0.0)
            v_s.append(jnp.where(half, v_pair, tail).astype(bf16))
            total = -jnp.sum(jnp.where(half, grad_pair * mixed, 0.0), axis=1, keepdims=True)
            one = total.astype(bf16).astype(f32)
            tail = jnp.where(lane == e, one, jnp.where(lane == e + 1, total - one, 0.0))
            g_s.append(jnp.where(half, grad_pair, tail).astype(bf16))
        sub = lax.broadcasted_iota(jnp.int32, (128, 1), 0)
        for start in range(0, ROWS, KEYS):
            rows = slice(start, start + KEYS)
            made_k, made_v, made_q = [], [], []
            for h in range(2):
                probs = jnp.exp(dot_nt(k_s[h][rows], q_s[h]))
                made_v.append(dot(probs.astype(bf16), g_s[h]))
                change = (probs * dot_nt(v_s[h][rows], g_s[h])).astype(bf16)
                made_k.append(dot(change, q_s[h]))
                made_q.append(dot_tn(k_s[h][rows], change))
            k.gu[rows, aligned(LOCAL + p * 128, 128)] = jnp.where(lane < 64, made_k[0], made_k[1]).astype(bf16)
            k.gu[rows, aligned(2 * LOCAL + p * 128, 128)] = jnp.where(lane < 64, made_v[0], made_v[1]).astype(bf16)
            total = jnp.where(sub < 64, made_q[0], made_q[1])
            if start == 0:
                k.gqt[...] = total
            else:
                k.gqt[...] += total
        k.gu[:, cols] = (k.gqt[...] * HEAD_DIM ** (-0.5)).T.astype(bf16)

    def qkv_grad(half):
        for m in range(3):
            k.upw[:, pl.ds(half * 768 + m * 256, 256)] = dot(
                k.first_t[...], k.gu[:, pl.ds(m * LOCAL + half * 256, 256)]
            ).astype(bf16)

    def pairs(first, last):
        def body(p, carry):
            backward_pair(p)
            return carry

        lax.fori_loop(first, last, body, 0)

    pairs(0, 1)
    sums["u0"].x()
    sums["u1"].x()
    pairs(1, 2)
    og_copy.wait()
    lp_copy.wait()

    def og_add(i, carry):
        rows = aligned(i * 64, 64)
        k.og[rows, :] = (k.og[rows, :].astype(f32) + k.og_recv[rows, :].astype(f32)).astype(bf16)
        return carry

    lax.fori_loop(0, 8, og_add, 0)
    k.og[512:560, :] = (
        k.og_send[512:560, :].astype(f32) + k.og_recv[512:560, :].astype(f32)
    ).astype(bf16)
    k.og[560:592, :] = k.nt[:, 0:1024].astype(bf16)
    k.og[592:624, :] = k.nt[:, 1024:2048].astype(bf16)
    k.og[624:640, :] = jnp.concatenate([k.ub[:, 0:1024], k.ub[:, 1024:2048]], axis=0).astype(bf16)
    grads = k.gd[...].astype(f32)
    k.og[640:656, 0:128] = jnp.broadcast_to(jnp.sum(grads, axis=0, keepdims=True), (16, 128)).astype(bf16)
    k.og[640:656, 128:1024] = jnp.zeros((16, 896), bf16)
    k.og[656:768, :] = jnp.zeros((112, WIDTH), bf16)
    sums["o"].core()
    both = (k.lpt[...] + k.lpr[...]).T
    k.logits[...] = both + k.head_b[...].astype(f32)
    qkv_grad(0)
    sums["q0"].core()
    sums["u0"].spread()
    sums["u1"].spread()
    sums["o"].x()
    sums["q0"].x()
    pairs(2, 3)
    sums["u0"].gather()
    sums["u1"].gather()
    sums["o"].spread()
    pairs(3, 4)
    qkv_grad(1)
    sums["q1"].core()
    sums["q0"].spread()
    sums["q1"].x()

    def f_copy(i):
        rows = aligned(i * CHUNK, CHUNK)
        return k.copy(SEM_F + i, k.first.at[rows, :], k.f_recv.at[rows, :], k.y_peer)

    def f_out(i):
        rows = aligned(i * CHUNK, CHUNK)
        return pltpu.make_async_copy(
            k.first.at[rows, :], k.frames_grad.at[rows, :], k.sem.at[SEM_LOCAL + 8 + i]
        )

    k.cs[...] = jnp.zeros_like(k.cs)

    def last(i, carry):
        start = i * CHUNK
        rows = aligned(start, CHUNK)
        filled, flag = filled_rows(start, CHUNK)
        _, unit, inverse = norm_stats(filled, gain1, bias1)
        grad = dot_nt(k.gu[rows, 0:LOCAL], k.wqkv[0])
        grad += dot_nt(k.gu[rows, LOCAL : 2 * LOCAL], k.wqkv[1])
        grad += dot_nt(k.gu[rows, 2 * LOCAL : 3 * LOCAL], k.wqkv[2])
        k.cs[1:2, :] += col_sum(grad * unit)
        k.cs[2:3, :] += col_sum(grad)
        total = k.pb[rows, :].astype(f32) + norm_back(grad, unit, inverse, gain1)
        k.cs[0:1, :] += col_sum(jnp.where(flag, total, 0.0))
        k.first[rows, :] = jnp.where(flag, 0.0, total).astype(bf16)
        f_copy(i).start()
        return carry

    lax.fori_loop(0, ROWS // CHUNK, last, 0)
    sums["u0"].x_back()
    sums["u1"].x_back()
    sums["o"].gather()
    k.ty[0] = k.cs[...]
    ty = k.copy(SEM_TINY, k.ty.at[0], k.ty.at[1], k.y_peer)
    ty.start()
    sums["q0"].gather()
    sums["q1"].spread()
    ty.wait()
    value = k.ty[0] + k.ty[1]
    raw = jnp.concatenate(
        [col_sum(k.gu[:, pl.ds(m * LOCAL, LOCAL)].astype(f32)) for m in (0, 2)], axis=1
    )
    sub = lax.broadcasted_iota(jnp.int32, (16, 1), 0)
    k.ty[0] = jnp.where(sub == 8, raw, value)
    tc = k.copy(SEM_TINY + 1, k.ty.at[0], k.tc, k.core_peer)
    tc.start()
    sums["u0"].core_back()
    sums["u1"].core_back()
    sums["o"].x_back()
    tc.wait()
    k.cs[...] = k.ty[0] + k.tc[...]
    tx = k.copy(SEM_TINY + 2, k.cs, k.tx, k.x_peer)
    tx.start()
    sums["q1"].gather()
    sums["q0"].x_back()
    tx.wait()
    k.ty[1] = k.cs[...] + k.tx[...]
    handles = []
    for s in range(1, 4):
        handle = k.copy(SEM_TINY + 2 + s, k.ty.at[1], k.tz.at[s], k.z_peer(s))
        handle.start()
        handles.append(handle)
    k.tz[0] = k.ty[1]
    sums["o"].core_back()
    sums["q1"].x_back()
    sums["q0"].core_back()
    for handle in handles:
        handle.wait()
    total = None
    for zz in range(4):
        term = k.tz[lax.rem(k.z - zz + 4, 4)]
        total = term if total is None else total + term
    k.tiny_o[...] = total

    def f_end(i, carry):
        f_copy(i).wait()
        rows = aligned(i * CHUNK, CHUNK)
        k.first[rows, :] = (
            k.first[rows, :].astype(f32) + k.f_recv[rows, :].astype(f32)
        ).astype(bf16)
        f_out(i).start()
        return carry

    lax.fori_loop(0, ROWS // CHUNK, f_end, 0)
    sums["q1"].core_back()
    for name in sums:
        sums[name].end()

    def f_done(i, carry):
        f_out(i).wait()
        return carry

    lax.fori_loop(0, ROWS // CHUNK, f_done, 0)


def local_fused(
    frames,
    lengths,
    span_starts,
    mask_embedding,
    norm1_gain,
    norm1_bias,
    qkv_weight,
    qv_bias,
    out_weight,
    out_bias,
    norm2_gain,
    norm2_bias,
    up_weight,
    up_bias,
    down_weight,
    down_bias,
    head_weight,
    head_bias,
    logit_grad,
):
    vectors = jnp.concatenate(
        [
            item.astype(f32).reshape(-1, WIDTH)
            for item in (
                mask_embedding,
                norm1_gain,
                norm1_bias,
                out_bias,
                norm2_gain,
                norm2_bias,
                down_bias,
                jnp.pad(qv_bias, ((0, 0), (0, WIDTH - LOCAL))),
                up_bias,
            )
        ]
    )
    inputs = dict(
        frames=frames,
        lengths=lengths,
        starts=span_starts,
        vectors=vectors,
        qkv_w=jnp.transpose(qkv_weight, (1, 0, 2)),
        out_w=out_weight,
        up_w=up_weight,
        down_w=down_weight,
        head_w=head_weight,
        head_b=head_bias.reshape(1, CHARS),
        logit_grad=logit_grad,
    )
    spaces = {None: pl.ANY, "vmem": pltpu.VMEM, "smem": pltpu.SMEM}
    scratch = SCRATCH + rest_shapes()
    names = (
        [n for n, _ in INPUTS]
        + [o[0] for o in OUTPUTS]
        + [s[0] for s in scratch]
        + ["sem", "rsem"]
    )
    outs = pl.pallas_call(
        partial(fused, names),
        out_shape=[jax.ShapeDtypeStruct(o[1], o[2]) for o in OUTPUTS],
        in_specs=[pl.BlockSpec(memory_space=spaces[s]) for _, s in INPUTS],
        out_specs=[pl.BlockSpec(memory_space=spaces[o[3]]) for o in OUTPUTS],
        scratch_shapes=[pltpu.VMEM(s[1], s[2]) for s in scratch]
        + [pltpu.SemaphoreType.DMA((SEM_COUNT,)), pltpu.SemaphoreType.DMA((SEM_COUNT,))],
        compiler_params=pltpu.CompilerParams(
            collective_id=0, has_side_effects=True, vmem_limit_bytes=63 * 2**20
        ),
        name="layer",
    )(*[inputs[n] for n, _ in INPUTS])
    logits, frames_grad, up_o, out_o, qkv_o, tiny = outs
    activ_head = out_o[560:624].reshape(2, CHARS, WIDTH).astype(bf16)
    down_grad = jnp.einsum(
        "jvf,dv->jfd", activ_head, head_weight, preferred_element_type=f32
    ).reshape(FFL, WIDTH)
    head_bias_grad = out_o[640, 0:CHARS].astype(f32)
    qkv_grad = (
        qkv_o.reshape(WIDTH, 2, 3, 256).transpose(0, 2, 1, 3).reshape(WIDTH, 3, LOCAL).astype(f32)
    )
    return (
        logits,
        frames_grad.astype(f32),
        tiny[0],
        tiny[1],
        tiny[2],
        qkv_grad,
        tiny[8].reshape(2, LOCAL),
        out_o[0:LOCAL].astype(f32),
        out_o[549].astype(f32),
        out_o[547].astype(f32),
        out_o[548].astype(f32),
        up_o.astype(f32),
        out_o[624:640:8].astype(f32).reshape(FFL),
        down_grad,
        jnp.dot(head_weight.astype(f32), head_bias_grad, precision=lax.Precision.HIGHEST),
        out_o[512:544].astype(f32).T,
        head_bias_grad,
    )


def solution(mesh):
    placed = (
        P("dp", None),
        P("dp"),
        P("dp", None),
        P(),
        P(),
        P(),
        P(None, None, "tensor"),
        P(None, "tensor"),
        P("tensor", None),
        P(),
        P(),
        P(),
        P(None, "tensor"),
        P("tensor"),
        P("tensor", None),
        P(),
        P(),
        P(),
        P("dp", None),
    )
    fits = mesh.shape["dp"] == 16 and mesh.shape["tensor"] == 2
    return jax.shard_map(
        local_fused if fits else local,
        mesh=mesh,
        in_specs=placed,
        out_specs=(
            P("dp", None),
            P("dp", None),
            P(),
            P(),
            P(),
            P(None, None, "tensor"),
            P(None, "tensor"),
            P("tensor", None),
            P(),
            P(),
            P(),
            P(None, "tensor"),
            P("tensor"),
            P("tensor", None),
            P(),
            P(),
            P(),
        ),
        check_vma=False,
    )
```

```python
from functools import partial
from types import SimpleNamespace

import jax
import jax.numpy as jnp
from jax import lax
from jax.experimental import pallas as pl
from jax.experimental.pallas import tpu as pltpu
from jax.sharding import PartitionSpec as P

HEAD_DIM = 64
MASK_SPAN = 10


EPS = 1e-05
NEG = -1e30


def norm_stats(row_block, gain, shift):
    center = row_block - jnp.mean(row_block, axis=-1, keepdims=True)
    spread = jnp.mean(center * center, axis=-1, keepdims=True)
    inverse = lax.rsqrt(spread + EPS)
    unit_rows = center * inverse
    return (unit_rows * gain + shift, unit_rows, inverse)


def norm_back(grad_rows, unit_rows, inverse, gain):
    grad_unit = grad_rows * gain
    first_mean = jnp.mean(grad_unit, axis=-1, keepdims=True)
    second_mean = jnp.mean(grad_unit * unit_rows, axis=-1, keepdims=True)
    return inverse * (grad_unit - first_mean - unit_rows * second_mean)


def masked_scores(queries, key_rows, key_valid):
    factor = HEAD_DIM ** (-0.5)
    scores = (
        jnp.einsum("qhd,khd->hqk", queries, key_rows, preferred_element_type=jnp.float32) * factor
    )
    return jnp.where(key_valid[None, None, :], scores, NEG)


def attend_forward(packed):
    queries, key_rows, values, key_valid = packed
    scores = masked_scores(queries, key_rows, key_valid)
    row_peak = jnp.max(scores, axis=-1, keepdims=True)
    exp_scores = jnp.exp(scores - row_peak)
    row_total = jnp.sum(exp_scores, axis=-1, keepdims=True)
    prob_rows = (exp_scores / row_total).astype(jnp.bfloat16)
    mixture = jnp.einsum("hqk,khd->qhd", prob_rows, values, preferred_element_type=jnp.float32)
    return (mixture, row_peak + jnp.log(row_total))


def attend_backward(packed):
    queries, key_rows, values, key_valid, log_total, grad_mixture = packed
    factor = HEAD_DIM ** (-0.5)
    scores = masked_scores(queries, key_rows, key_valid)
    prob_rows = jnp.exp(scores - log_total)
    grad_values = jnp.einsum(
        "hqk,qhd->khd",
        prob_rows.astype(jnp.bfloat16),
        grad_mixture,
        preferred_element_type=jnp.float32,
    )
    grad_probs = jnp.einsum(
        "qhd,khd->hqk", grad_mixture, values, preferred_element_type=jnp.float32
    )
    row_dot = jnp.sum(prob_rows * grad_probs, axis=-1, keepdims=True)
    grad_scores = (prob_rows * (grad_probs - row_dot)).astype(jnp.bfloat16)
    grad_queries = (
        jnp.einsum("hqk,khd->qhd", grad_scores, key_rows, preferred_element_type=jnp.float32)
        * factor
    )
    grad_keys = (
        jnp.einsum("hqk,qhd->khd", grad_scores, queries, preferred_element_type=jnp.float32)
        * factor
    )
    return (grad_queries, grad_keys, grad_values)


def local(
    frames,
    lengths,
    span_starts,
    mask_embedding,
    norm1_gain,
    norm1_bias,
    qkv_weight,
    qv_bias,
    out_weight,
    out_bias,
    norm2_gain,
    norm2_bias,
    up_weight,
    up_bias,
    down_weight,
    down_bias,
    head_weight,
    head_bias,
    logit_grad,
):
    utterances_here, span_count = span_starts.shape
    row_count, model_width = frames.shape
    frame_count = row_count // utterances_here
    local_width = qkv_weight.shape[2]
    heads_here = local_width // HEAD_DIM
    f32, bf16 = jnp.float32, jnp.bfloat16
    first_share = lax.axis_index("tensor") == 0

    def mm(spec, left, right):
        return jnp.einsum(spec, left, right, preferred_element_type=f32)

    def split(wide):
        high = wide.astype(bf16)
        return jnp.concatenate([high, (wide - high.astype(f32)).astype(bf16)], axis=-1)

    places = jnp.arange(frame_count, dtype=jnp.int32)
    covered = (places[None, None, :] >= span_starts[:, :, None]) & (
        places[None, None, :] < span_starts[:, :, None] + MASK_SPAN
    )
    masked = jnp.any(covered, axis=1).reshape(row_count, 1)
    key_valid = places[None, :] < lengths[:, None]
    gain_one = norm1_gain.astype(f32)
    gain_two = norm2_gain.astype(f32)
    filled = jnp.where(masked, mask_embedding.astype(f32)[None, :], frames.astype(f32))
    first_norm, first_unit, first_inverse = norm_stats(filled, gain_one, norm1_bias.astype(f32))
    first_low = first_norm.astype(bf16)
    weight_flat = qkv_weight.reshape(model_width, 3 * local_width)
    bias_full = jnp.stack(
        [qv_bias[0].astype(f32), jnp.zeros((local_width,), f32), qv_bias[1].astype(f32)]
    ).reshape(3 * local_width)
    projected = (mm("rd,dc->rc", first_low, weight_flat) + bias_full).astype(bf16)
    triple = projected.reshape(utterances_here, frame_count, 3, heads_here, HEAD_DIM)
    queries = triple[:, :, 0]
    key_rows = triple[:, :, 1]
    values = triple[:, :, 2]
    mixture, log_total = lax.map(attend_forward, (queries, key_rows, values, key_valid))
    mixture_low = mixture.astype(bf16).reshape(row_count, local_width)
    mixture_all = lax.all_gather(mixture_low, "tensor", axis=1, tiled=True)
    out_all = lax.all_gather(out_weight, "tensor", axis=0, tiled=True)
    hidden = filled + mm("rl,ld->rd", mixture_all, out_all) + out_bias.astype(f32)
    second_norm, second_unit, second_inverse = norm_stats(hidden, gain_two, norm2_bias.astype(f32))
    second_low = second_norm.astype(bf16)
    up_rows = mm("rd,df->rf", second_low, up_weight) + up_bias.astype(f32)
    activ, gelu_pull = jax.vjp(partial(jax.nn.gelu, approximate=False), up_rows)
    activ_low = activ.astype(bf16)
    down_head = split(mm("fd,dv->fv", down_weight, head_weight))
    characters = head_weight.shape[1]
    own_logits = mm("rf,fv->rv", activ_low, down_head)
    own_logits = own_logits[:, :characters] + own_logits[:, characters:]
    hidden_down = (hidden + down_bias.astype(f32)).astype(bf16)
    logits = (
        lax.psum(own_logits, "tensor")
        + mm("rd,dv->rv", hidden_down, head_weight)
        + head_bias.astype(f32)
    )
    twice = jnp.concatenate([logit_grad, logit_grad], axis=1)
    grad_activ = mm("rv,fv->rf", twice, down_head)
    grad_up = gelu_pull(grad_activ)[0].astype(bf16)
    activ_head = mm("rf,rv->fv", activ_low, logit_grad)
    hidden_head = mm("rd,rv->dv", hidden_down, logit_grad)
    head_bias_grad = jnp.sum(logit_grad.astype(f32), axis=0)
    up_grad = mm("rd,rf->df", second_low, grad_up)
    up_bias_grad = jnp.sum(grad_up.astype(f32), axis=0)
    grad_second = mm("rf,df->rd", grad_up, up_weight)
    norm2_gain_grad = jnp.sum(grad_second * second_unit, axis=0)
    norm2_bias_grad = jnp.sum(grad_second, axis=0)
    grad_output = mm("rv,dv->rd", logit_grad, head_weight)
    grad_hidden = norm_back(grad_second, second_unit, second_inverse, gain_two) + jnp.where(
        first_share, grad_output, 0.0
    )
    grad_attn = grad_hidden.astype(bf16)
    out_bias_grad = jnp.sum(grad_hidden, axis=0)
    grad_mixture = lax.psum_scatter(
        mm("rd,ld->rl", grad_attn, out_all).astype(bf16), "tensor", scatter_dimension=1, tiled=True
    )
    out_grad = lax.psum_scatter(
        mm("rl,rd->ld", mixture_all, grad_attn).astype(bf16),
        "tensor",
        scatter_dimension=0,
        tiled=True,
    )
    grad_mixture = grad_mixture.reshape(utterances_here, frame_count, heads_here, HEAD_DIM)
    grad_queries, grad_keys, grad_values = lax.map(
        attend_backward, (queries, key_rows, values, key_valid, log_total, grad_mixture)
    )
    grad_triple = (
        jnp.stack([grad_queries, grad_keys, grad_values], axis=2)
        .astype(bf16)
        .reshape(row_count, 3 * local_width)
    )
    qkv_grad = mm("rd,rc->dc", first_low, grad_triple).reshape(model_width, 3, local_width)
    column_sums = jnp.sum(grad_triple.astype(f32), axis=0).reshape(3, local_width)
    qv_bias_grad = jnp.stack([column_sums[0], column_sums[2]])
    grad_first = mm("rc,dc->rd", grad_triple, weight_flat)
    norm1_gain_grad = jnp.sum(grad_first * first_unit, axis=0)
    norm1_bias_grad = jnp.sum(grad_first, axis=0)
    grad_filled = grad_hidden + norm_back(grad_first, first_unit, first_inverse, gain_one)
    mask_grad = jnp.sum(jnp.where(masked, grad_filled, 0.0), axis=0)
    frames_grad = jnp.where(masked, 0.0, grad_filled).astype(bf16)
    frames_grad = lax.all_gather(
        lax.psum_scatter(frames_grad, "tensor", scatter_dimension=0, tiled=True),
        "tensor",
        axis=0,
        tiled=True,
    ).astype(f32)
    up_grad = lax.psum(up_grad.astype(bf16), "dp").astype(f32)
    out_grad = lax.psum(out_grad, "dp").astype(f32)
    qkv_grad = lax.psum(qkv_grad.astype(bf16), "dp").astype(f32)
    activ_head, up_bias_grad, qv_bias_grad, head_bias_grad, hidden_head = lax.psum(
        (activ_head, up_bias_grad, qv_bias_grad, head_bias_grad, hidden_head), "dp"
    )
    activ_split = split(activ_head)
    head_twice = jnp.concatenate([head_weight, head_weight], axis=1)
    down_grad = mm("fv,dv->fd", activ_split, head_twice)
    down_head_grad = mm("fd,fv->dv", down_weight, activ_split)
    down_head_grad = down_head_grad[:, :characters] + down_head_grad[:, characters:]
    down_bias_grad = jnp.dot(
        head_weight.astype(f32), head_bias_grad, precision=lax.Precision.HIGHEST
    )
    mask_grad, norm1_gain_grad, norm1_bias_grad, norm2_gain_grad, norm2_bias_grad, out_bias_grad = (
        lax.psum(
            (
                mask_grad,
                norm1_gain_grad,
                norm1_bias_grad,
                norm2_gain_grad,
                norm2_bias_grad,
                out_bias_grad,
            ),
            ("dp", "tensor"),
        )
    )
    head_grad = hidden_head + lax.psum(down_head_grad, "tensor")
    return (
        logits,
        frames_grad,
        mask_grad,
        norm1_gain_grad,
        norm1_bias_grad,
        qkv_grad,
        qv_bias_grad,
        out_grad,
        out_bias_grad,
        norm2_gain_grad,
        norm2_bias_grad,
        up_grad,
        up_bias_grad,
        down_grad,
        down_bias_grad,
        head_grad,
        head_bias_grad,
    )


f32, bf16 = jnp.float32, jnp.bfloat16
WIDTH = 1024
LOCAL = 512
FFL = 2048
ROWS = 896
CHARS = 32
CHUNK = 224
KEYS = 224
QROWS = 224


def dot(left, right):
    return lax.dot_general(left, right, (((1,), (0,)), ((), ())), preferred_element_type=f32)


def dot_nt(left, right):
    return lax.dot_general(left, right, (((1,), (1,)), ((), ())), preferred_element_type=f32)


def dot_tn(left, right):
    return lax.dot_general(left, right, (((0,), (0,)), ((), ())), preferred_element_type=f32)


def aligned(start, size):
    return pl.ds(pl.multiple_of(start, size), size)


def col_sum(block):
    rows, width = block.shape
    return jnp.sum(jnp.sum(block.reshape(rows // 8, 8, width), axis=0), axis=0, keepdims=True)


def gelu_parts(block):
    bell = jnp.exp(block * block * -0.5)
    cdf = 0.5 + 0.5 * lax.erf(block * (0.5**0.5))
    return block * cdf, cdf + block * bell * 0.3989422804014327


VECTORS = (
    "mask_embedding",
    "norm1_gain",
    "norm1_bias",
    "out_bias",
    "norm2_gain",
    "norm2_bias",
    "down_bias",
)
INPUTS = (
    ("frames", None),
    ("lengths", "vmem"),
    ("starts", "vmem"),
    ("mask_embedding", "vmem"),
    ("norm1_gain", "vmem"),
    ("norm1_bias", "vmem"),
    ("out_bias", "vmem"),
    ("norm2_gain", "vmem"),
    ("norm2_bias", "vmem"),
    ("down_bias", "vmem"),
    ("qv_bias", "vmem"),
    ("up_bias", "vmem"),
    ("qkv_w", None),
    ("out_w", None),
    ("up_w", None),
    ("down_w", None),
    ("head_w", "vmem"),
    ("head_b", "vmem"),
    ("logit_grad", "vmem"),
)
OUTPUTS = (
    ("logits", (CHARS, ROWS), f32, "vmem"),
    ("frames_grad", (ROWS, WIDTH), bf16, None),
    ("up_o", (WIDTH, FFL), bf16, None),
    ("out_o", (LOCAL, WIDTH), bf16, None),
    ("qkv_o", (3 * WIDTH, LOCAL), bf16, None),
    ("small_o", (256, LOCAL), bf16, None),
    ("tiny_o", (16, WIDTH), f32, "vmem"),
)
SCRATCH = (
    ("vec", (16, WIDTH), f32),
    ("x", (ROWS, WIDTH), bf16),
    ("wqkv", (3, WIDTH, LOCAL), bf16),
    ("first", (ROWS, WIDTH), bf16),
    ("first_t", (WIDTH, ROWS), bf16),
    ("qkv", (3, ROWS, LOCAL), bf16),
    ("mix", (ROWS, WIDTH), bf16),
    ("ow", (WIDTH, WIDTH), bf16),
    ("upw", (4 * WIDTH, LOCAL), bf16),
    ("big", (2 * WIDTH, WIDTH), bf16),
    ("lse", (ROWS, 128), f32),
    ("dh", (FFL, 128), bf16),
    ("hw2", (WIDTH, 128), bf16),
    ("hw1", (WIDTH, 128), bf16),
    ("gd", (ROWS, 128), bf16),
    ("lp", (ROWS, 128), f32),
    ("lpt", (CHARS, ROWS), f32),
    ("lpr", (CHARS, ROWS), f32),
    ("second", (ROWS, WIDTH), bf16),
    ("unit", (ROWS, WIDTH), bf16),
    ("gu", (ROWS, FFL), bf16),
    ("pb", (ROWS, WIDTH), bf16),
    ("pm_own", (ROWS, LOCAL), bf16),
    ("pm_send", (ROWS, LOCAL), bf16),
    ("pm_recv", (ROWS, LOCAL), bf16),
    ("nt", (CHARS, FFL), f32),
    ("hh", (CHARS, WIDTH), f32),
    ("ub", (8, FFL), f32),
    ("cs", (16, WIDTH), f32),
    ("gqt", (128, ROWS), f32),
    ("turn", (WIDTH, ROWS), bf16),
    ("og", (WIDTH, WIDTH), bf16),
    ("og_rc", (2, 256, WIDTH), bf16),
    ("og_ry", (256, WIDTH), bf16),
    ("sy", (48, WIDTH), f32),
    ("sy_r", (48, WIDTH), f32),
    ("sm", (256, LOCAL), bf16),
    ("f_recv", (ROWS, WIDTH), bf16),
    ("ty", (2, 16, WIDTH), f32),
    ("tc", (16, WIDTH), f32),
    ("tx", (16, WIDTH), f32),
    ("tz", (4, 16, WIDTH), f32),
)
PARTS = (
    ("u0", "big", 1024, 512, 0, 0, "up_o", 0),
    ("u1", "big", 1024, 512, 0, 512, "up_o", 512),
    ("u2", "big", 1024, 512, 1024, 0, "up_o", 1024),
    ("u3", "big", 1024, 512, 1024, 512, "up_o", 1536),
    ("o", "og", 512, 1024, 0, 0, "out_o", 0),
    ("s", "sm", 256, 512, 0, 0, "small_o", 0),
    ("q0", "upw", 3072, 256, 0, 0, "qkv_o", 0),
    ("q1", "upw", 3072, 256, 0, 256, "qkv_o", 256),
)


class Sum:
    def __init__(self, k, part, base):
        name, src, rows, width, row0, col0, out, ocol0 = part
        self.k, self.rows, self.width = k, rows, width
        self.src, self.row0, self.col0 = getattr(k, src), row0, col0
        self.out, self.ocol0 = getattr(k, out), ocol0
        if name == "o":
            self.row0 = k.t * LOCAL
        self.rx, self.rz = getattr(k, name + "_rx"), getattr(k, name + "_rz")
        self.rc = getattr(k, name + "_rc", None)
        self.base = base
        self.half, self.quarter, self.piece = rows // 2, rows // 4, rows // 16
        self.b1 = k.c * self.half
        self.b2 = self.b1 + k.x_ * self.quarter
        self.b3 = self.b2 + k.z * self.piece

    def at(self, start, size):
        return self.src.at[aligned(self.row0 + start, size), pl.ds(self.col0, self.width)]

    def out_at(self, start, size):
        return self.out.at[aligned(start, size), pl.ds(self.ocol0, self.width)]

    def add(self, start, size, others):
        step = min(size, 64 if size % 64 == 0 else 96 if size % 96 == 0 else 32)

        def body(i, carry):
            rows = aligned(self.row0 + start + i * step, step)
            cols = pl.ds(self.col0, self.width)
            total = self.src[rows, cols].astype(f32)
            for other in others:
                total += other[aligned(i * step, step), :].astype(f32)
            self.src[rows, cols] = total.astype(bf16)
            return carry

        lax.fori_loop(0, size // step, body, 0)

    def core(self):
        k = self.k
        self.h_core = k.copy(self.base, self.at((1 - k.c) * self.half, self.half), self.rc, k.core_peer)
        self.h_core.start()

    def x(self):
        k = self.k
        if self.rc is not None:
            self.h_core.wait()
            self.add(self.b1, self.half, [self.rc])
        self.h_x = k.copy(
            self.base + 1,
            self.at(self.b1 + (1 - k.x_) * self.quarter, self.quarter),
            self.rx,
            k.x_peer,
        )
        self.h_x.start()

    def spread(self):
        k = self.k
        self.h_x.wait()
        self.add(self.b2, self.quarter, [self.rx])
        self.h_z = []
        for s in range(1, 4):
            there = lax.rem(k.z + s, 4)
            handle = k.copy(
                self.base + 1 + s,
                self.at(self.b2 + there * self.piece, self.piece),
                self.rz.at[s - 1],
                k.z_peer(s),
            )
            handle.start()
            self.h_z.append(handle)

    def gather(self):
        k = self.k
        for handle in self.h_z:
            handle.wait()
        self.add(self.b3, self.piece, [self.rz.at[s] for s in range(3)])
        mine = self.out_at(self.b3, self.piece)
        self.h_own = pltpu.make_async_copy(self.at(self.b3, self.piece), mine, k.sem.at[self.base + 10])
        self.h_own.start()
        self.h_zg = []
        for s in range(1, 4):
            handle = k.copy(self.base + 4 + s, self.at(self.b3, self.piece), mine, k.z_peer(s))
            handle.start()
            self.h_zg.append(handle)

    def x_back(self):
        k = self.k
        self.h_own.wait()
        for handle in self.h_zg:
            handle.wait()
        block = self.out_at(self.b2, self.quarter)
        self.h_xg = k.copy(self.base + 8, block, block, k.x_peer)
        self.h_xg.start()

    def core_back(self):
        k = self.k
        self.h_xg.wait()
        block = self.out_at(self.b1, self.half)
        self.h_cg = k.copy(self.base + 9, block, block, k.core_peer)
        self.h_cg.start()

    def end(self):
        self.h_cg.wait()


SEM_LOCAL, SEM_OW, SEM_MIX, SEM_PM, SEM_OG, SEM_F, SEM_TINY, SEM_SUM = 0, 16, 20, 24, 28, 36, 40, 48
SEM_COUNT = SEM_SUM + 11 * len(PARTS)


def rest_shapes():
    shapes = []
    for name, _, rows, width, *_ in PARTS:
        if name != "o":
            shapes.append((name + "_rc", (rows // 2, width), bf16))
        shapes += [
            (name + "_rx", (rows // 4, width), bf16),
            (name + "_rz", (3, rows // 16, width), bf16),
        ]
    return tuple(shapes)


def fused(names, *refs):
    k = SimpleNamespace(**dict(zip(names, refs)))
    place = lax.axis_index("dp")
    k.t = lax.axis_index("tensor")
    k.z, k.x_, k.c = place // 4, lax.rem(place // 2, 2), lax.rem(place, 2)
    k.core_peer = {"dp": place + 1 - 2 * k.c}
    k.x_peer = {"dp": place + 2 - 4 * k.x_}
    k.y_peer = {"tensor": 1 - k.t}
    k.z_peer = lambda s: {"dp": lax.rem(k.z + s, 4) * 4 + k.x_ * 2 + k.c}

    def copy(number, src, dst, device):
        return pltpu.make_async_remote_copy(
            src_ref=src,
            dst_ref=dst,
            send_sem=k.sem.at[number],
            recv_sem=k.rsem.at[number],
            device_id=device,
            device_id_type=pl.DeviceIdType.MESH,
        )

    k.copy = copy
    loads = {}
    mine = aligned(k.t * LOCAL, LOCAL)
    for number, (name, src, dst) in enumerate(
        (
            ("x", k.frames, k.x),
            ("wqkv", k.qkv_w, k.wqkv),
            ("ow", k.out_w, k.ow.at[mine, :]),
            ("big", k.down_w, k.big),
        )
        + tuple(
            (f"upw{j}", k.up_w.at[:, pl.ds(j * 512, 512)], k.upw.at[pl.ds(j * 1024, 1024), :])
            for j in range(4)
        )
    ):
        loads[name] = pltpu.make_async_copy(src, dst, k.sem.at[SEM_LOCAL + number])
        loads[name].start()
    barrier = pltpu.get_barrier_semaphore()
    peers = [k.core_peer, k.x_peer, k.y_peer, k.z_peer(1), k.z_peer(2), k.z_peer(3)]
    for peer in peers:
        pl.semaphore_signal(barrier, inc=1, device_id=peer, device_id_type=pl.DeviceIdType.MESH)
    pl.semaphore_wait(barrier, len(peers))

    for number, name in enumerate(VECTORS):
        k.vec[number : number + 1, :] = getattr(k, name)[...].astype(f32).reshape(1, WIDTH)
    k.vec[7:9, 0:LOCAL] = k.qv_bias[...].astype(f32)
    k.vec[9:11, :] = k.up_bias[...].astype(f32).reshape(2, WIDTH)
    emb, gain1, bias1, out_bias, gain2, bias2, down_bias = (
        k.vec[i : i + 1, :] for i in range(7)
    )
    lane = lax.broadcasted_iota(jnp.int32, (1, 128), 1)
    first_share = jnp.where(k.t == 0, 1.0, 0.0).astype(f32)

    def filled_rows(start, size):
        ids = lax.broadcasted_iota(jnp.int32, (size, k.starts.shape[1]), 0) + start
        begin = k.starts[...]
        inside = jnp.where((ids >= begin) & (ids < begin + MASK_SPAN), 1.0, 0.0)
        column = jnp.max(inside, axis=1, keepdims=True)
        flag = jnp.broadcast_to(column, (size, WIDTH)) > 0.5
        return jnp.where(flag, emb, k.x[aligned(start, size), :].astype(f32)), flag

    loads["ow"].wait()
    own_half = k.ow.at[aligned(k.t * LOCAL + k.c * 256, 256), :]
    ow_y = k.copy(SEM_OW, own_half, own_half, k.y_peer)
    ow_y.start()

    loads["x"].wait()

    def ln1(i, carry):
        filled, _ = filled_rows(i * 128, 128)
        norm, _, _ = norm_stats(filled, gain1, bias1)
        k.first[aligned(i * 128, 128), :] = norm.astype(bf16)
        return carry

    lax.fori_loop(0, ROWS // 128, ln1, 0)
    key_bias = jnp.where(
        lax.broadcasted_iota(jnp.int32, (ROWS, 1), 0) < k.lengths[...].reshape(1, 1), 0.0, NEG
    ).astype(f32)

    def pair_cols(p):
        return aligned(p * 128, 128)

    def mix_copy(p):
        strip = k.mix.at[:, aligned(k.t * LOCAL + p * 128, 128)]
        return k.copy(SEM_MIX + p, strip, strip, k.y_peer)

    def forward_pair(p, carry):
        cols = pair_cols(p)
        q_pair = k.qkv[0, :, cols].astype(f32) * HEAD_DIM ** (-0.5)
        k_pair = k.qkv[1, :, cols].astype(f32)
        v_pair = k.qkv[2, :, cols].astype(f32)
        for start in range(0, ROWS, QROWS):
            parts = []
            stats = []
            for h in range(2):
                half = (lane < 64) if h == 0 else (lane >= 64)
                extra = 64 if h == 0 else 0
                spot = lane == extra
                q_h = jnp.where(half, q_pair[start : start + QROWS], jnp.where(spot, 1.0, 0.0))
                k_h = jnp.where(half, k_pair, jnp.where(spot, key_bias, 0.0))
                v_h = jnp.where(half, v_pair, jnp.where(spot, 1.0, 0.0))
                scores = dot_nt(q_h.astype(bf16), k_h.astype(bf16))
                peak = jnp.max(scores, axis=1, keepdims=True)
                weights = jnp.exp(scores - peak).astype(bf16)
                both = dot(weights, v_h.astype(bf16))
                total = both[:, extra : extra + 1]
                parts.append(both / total)
                stats.append(peak + jnp.log(total))
            k.mix[start : start + QROWS, aligned(k.t * LOCAL + p * 128, 128)] = jnp.where(
                lane < 64, parts[0], parts[1]
            ).astype(bf16)
            rows = slice(start, start + QROWS)
            k.lse[rows, :] = jnp.where(
                lane == 2 * p, stats[0], jnp.where(lane == 2 * p + 1, stats[1], k.lse[rows, :])
            )
        mix_copy(p).start()
        return carry

    loads["wqkv"].wait()
    k.lse[...] = jnp.zeros_like(k.lse)
    for half in range(2):
        cols = pl.ds(half * 256, 256)
        for m in range(3):
            bias = None if m == 1 else k.vec[7 + m // 2 : 8 + m // 2, cols]

            def project(i, carry, m=m, bias=bias, cols=cols):
                rows = aligned(i * 448, 448)
                value = dot(k.first[rows, :], k.wqkv[m, :, cols])
                k.qkv[m, rows, cols] = (value if bias is None else value + bias).astype(bf16)
                return carry

            lax.fori_loop(0, ROWS // 448, project, 0)
        lax.fori_loop(2 * half, 2 * half + 2, forward_pair, 0)
        if half == 0:
            ow_y.wait()
            got = k.ow.at[aligned((1 - k.t) * LOCAL + k.c * 256, 256), :]
            ow_core = k.copy(SEM_OW + 1, got, got, k.core_peer)
            ow_core.start()

    def turn_rows(src, dst):
        def body(i, carry):
            cols = aligned(i * 128, 128)
            dst[cols, :] = src[:, cols].T
            return carry

        lax.fori_loop(0, WIDTH // 128, body, 0)

    turn_rows(k.first, k.first_t)
    pick = lax.broadcasted_iota(jnp.int32, (CHARS, 128), 0)
    spot = lax.broadcasted_iota(jnp.int32, (CHARS, 128), 1)
    once = jnp.where(pick == spot, 1.0, 0.0).astype(bf16)
    twice = jnp.where((pick == spot) | (pick + CHARS == spot), 1.0, 0.0).astype(bf16)
    k.hw1[...] = dot_tn(k.head_w[...], once).astype(bf16)
    k.hw2[...] = dot_tn(k.head_w[...], twice).astype(bf16)
    k.gd[...] = dot_tn(k.logit_grad[...], twice).astype(bf16)
    loads["big"].wait()

    def fold(i, carry):
        rows = aligned(i * 512, 512)
        value = dot(k.big[rows, :], k.hw2[...])
        high = value.astype(bf16).astype(f32)
        k.dh[rows, :] = jnp.where(lane < CHARS, high, value - high).astype(bf16)
        return carry

    lax.fori_loop(0, 4, fold, 0)
    k.nt[...] = jnp.zeros_like(k.nt)
    k.hh[...] = jnp.zeros_like(k.hh)
    k.ub[...] = jnp.zeros_like(k.ub)
    k.cs[...] = jnp.zeros_like(k.cs)
    ow_core.wait()
    for j in range(4):
        loads[f"upw{j}"].wait()

    def mix_wait(p, carry):
        mix_copy(p).wait()
        return carry

    lax.fori_loop(0, 4, mix_wait, 0)

    def pm_copy(i):
        rows = aligned(i * CHUNK, CHUNK)
        return k.copy(SEM_PM + i, k.pm_send.at[rows, :], k.pm_recv.at[rows, :], k.y_peer)

    def feed(i, carry):
        start = i * CHUNK
        rows = aligned(start, CHUNK)
        filled, _ = filled_rows(start, CHUNK)
        hidden = filled + dot(k.mix[rows, :], k.ow[...]) + out_bias
        second, unit, inverse = norm_stats(hidden, gain2, bias2)
        low = second.astype(bf16)
        k.second[rows, :] = low
        k.unit[rows, :] = unit.astype(bf16)
        down = (hidden + down_bias).astype(bf16)
        grad = k.gd[rows, :]
        head = dot(down, k.hw1[...]) * 0.5
        k.hh[...] += dot_tn(grad, down)[:CHARS] * first_share
        for j in range(4):
            cols = pl.ds(j * 512, 512)
            up = dot(low, k.upw[pl.ds(j * 1024, 1024), :])
            up += k.vec[9 + j // 2 : 10 + j // 2, pl.ds((j % 2) * 512, 512)]
            act, slope = gelu_parts(up)
            act = act.astype(bf16)
            head += dot(act, k.dh[cols, :])
            k.nt[:, cols] += dot_tn(grad, act)[:CHARS]
            grad_up = (dot_nt(grad, k.dh[cols, :]) * slope).astype(bf16)
            k.gu[rows, cols] = grad_up
            k.ub[0:1, cols] += col_sum(grad_up.astype(f32))
        k.lp[rows, :] = jnp.where(lane == 64, inverse, head)
        return carry

    lax.fori_loop(0, ROWS // CHUNK, feed, 0)

    def norm2_back(i):
        rows = pl.ds(i * CHUNK, CHUNK)
        grad_second = dot_nt(k.gu[rows, 0:512], k.upw[0:1024, :])
        for j in range(1, 4):
            grad_second += dot_nt(
                k.gu[rows, pl.ds(j * 512, 512)], k.upw[pl.ds(j * 1024, 1024), :]
            )
        unit = k.unit[rows, :].astype(f32)
        inverse = k.lp[rows, 64:65]
        k.cs[3:4, :] += col_sum(grad_second * unit)
        k.cs[4:5, :] += col_sum(grad_second)
        spread = norm_back(grad_second, unit, inverse, gain2)
        spread += dot_nt(k.gd[rows, :], k.hw1[...]) * first_share
        k.cs[5:6, :] += col_sum(spread)
        low = spread.astype(bf16)
        k.pb[rows, :] = low
        other = aligned((1 - k.t) * LOCAL, LOCAL)
        k.pm_send[rows, :] = dot_nt(low, k.ow[other, :]).astype(bf16)
        pm_copy(i).start()
        k.pm_own[rows, :] = dot_nt(low, k.ow[mine, :]).astype(bf16)

    sums = {part[0]: Sum(k, part, SEM_SUM + 11 * n) for n, part in enumerate(PARTS)}
    turn_rows(k.second, k.turn)
    turned = k.nt[...]
    high = turned.astype(bf16)
    rest = (turned - high.astype(f32)).astype(bf16)
    hh = k.hh[...]
    for j in range(2):
        cols = slice(j * 1024, (j + 1) * 1024)
        hh += dot(high[:, cols], k.big[cols, :]) + dot(rest[:, cols], k.big[cols, :])
    k.hh[...] = hh
    for i in range(4):
        norm2_back(i)

        def up_block(n, carry, i=i):
            k.big[
                pl.ds((i // 2) * 1024, 1024), aligned((i % 2) * 512 + n * 256, 256)
            ] = dot(k.turn[...], k.gu[:, aligned(i * 512 + n * 256, 256)]).astype(bf16)
            return carry

        lax.fori_loop(0, 2, up_block, 0)
        sums[f"u{i}"].core()
        if i >= 1:
            sums[f"u{i - 1}"].x()
        if i >= 3:
            sums[f"u{i - 3}"].spread()
    turn_rows(k.mix, k.turn)

    def out_block(i, carry):
        cols = aligned(i * 256, 256)
        k.og[:, cols] = dot(k.turn[...], k.pb[:, cols]).astype(bf16)
        return carry

    lax.fori_loop(0, 4, out_block, 0)
    og_core = []
    for part in range(2):
        handle = k.copy(
            SEM_OG + part,
            k.og.at[aligned(part * LOCAL + (1 - k.c) * 256, 256), :],
            k.og_rc.at[part],
            k.core_peer,
        )
        handle.start()
        og_core.append(handle)
    k.sy[0:32, :] = k.hh[...]
    k.sy[32:48, :] = k.cs[...]
    sy_copy = k.copy(SEM_OG + 2, k.sy, k.sy_r, k.y_peer)
    sy_copy.start()
    k.lpt[...] = (k.lp[...] + pltpu.roll(k.lp[...], 96, 1)).T[:CHARS]
    lp_copy = k.copy(SEM_OG + 3, k.lpt, k.lpr, k.y_peer)
    lp_copy.start()

    def og_add(base, other):
        def body(i, carry):
            rows = aligned(base + i * 64, 64)
            total = k.og[rows, :].astype(f32) + other[aligned(i * 64, 64), :].astype(f32)
            k.og[rows, :] = total.astype(bf16)
            return carry

        lax.fori_loop(0, 4, body, 0)

    def og_pair():
        for part in range(2):
            og_core[part].wait()
            og_add(part * LOCAL + k.c * 256, k.og_rc.at[part])
        handle = k.copy(
            SEM_OG + 4,
            k.og.at[aligned((1 - k.t) * LOCAL + k.c * 256, 256), :],
            k.og_ry,
            k.y_peer,
        )
        handle.start()
        return handle

    def og_cross(handle):
        handle.wait()
        og_add(k.t * LOCAL + k.c * 256, k.og_ry)
        sums["o"].x()

    def small():
        sy_copy.wait()
        lp_copy.wait()
        k.logits[...] = k.lpt[...] + k.lpr[...] + k.head_b[...].astype(f32).reshape(CHARS, 1)
        k.sy[...] += k.sy_r[...]
        for j in range(4):
            k.sm[j * 32 : j * 32 + 32, :] = k.nt[:, j * 512 : (j + 1) * 512].astype(bf16)
        for j in range(2):
            cols = slice(j * 512, (j + 1) * 512)
            k.sm[128 + j * 32 : 160 + j * 32, :] = k.sy[0:32, cols].astype(bf16)
            k.sm[192 + j * 16 : 208 + j * 16, :] = k.sy[32:48, cols].astype(bf16)
        sub = lax.broadcasted_iota(jnp.int32, (16, 1), 0)
        total = jnp.sum(k.gd[...].astype(f32), axis=0, keepdims=True)
        total = jnp.concatenate([total, jnp.zeros((1, 384), f32)], axis=1)
        last_rows = jnp.where(sub == 4, total, 0.0)
        for j in range(4):
            last_rows = jnp.where(sub == j, k.ub[0:1, j * 512 : (j + 1) * 512], last_rows)
        k.sm[224:240, :] = last_rows.astype(bf16)
        k.sm[240:256, :] = jnp.zeros((16, LOCAL), bf16)
        sums["s"].core()

    def pm_wait(i, carry):
        pm_copy(i).wait()
        return carry

    lax.fori_loop(0, ROWS // CHUNK, pm_wait, 0)

    def backward_pair(p, part):
        cols = pair_cols(p)
        mixed = k.mix[:, aligned(k.t * LOCAL + p * 128, 128)].astype(f32)
        grad_pair = (k.pm_own[:, cols].astype(f32) + k.pm_recv[:, cols].astype(f32)).astype(bf16).astype(f32)
        q_pair = k.qkv[0, :, cols].astype(f32) * HEAD_DIM ** (-0.5)
        k_pair = k.qkv[1, :, cols].astype(f32)
        v_pair = k.qkv[2, :, cols].astype(f32)
        lse = k.lse[...]
        q_s, k_s, v_s, g_s = [], [], [], []
        for h in range(2):
            half = (lane < 64) if h == 0 else (lane >= 64)
            e = 64 if h == 0 else 0
            shift = -lse[:, 2 * p + h : 2 * p + h + 1]
            one = shift.astype(bf16).astype(f32)
            two = (shift - one).astype(bf16).astype(f32)
            three = shift - one - two
            tail = jnp.where(
                lane == e, 1.0, jnp.where(lane == e + 1, one, jnp.where(lane == e + 2, two, jnp.where(lane == e + 3, three, 0.0)))
            )
            q_s.append(jnp.where(half, q_pair, tail).astype(bf16))
            tail = jnp.where(lane == e, key_bias, jnp.where((lane > e) & (lane < e + 4), 1.0, 0.0))
            k_s.append(jnp.where(half, k_pair, tail).astype(bf16))
            tail = jnp.where((lane >= e) & (lane < e + 2), 1.0, 0.0)
            v_s.append(jnp.where(half, v_pair, tail).astype(bf16))
            total = -jnp.sum(jnp.where(half, grad_pair * mixed, 0.0), axis=1, keepdims=True)
            one = total.astype(bf16).astype(f32)
            tail = jnp.where(lane == e, one, jnp.where(lane == e + 1, total - one, 0.0))
            g_s.append(jnp.where(half, grad_pair, tail).astype(bf16))
        sub = lax.broadcasted_iota(jnp.int32, (128, 1), 0)
        for start in range(part * 448, part * 448 + 448, KEYS):
            rows = slice(start, start + KEYS)
            made_k, made_v, made_q = [], [], []
            for h in range(2):
                probs = jnp.exp(dot_nt(k_s[h][rows], q_s[h]))
                made_v.append(dot(probs.astype(bf16), g_s[h]))
                change = (probs * dot_nt(v_s[h][rows], g_s[h])).astype(bf16)
                made_k.append(dot(change, q_s[h]))
                made_q.append(dot_tn(k_s[h][rows], change))
            k.gu[rows, aligned(LOCAL + p * 128, 128)] = jnp.where(lane < 64, made_k[0], made_k[1]).astype(bf16)
            k.gu[rows, aligned(2 * LOCAL + p * 128, 128)] = jnp.where(lane < 64, made_v[0], made_v[1]).astype(bf16)
            total = jnp.where(sub < 64, made_q[0], made_q[1])
            if start == 0:
                k.gqt[...] = total
            else:
                k.gqt[...] += total
        if part == 1:
            k.gu[:, cols] = (k.gqt[...] * HEAD_DIM ** (-0.5)).T.astype(bf16)

    def qkv_grad(half):
        for m in range(3):
            k.upw[pl.ds(m * 1024, 1024), pl.ds(half * 256, 256)] = dot(
                k.first_t[...], k.gu[:, pl.ds(m * LOCAL + half * 256, 256)]
            ).astype(bf16)
        sums[f"q{half}"].core()

    backward_pair(0, 0)
    sums["u3"].x()
    sums["u1"].spread()
    crossing = og_pair()
    backward_pair(0, 1)
    sums["u0"].gather()
    small()
    backward_pair(1, 0)
    sums["u2"].spread()
    sums["u1"].gather()
    backward_pair(1, 1)
    qkv_grad(0)
    sums["u0"].x_back()
    sums["u3"].spread()
    og_cross(crossing)
    backward_pair(2, 0)
    sums["u2"].gather()
    sums["q0"].x()
    sums["s"].x()
    backward_pair(2, 1)
    sums["u1"].x_back()
    sums["u3"].gather()
    backward_pair(3, 0)
    sums["o"].spread()
    sums["u0"].core_back()
    backward_pair(3, 1)
    qkv_grad(1)
    sums["q0"].spread()

    def f_copy(i):
        rows = aligned(i * CHUNK, CHUNK)
        return k.copy(SEM_F + i, k.first.at[rows, :], k.f_recv.at[rows, :], k.y_peer)

    def f_out(i):
        rows = aligned(i * CHUNK, CHUNK)
        return pltpu.make_async_copy(
            k.first.at[rows, :], k.frames_grad.at[rows, :], k.sem.at[SEM_LOCAL + 8 + i]
        )

    k.cs[...] = jnp.zeros_like(k.cs)

    def last(i, carry):
        start = i * CHUNK
        rows = aligned(start, CHUNK)
        filled, flag = filled_rows(start, CHUNK)
        _, unit, inverse = norm_stats(filled, gain1, bias1)
        grad = dot_nt(k.gu[rows, 0:LOCAL], k.wqkv[0])
        grad += dot_nt(k.gu[rows, LOCAL : 2 * LOCAL], k.wqkv[1])
        grad += dot_nt(k.gu[rows, 2 * LOCAL : 3 * LOCAL], k.wqkv[2])
        k.cs[1:2, :] += col_sum(grad * unit)
        k.cs[2:3, :] += col_sum(grad)
        total = k.pb[rows, :].astype(f32) + norm_back(grad, unit, inverse, gain1)
        k.cs[0:1, :] += col_sum(jnp.where(flag, total, 0.0))
        k.first[rows, :] = jnp.where(flag, 0.0, total).astype(bf16)
        f_copy(i).start()
        return carry

    lax.fori_loop(0, ROWS // CHUNK, last, 0)
    sums["q1"].x()
    sums["u2"].x_back()
    sums["s"].spread()
    sums["o"].gather()
    k.ty[0] = k.cs[...]
    ty = k.copy(SEM_TINY, k.ty.at[0], k.ty.at[1], k.y_peer)
    ty.start()
    sums["q0"].gather()
    sums["u3"].x_back()
    sums["u1"].core_back()
    ty.wait()
    value = k.ty[0] + k.ty[1]
    raw = jnp.concatenate(
        [col_sum(k.gu[:, pl.ds(m * LOCAL, LOCAL)].astype(f32)) for m in (0, 2)], axis=1
    )
    sub = lax.broadcasted_iota(jnp.int32, (16, 1), 0)
    k.ty[0] = jnp.where(sub == 8, raw, value)
    tc = k.copy(SEM_TINY + 1, k.ty.at[0], k.tc, k.core_peer)
    tc.start()
    sums["q1"].spread()
    sums["s"].gather()
    tc.wait()
    k.cs[...] = k.ty[0] + k.tc[...]
    tx = k.copy(SEM_TINY + 2, k.cs, k.tx, k.x_peer)
    tx.start()
    sums["o"].x_back()
    sums["u2"].core_back()
    tx.wait()
    k.ty[1] = k.cs[...] + k.tx[...]
    handles = []
    for s in range(1, 4):
        handle = k.copy(SEM_TINY + 2 + s, k.ty.at[1], k.tz.at[s], k.z_peer(s))
        handle.start()
        handles.append(handle)
    k.tz[0] = k.ty[1]
    sums["q0"].x_back()
    sums["q1"].gather()
    sums["s"].x_back()
    sums["u3"].core_back()
    for handle in handles:
        handle.wait()
    total = None
    for zz in range(4):
        term = k.tz[lax.rem(k.z - zz + 4, 4)]
        total = term if total is None else total + term
    k.tiny_o[...] = total

    def f_end(i, carry):
        f_copy(i).wait()
        rows = aligned(i * CHUNK, CHUNK)
        k.first[rows, :] = (
            k.first[rows, :].astype(f32) + k.f_recv[rows, :].astype(f32)
        ).astype(bf16)
        f_out(i).start()
        return carry

    lax.fori_loop(0, ROWS // CHUNK, f_end, 0)
    sums["o"].core_back()
    sums["q0"].core_back()
    sums["q1"].x_back()
    sums["s"].core_back()
    sums["q1"].core_back()
    for name in sums:
        sums[name].end()

    def f_done(i, carry):
        f_out(i).wait()
        return carry

    lax.fori_loop(0, ROWS // CHUNK, f_done, 0)


def local_fused(
    frames,
    lengths,
    span_starts,
    mask_embedding,
    norm1_gain,
    norm1_bias,
    qkv_weight,
    qv_bias,
    out_weight,
    out_bias,
    norm2_gain,
    norm2_bias,
    up_weight,
    up_bias,
    down_weight,
    down_bias,
    head_weight,
    head_bias,
    logit_grad,
):
    inputs = dict(
        frames=frames,
        lengths=lengths,
        starts=span_starts,
        mask_embedding=mask_embedding,
        norm1_gain=norm1_gain,
        norm1_bias=norm1_bias,
        out_bias=out_bias,
        norm2_gain=norm2_gain,
        norm2_bias=norm2_bias,
        down_bias=down_bias,
        qv_bias=qv_bias,
        up_bias=up_bias,
        qkv_w=jnp.transpose(qkv_weight, (1, 0, 2)),
        out_w=out_weight,
        up_w=up_weight,
        down_w=down_weight,
        head_w=head_weight.T,
        head_b=head_bias,
        logit_grad=logit_grad.T,
    )
    spaces = {None: pl.ANY, "vmem": pltpu.VMEM}
    scratch = SCRATCH + rest_shapes()
    names = (
        [n for n, _ in INPUTS]
        + [o[0] for o in OUTPUTS]
        + [s[0] for s in scratch]
        + ["sem", "rsem"]
    )
    outs = pl.pallas_call(
        partial(fused, names),
        out_shape=[jax.ShapeDtypeStruct(o[1], o[2]) for o in OUTPUTS],
        in_specs=[pl.BlockSpec(memory_space=spaces[s]) for _, s in INPUTS],
        out_specs=[pl.BlockSpec(memory_space=spaces[o[3]]) for o in OUTPUTS],
        scratch_shapes=[pltpu.VMEM(s[1], s[2]) for s in scratch]
        + [pltpu.SemaphoreType.DMA((SEM_COUNT,)), pltpu.SemaphoreType.DMA((SEM_COUNT,))],
        compiler_params=pltpu.CompilerParams(
            collective_id=0, has_side_effects=True, vmem_limit_bytes=63 * 2**20
        ),
        name="layer",
    )(*[inputs[n] for n, _ in INPUTS])
    logits, frames_grad, up_o, out_o, qkv_o, small_o, tiny = outs
    wide = widen(frames_grad, up_o, out_o, qkv_o, small_o, tiny, head_weight.T)
    frames_grad, up_grad, out_grad, qkv_grad, down_grad, head_grad, qv_grad = wide[:7]
    up_bias_grad, down_bias_grad, head_bias_grad = wide[7:10]
    mask_grad, gain1_grad, bias1_grad, gain2_grad, bias2_grad, out_bias_grad = wide[10:]
    return (
        logits.T,
        frames_grad,
        mask_grad,
        gain1_grad,
        bias1_grad,
        jnp.transpose(qkv_grad.reshape(3, WIDTH, LOCAL), (1, 0, 2)),
        qv_grad,
        out_grad,
        out_bias_grad,
        gain2_grad,
        bias2_grad,
        up_grad,
        up_bias_grad,
        down_grad,
        down_bias_grad,
        head_grad.T,
        head_bias_grad,
    )


STEPS = 8


def widen_kernel(fg, uo, oo, qo, so, ti, hw, fg_w, u_w, o_w, q_w, d_w, hg, qv, ub, db, hb, *vectors):
    step = pl.program_id(0)
    fg_w[...] = fg[...].astype(f32)
    u_w[...] = uo[...].astype(f32)
    o_w[...] = oo[...].astype(f32)
    q_w[...] = qo[...].astype(f32)
    for j in range(4):

        @pl.when(step // 2 == j)
        def _(j=j):
            for n in range(2):

                @pl.when(lax.rem(step, 2) == n)
                def _(n=n):
                    d_w[...] = dot_tn(
                        so[j * 32 : j * 32 + 32, n * 256 : (n + 1) * 256], hw[...]
                    )

    @pl.when(step == 0)
    def _():
        for j in range(2):
            cols = slice(j * 512, (j + 1) * 512)
            hg[:, cols] = so[128 + j * 32 : 160 + j * 32, :].astype(f32)
            qv[j : j + 1, :] = ti[8:9, cols]
        tail = so[224:240, :].astype(f32)
        for j in range(4):
            ub[pl.ds(j * 512, 512)] = tail[j : j + 1, :].reshape(512)
        hb[...] = tail[4:5, 0:CHARS].reshape(CHARS)
        grads = tail[4:5, 0:CHARS].reshape(CHARS, 1)
        db[...] = jnp.sum(hw[...].astype(f32) * grads, axis=0, keepdims=True).reshape(WIDTH)
        for number in range(3):
            vectors[number][...] = ti[number : number + 1, :].reshape(WIDTH)
        for number in range(3):
            for j in range(2):
                block = so[192 + j * 16 : 208 + j * 16, :].astype(f32)
                vectors[3 + number][pl.ds(j * 512, 512)] = block[3 + number : 4 + number, :].reshape(512)


def widen(frames_grad, up_o, out_o, qkv_o, small_o, tiny, head_t):
    def strip(array):
        return pl.BlockSpec((array.shape[0] // STEPS, array.shape[1]), lambda i: (i, 0))

    def whole(*shape):
        return pl.BlockSpec(shape, lambda i: (0,) * len(shape))

    def shaped(*shape):
        return jax.ShapeDtypeStruct(shape, f32)

    large = (frames_grad, up_o, out_o, qkv_o)
    down = shaped(FFL, WIDTH)
    rest = [shaped(CHARS, WIDTH), shaped(2, LOCAL), shaped(FFL), shaped(WIDTH), shaped(CHARS)]
    rest += [shaped(WIDTH)] * 6
    return pl.pallas_call(
        widen_kernel,
        grid=(STEPS,),
        out_shape=[shaped(*a.shape) for a in large] + [down] + rest,
        in_specs=[strip(a) for a in large]
        + [whole(*small_o.shape), whole(*tiny.shape), whole(*head_t.shape)],
        out_specs=[strip(a) for a in large] + [strip(down)] + [whole(*r.shape) for r in rest],
        compiler_params=pltpu.CompilerParams(vmem_limit_bytes=60 * 2**20),
        name="widen",
    )(*large, small_o, tiny, head_t)


def solution(mesh):
    placed = (
        P("dp", None),
        P("dp"),
        P("dp", None),
        P(),
        P(),
        P(),
        P(None, None, "tensor"),
        P(None, "tensor"),
        P("tensor", None),
        P(),
        P(),
        P(),
        P(None, "tensor"),
        P("tensor"),
        P("tensor", None),
        P(),
        P(),
        P(),
        P("dp", None),
    )
    fits = mesh.shape["dp"] == 16 and mesh.shape["tensor"] == 2
    return jax.shard_map(
        local_fused if fits else local,
        mesh=mesh,
        in_specs=placed,
        out_specs=(
            P("dp", None),
            P("dp", None),
            P(),
            P(),
            P(),
            P(None, None, "tensor"),
            P(None, "tensor"),
            P("tensor", None),
            P(),
            P(),
            P(),
            P(None, "tensor"),
            P("tensor"),
            P("tensor", None),
            P(),
            P(),
            P(),
        ),
        check_vma=False,
    )
```

```python
from functools import partial
from types import SimpleNamespace

import jax
import jax.numpy as jnp
from jax import lax
from jax.experimental import pallas as pl
from jax.experimental.pallas import tpu as pltpu
from jax.sharding import PartitionSpec as P

HEAD_DIM = 64
MASK_SPAN = 10


EPS = 1e-05
NEG = -1e30


def norm_stats(row_block, gain, shift):
    center = row_block - jnp.mean(row_block, axis=-1, keepdims=True)
    spread = jnp.mean(center * center, axis=-1, keepdims=True)
    inverse = lax.rsqrt(spread + EPS)
    unit_rows = center * inverse
    return (unit_rows * gain + shift, unit_rows, inverse)


def norm_back(grad_rows, unit_rows, inverse, gain):
    grad_unit = grad_rows * gain
    first_mean = jnp.mean(grad_unit, axis=-1, keepdims=True)
    second_mean = jnp.mean(grad_unit * unit_rows, axis=-1, keepdims=True)
    return inverse * (grad_unit - first_mean - unit_rows * second_mean)


def masked_scores(queries, key_rows, key_valid):
    factor = HEAD_DIM ** (-0.5)
    scores = (
        jnp.einsum("qhd,khd->hqk", queries, key_rows, preferred_element_type=jnp.float32) * factor
    )
    return jnp.where(key_valid[None, None, :], scores, NEG)


def attend_forward(packed):
    queries, key_rows, values, key_valid = packed
    scores = masked_scores(queries, key_rows, key_valid)
    row_peak = jnp.max(scores, axis=-1, keepdims=True)
    exp_scores = jnp.exp(scores - row_peak)
    row_total = jnp.sum(exp_scores, axis=-1, keepdims=True)
    prob_rows = (exp_scores / row_total).astype(jnp.bfloat16)
    mixture = jnp.einsum("hqk,khd->qhd", prob_rows, values, preferred_element_type=jnp.float32)
    return (mixture, row_peak + jnp.log(row_total))


def attend_backward(packed):
    queries, key_rows, values, key_valid, log_total, grad_mixture = packed
    factor = HEAD_DIM ** (-0.5)
    scores = masked_scores(queries, key_rows, key_valid)
    prob_rows = jnp.exp(scores - log_total)
    grad_values = jnp.einsum(
        "hqk,qhd->khd",
        prob_rows.astype(jnp.bfloat16),
        grad_mixture,
        preferred_element_type=jnp.float32,
    )
    grad_probs = jnp.einsum(
        "qhd,khd->hqk", grad_mixture, values, preferred_element_type=jnp.float32
    )
    row_dot = jnp.sum(prob_rows * grad_probs, axis=-1, keepdims=True)
    grad_scores = (prob_rows * (grad_probs - row_dot)).astype(jnp.bfloat16)
    grad_queries = (
        jnp.einsum("hqk,khd->qhd", grad_scores, key_rows, preferred_element_type=jnp.float32)
        * factor
    )
    grad_keys = (
        jnp.einsum("hqk,qhd->khd", grad_scores, queries, preferred_element_type=jnp.float32)
        * factor
    )
    return (grad_queries, grad_keys, grad_values)


def local(
    frames,
    lengths,
    span_starts,
    mask_embedding,
    norm1_gain,
    norm1_bias,
    qkv_weight,
    qv_bias,
    out_weight,
    out_bias,
    norm2_gain,
    norm2_bias,
    up_weight,
    up_bias,
    down_weight,
    down_bias,
    head_weight,
    head_bias,
    logit_grad,
):
    utterances_here, span_count = span_starts.shape
    row_count, model_width = frames.shape
    frame_count = row_count // utterances_here
    local_width = qkv_weight.shape[2]
    heads_here = local_width // HEAD_DIM
    f32, bf16 = jnp.float32, jnp.bfloat16
    first_share = lax.axis_index("tensor") == 0

    def mm(spec, left, right):
        return jnp.einsum(spec, left, right, preferred_element_type=f32)

    def split(wide):
        high = wide.astype(bf16)
        return jnp.concatenate([high, (wide - high.astype(f32)).astype(bf16)], axis=-1)

    places = jnp.arange(frame_count, dtype=jnp.int32)
    covered = (places[None, None, :] >= span_starts[:, :, None]) & (
        places[None, None, :] < span_starts[:, :, None] + MASK_SPAN
    )
    masked = jnp.any(covered, axis=1).reshape(row_count, 1)
    key_valid = places[None, :] < lengths[:, None]
    gain_one = norm1_gain.astype(f32)
    gain_two = norm2_gain.astype(f32)
    filled = jnp.where(masked, mask_embedding.astype(f32)[None, :], frames.astype(f32))
    first_norm, first_unit, first_inverse = norm_stats(filled, gain_one, norm1_bias.astype(f32))
    first_low = first_norm.astype(bf16)
    weight_flat = qkv_weight.reshape(model_width, 3 * local_width)
    bias_full = jnp.stack(
        [qv_bias[0].astype(f32), jnp.zeros((local_width,), f32), qv_bias[1].astype(f32)]
    ).reshape(3 * local_width)
    projected = (mm("rd,dc->rc", first_low, weight_flat) + bias_full).astype(bf16)
    triple = projected.reshape(utterances_here, frame_count, 3, heads_here, HEAD_DIM)
    queries = triple[:, :, 0]
    key_rows = triple[:, :, 1]
    values = triple[:, :, 2]
    mixture, log_total = lax.map(attend_forward, (queries, key_rows, values, key_valid))
    mixture_low = mixture.astype(bf16).reshape(row_count, local_width)
    mixture_all = lax.all_gather(mixture_low, "tensor", axis=1, tiled=True)
    out_all = lax.all_gather(out_weight, "tensor", axis=0, tiled=True)
    hidden = filled + mm("rl,ld->rd", mixture_all, out_all) + out_bias.astype(f32)
    second_norm, second_unit, second_inverse = norm_stats(hidden, gain_two, norm2_bias.astype(f32))
    second_low = second_norm.astype(bf16)
    up_rows = mm("rd,df->rf", second_low, up_weight) + up_bias.astype(f32)
    activ, gelu_pull = jax.vjp(partial(jax.nn.gelu, approximate=False), up_rows)
    activ_low = activ.astype(bf16)
    down_head = split(mm("fd,dv->fv", down_weight, head_weight))
    characters = head_weight.shape[1]
    own_logits = mm("rf,fv->rv", activ_low, down_head)
    own_logits = own_logits[:, :characters] + own_logits[:, characters:]
    hidden_down = (hidden + down_bias.astype(f32)).astype(bf16)
    logits = (
        lax.psum(own_logits, "tensor")
        + mm("rd,dv->rv", hidden_down, head_weight)
        + head_bias.astype(f32)
    )
    twice = jnp.concatenate([logit_grad, logit_grad], axis=1)
    grad_activ = mm("rv,fv->rf", twice, down_head)
    grad_up = gelu_pull(grad_activ)[0].astype(bf16)
    activ_head = mm("rf,rv->fv", activ_low, logit_grad)
    hidden_head = mm("rd,rv->dv", hidden_down, logit_grad)
    head_bias_grad = jnp.sum(logit_grad.astype(f32), axis=0)
    up_grad = mm("rd,rf->df", second_low, grad_up)
    up_bias_grad = jnp.sum(grad_up.astype(f32), axis=0)
    grad_second = mm("rf,df->rd", grad_up, up_weight)
    norm2_gain_grad = jnp.sum(grad_second * second_unit, axis=0)
    norm2_bias_grad = jnp.sum(grad_second, axis=0)
    grad_output = mm("rv,dv->rd", logit_grad, head_weight)
    grad_hidden = norm_back(grad_second, second_unit, second_inverse, gain_two) + jnp.where(
        first_share, grad_output, 0.0
    )
    grad_attn = grad_hidden.astype(bf16)
    out_bias_grad = jnp.sum(grad_hidden, axis=0)
    grad_mixture = lax.psum_scatter(
        mm("rd,ld->rl", grad_attn, out_all).astype(bf16), "tensor", scatter_dimension=1, tiled=True
    )
    out_grad = lax.psum_scatter(
        mm("rl,rd->ld", mixture_all, grad_attn).astype(bf16),
        "tensor",
        scatter_dimension=0,
        tiled=True,
    )
    grad_mixture = grad_mixture.reshape(utterances_here, frame_count, heads_here, HEAD_DIM)
    grad_queries, grad_keys, grad_values = lax.map(
        attend_backward, (queries, key_rows, values, key_valid, log_total, grad_mixture)
    )
    grad_triple = (
        jnp.stack([grad_queries, grad_keys, grad_values], axis=2)
        .astype(bf16)
        .reshape(row_count, 3 * local_width)
    )
    qkv_grad = mm("rd,rc->dc", first_low, grad_triple).reshape(model_width, 3, local_width)
    column_sums = jnp.sum(grad_triple.astype(f32), axis=0).reshape(3, local_width)
    qv_bias_grad = jnp.stack([column_sums[0], column_sums[2]])
    grad_first = mm("rc,dc->rd", grad_triple, weight_flat)
    norm1_gain_grad = jnp.sum(grad_first * first_unit, axis=0)
    norm1_bias_grad = jnp.sum(grad_first, axis=0)
    grad_filled = grad_hidden + norm_back(grad_first, first_unit, first_inverse, gain_one)
    mask_grad = jnp.sum(jnp.where(masked, grad_filled, 0.0), axis=0)
    frames_grad = jnp.where(masked, 0.0, grad_filled).astype(bf16)
    frames_grad = lax.all_gather(
        lax.psum_scatter(frames_grad, "tensor", scatter_dimension=0, tiled=True),
        "tensor",
        axis=0,
        tiled=True,
    ).astype(f32)
    up_grad = lax.psum(up_grad.astype(bf16), "dp").astype(f32)
    out_grad = lax.psum(out_grad, "dp").astype(f32)
    qkv_grad = lax.psum(qkv_grad.astype(bf16), "dp").astype(f32)
    activ_head, up_bias_grad, qv_bias_grad, head_bias_grad, hidden_head = lax.psum(
        (activ_head, up_bias_grad, qv_bias_grad, head_bias_grad, hidden_head), "dp"
    )
    activ_split = split(activ_head)
    head_twice = jnp.concatenate([head_weight, head_weight], axis=1)
    down_grad = mm("fv,dv->fd", activ_split, head_twice)
    down_head_grad = mm("fd,fv->dv", down_weight, activ_split)
    down_head_grad = down_head_grad[:, :characters] + down_head_grad[:, characters:]
    down_bias_grad = jnp.dot(
        head_weight.astype(f32), head_bias_grad, precision=lax.Precision.HIGHEST
    )
    mask_grad, norm1_gain_grad, norm1_bias_grad, norm2_gain_grad, norm2_bias_grad, out_bias_grad = (
        lax.psum(
            (
                mask_grad,
                norm1_gain_grad,
                norm1_bias_grad,
                norm2_gain_grad,
                norm2_bias_grad,
                out_bias_grad,
            ),
            ("dp", "tensor"),
        )
    )
    head_grad = hidden_head + lax.psum(down_head_grad, "tensor")
    return (
        logits,
        frames_grad,
        mask_grad,
        norm1_gain_grad,
        norm1_bias_grad,
        qkv_grad,
        qv_bias_grad,
        out_grad,
        out_bias_grad,
        norm2_gain_grad,
        norm2_bias_grad,
        up_grad,
        up_bias_grad,
        down_grad,
        down_bias_grad,
        head_grad,
        head_bias_grad,
    )


f32, bf16 = jnp.float32, jnp.bfloat16
WIDTH = 1024
LOCAL = 512
FFL = 2048
ROWS = 896
CHARS = 32
CHUNK = 224
PIECE = 32
FEED = 448


def dot(left, right):
    return lax.dot_general(left, right, (((1,), (0,)), ((), ())), preferred_element_type=f32)


def dot_nt(left, right):
    return lax.dot_general(left, right, (((1,), (1,)), ((), ())), preferred_element_type=f32)


def dot_tn(left, right):
    return lax.dot_general(left, right, (((0,), (0,)), ((), ())), preferred_element_type=f32)


def aligned(start, size):
    return pl.ds(pl.multiple_of(start, size), size)


def fold_rows(block):
    rows, width = block.shape
    return jnp.sum(block.reshape(rows // 8, 8, width), axis=0)


def col_sum(block):
    return jnp.sum(fold_rows(block), axis=0, keepdims=True)


def gelu_parts(block):
    bell = jnp.exp(block * block * -0.5)
    cdf = 0.5 + 0.5 * lax.erf(block * (0.5**0.5))
    return block * cdf, cdf + block * bell * 0.3989422804014327


MEM = pltpu.VMEM
INPUTS = dict(
    frames=None,
    lengths=MEM,
    starts=MEM,
    mask_embedding=MEM,
    norm1_gain=MEM,
    norm1_bias=MEM,
    out_bias=MEM,
    norm2_gain=MEM,
    norm2_bias=MEM,
    down_bias=MEM,
    qv_bias=MEM,
    up_bias=MEM,
    qkv_w=None,
    out_w=None,
    up_w=None,
    down_w=None,
    head_w=MEM,
    head_b=MEM,
    logit_grad=MEM,
)
OUTPUTS = dict(
    logits=((CHARS, ROWS), f32, MEM),
    frames_grad=((ROWS, WIDTH), bf16, None),
    up_o=((WIDTH, FFL), bf16, None),
    out_o=((LOCAL, WIDTH), bf16, None),
    qkv_o=((3 * WIDTH, LOCAL), bf16, None),
    small_o=((256, LOCAL), bf16, None),
    tiny_o=((16, WIDTH), f32, MEM),
)
SCRATCH = dict(
    vec=((16, WIDTH), f32),
    x=((ROWS, WIDTH), bf16),
    wqkv=((3, WIDTH, LOCAL), bf16),
    first=((ROWS, WIDTH), bf16),
    first_t=((WIDTH, ROWS), bf16),
    qkv=((3, ROWS, LOCAL), bf16),
    mix=((ROWS, WIDTH), bf16),
    ow=((WIDTH, WIDTH), bf16),
    upw=((4 * WIDTH, LOCAL), bf16),
    big=((2 * WIDTH, WIDTH), bf16),
    lse=((128, ROWS), f32),
    dh=((FFL, 128), bf16),
    hw2=((WIDTH, 128), bf16),
    hw1=((WIDTH, 128), bf16),
    gd=((ROWS, 128), bf16),
    lp=((ROWS, 128), f32),
    lpt=((CHARS, ROWS), f32),
    lpr=((CHARS, ROWS), f32),
    second=((ROWS, WIDTH), bf16),
    work=((256, WIDTH), f32),
    unit=((ROWS, WIDTH), bf16),
    gu=((ROWS, FFL), bf16),
    pb=((ROWS, WIDTH), bf16),
    pm_own=((ROWS, LOCAL), bf16),
    pm_recv=((ROWS, LOCAL), bf16),
    nt=((CHARS, FFL), f32),
    hh=((CHARS, WIDTH), f32),
    ub=((8, FFL), f32),
    cs=((16, WIDTH), f32),
    gqt=((256, ROWS), f32),
    gk=((ROWS, 256), f32),
    gv=((ROWS, 256), f32),
    turn=((WIDTH, ROWS), bf16),
    og=((WIDTH, WIDTH), bf16),
    og_rc=((2, 256, WIDTH), bf16),
    og_ry=((256, WIDTH), bf16),
    sy=((48, WIDTH), f32),
    sy_r=((48, WIDTH), f32),
    sm=((256, LOCAL), bf16),
    f_recv=((ROWS, WIDTH), bf16),
    ty=((2, 16, WIDTH), f32),
    tc=((16, WIDTH), f32),
    tt=((16, WIDTH), f32),
    ty_r=((16, WIDTH), f32),
    tx=((16, WIDTH), f32),
    tz=((4, 16, WIDTH), f32),
)
PARTS = dict(
    u0=(1024, 512),
    u1=(1024, 512),
    u2=(1024, 512),
    u3=(1024, 512),
    o=(512, 1024),
    s=(256, 512),
    q00=(1024, 256),
    q10=(1024, 256),
    q20=(1024, 256),
    q02=(1024, 128),
    q12=(1024, 128),
    q22=(1024, 128),
    q03=(1024, 128),
    q13=(1024, 128),
    q23=(1024, 128),
)


def places(k):
    found = dict(
        o=(k.og, k.t * LOCAL, 0, k.out_o, 0, 0),
        s=(k.sm, 0, 0, k.small_o, 0, 0),
        q00=(k.upw, 0, 0, k.qkv_o, 0, 0),
        q10=(k.upw, 1024, 0, k.qkv_o, 1024, 0),
        q20=(k.upw, 2048, 0, k.qkv_o, 2048, 0),
        q02=(k.upw, 0, 256, k.qkv_o, 0, 256),
        q12=(k.upw, 1024, 256, k.qkv_o, 1024, 256),
        q22=(k.upw, 2048, 256, k.qkv_o, 2048, 256),
        q03=(k.upw, 0, 384, k.qkv_o, 0, 384),
        q13=(k.upw, 1024, 384, k.qkv_o, 1024, 384),
        q23=(k.upw, 2048, 384, k.qkv_o, 2048, 384),
        u0=(k.big, 0, 0, k.up_o, 0, 0),
        u1=(k.big, 0, 512, k.up_o, 0, 512),
        u2=(k.big, 1024, 0, k.up_o, 0, 1024),
        u3=(k.big, 1024, 512, k.up_o, 0, 1536),
    )
    return found


class Sum:
    def __init__(self, k, shape, place, landing, base):
        self.k = k
        self.rows, self.width = rows, _ = shape
        self.src, self.row0, self.col0, self.out, self.orow0, self.ocol0 = place
        self.rx, self.rz, self.rc = landing
        self.base = base
        self.half, self.quarter, self.piece = rows // 2, rows // 4, rows // 16
        self.b1 = k.c * self.half
        self.b2 = self.b1 + k.x_ * self.quarter
        self.b3 = self.b2 + k.z * self.piece

    def at(self, start, size):
        return self.src.at[aligned(self.row0 + start, size), pl.ds(self.col0, self.width)]

    def out_at(self, start, size):
        return self.out.at[aligned(self.orow0 + start, size), pl.ds(self.ocol0, self.width)]

    def add(self, start, size, others):
        step = min(size, 64 if size % 64 == 0 else 96 if size % 96 == 0 else 32)

        def body(i, carry):
            rows = aligned(self.row0 + start + i * step, step)
            cols = pl.ds(self.col0, self.width)
            total = self.src[rows, cols].astype(f32)
            for other in others:
                total += other[aligned(i * step, step), :].astype(f32)
            self.src[rows, cols] = total.astype(bf16)
            return carry

        lax.fori_loop(0, size // step, body, 0)

    def core(self):
        k = self.k
        self.h_core = k.copy(self.base, self.at((1 - k.c) * self.half, self.half), self.rc, k.core_peer)
        self.h_core.start()

    def x(self):
        k = self.k
        if self.rc is not None:
            self.h_core.wait()
            self.add(self.b1, self.half, [self.rc])
        self.h_x = k.copy(
            self.base + 1,
            self.at(self.b1 + (1 - k.x_) * self.quarter, self.quarter),
            self.rx,
            k.x_peer,
        )
        self.h_x.start()

    def spread(self):
        k = self.k
        self.h_x.wait()
        self.add(self.b2, self.quarter, [self.rx])
        self.h_z = []
        for s in range(1, 4):
            there = lax.rem(k.z + s, 4)
            handle = k.copy(
                self.base + 1 + s,
                self.at(self.b2 + there * self.piece, self.piece),
                self.rz.at[s - 1],
                k.z_peer(s),
            )
            handle.start()
            self.h_z.append(handle)

    def gather(self):
        k = self.k
        for handle in self.h_z:
            handle.wait()
        self.add(self.b3, self.piece, [self.rz.at[s] for s in range(3)])
        mine = self.out_at(self.b3, self.piece)
        self.h_own = pltpu.make_async_copy(self.at(self.b3, self.piece), mine, k.sem.at[self.base + 10])
        self.h_own.start()
        self.h_zg = []
        for s in range(1, 4):
            handle = k.copy(self.base + 4 + s, self.at(self.b3, self.piece), mine, k.z_peer(s))
            handle.start()
            self.h_zg.append(handle)

    def x_back(self):
        k = self.k
        self.h_own.wait()
        for handle in self.h_zg:
            handle.wait()
        block = self.out_at(self.b2, self.quarter)
        self.h_xg = k.copy(self.base + 8, block, block, k.x_peer)
        self.h_xg.start()

    def core_back(self):
        k = self.k
        self.h_xg.wait()
        block = self.out_at(self.b1, self.half)
        self.h_cg = k.copy(self.base + 9, block, block, k.core_peer)
        self.h_cg.start()

    def end(self):
        self.h_cg.wait()


SEM_LOCAL, SEM_OW, SEM_MIX, SEM_PM, SEM_OG, SEM_F, SEM_TINY, SEM_SUM = 0, 16, 32, 36, 40, 48, 52, 60
SEM_COUNT = SEM_SUM + 11 * len(PARTS)


def landing_shapes():
    shapes = []
    for rows, width in PARTS.values():
        shapes += [(rows // 4, width), (3, rows // 16, width), (rows // 2, width)]
    return shapes


def fused(*refs):
    names = list(INPUTS) + list(OUTPUTS) + list(SCRATCH)
    k = SimpleNamespace(**dict(zip(names, refs)))
    landing = refs[len(names) : -2]
    k.sem, k.rsem = refs[-2:]
    place = lax.axis_index("dp")
    k.t = lax.axis_index("tensor")
    k.z, k.x_, k.c = place // 4, lax.rem(place // 2, 2), lax.rem(place, 2)
    k.core_peer = {"dp": place + 1 - 2 * k.c}
    k.x_peer = {"dp": place + 2 - 4 * k.x_}
    k.y_peer = {"tensor": 1 - k.t}
    k.z_peer = lambda s: {"dp": lax.rem(k.z + s, 4) * 4 + k.x_ * 2 + k.c}

    def copy(number, src, dst, device):
        return pltpu.make_async_remote_copy(
            src_ref=src,
            dst_ref=dst,
            send_sem=k.sem.at[number],
            recv_sem=k.rsem.at[number],
            device_id=device,
            device_id_type=pl.DeviceIdType.MESH,
        )

    k.copy = copy
    mine = aligned(k.t * LOCAL, LOCAL)
    other = aligned((1 - k.t) * LOCAL, LOCAL)

    def load(number, src, dst):
        handle = pltpu.make_async_copy(src, dst, k.sem.at[SEM_LOCAL + number])
        handle.start()
        return handle

    load_x = load(0, k.frames, k.x)
    load_wqkv = load(1, k.qkv_w, k.wqkv)
    load_ow = load(2, k.out_w, k.ow.at[mine, :])
    load_big = load(3, k.down_w, k.big)
    load_upw = [
        load(4 + j, k.up_w.at[:, pl.ds(j * 512, 512)], k.upw.at[pl.ds(j * 1024, 1024), :])
        for j in range(4)
    ]
    barrier = pltpu.get_barrier_semaphore()
    peers = [k.core_peer, k.x_peer, k.y_peer, k.z_peer(1), k.z_peer(2), k.z_peer(3)]
    for peer in peers:
        pl.semaphore_signal(barrier, inc=1, device_id=peer, device_id_type=pl.DeviceIdType.MESH)
    pl.semaphore_wait(barrier, len(peers))

    for number, ref in enumerate(
        (
            k.mask_embedding,
            k.norm1_gain,
            k.norm1_bias,
            k.out_bias,
            k.norm2_gain,
            k.norm2_bias,
            k.down_bias,
        )
    ):
        k.vec[number : number + 1, :] = ref[...].astype(f32).reshape(1, WIDTH)
    k.vec[7:9, 0:LOCAL] = k.qv_bias[...].astype(f32)
    k.vec[9:11, :] = k.up_bias[...].astype(f32).reshape(2, WIDTH)
    emb, gain1, bias1, out_bias, gain2, bias2, down_bias = (
        k.vec[i : i + 1, :] for i in range(7)
    )
    lane = lax.broadcasted_iota(jnp.int32, (1, 128), 1)
    first_share = jnp.where(k.t == 0, 1.0, 0.0).astype(f32)

    def filled_rows(start, size):
        ids = lax.broadcasted_iota(jnp.int32, (size, k.starts.shape[1]), 0) + start
        begin = k.starts[...]
        inside = jnp.where((ids >= begin) & (ids < begin + MASK_SPAN), 1.0, 0.0)
        column = jnp.max(inside, axis=1, keepdims=True)
        flag = jnp.broadcast_to(column, (size, WIDTH)) > 0.5
        if isinstance(start, int):
            rows = pl.ds(start, size)
        else:
            rows = aligned(start, size)
        return jnp.where(flag, emb, k.x[rows, :].astype(f32)), flag

    load_ow.wait()

    def ow_rows(tensor, x, z, size):
        return k.ow.at[aligned(tensor * LOCAL + k.c * 256 + x * 128 + z * 32, size), :]

    strip = ow_rows(k.t, k.x_, k.z, 32)
    ow_steps = [k.copy(SEM_OW, strip, strip, k.y_peer)]
    ow_steps[0].start()

    def ow_z():
        ow_steps[0].wait()
        strip = ow_rows(1 - k.t, k.x_, k.z, 32)
        for n in range(1, 4):
            ow_steps.append(k.copy(SEM_OW + n, strip, strip, k.z_peer(n)))
            ow_steps[-1].start()

    def ow_x():
        for handle in ow_steps[1:4]:
            handle.wait()
        strip = ow_rows(1 - k.t, k.x_, 0, 128)
        ow_steps.append(k.copy(SEM_OW + 4, strip, strip, k.x_peer))
        ow_steps[-1].start()

    def ow_core():
        ow_steps[4].wait()
        strip = ow_rows(1 - k.t, 0, 0, 256)
        ow_steps.append(k.copy(SEM_OW + 5, strip, strip, k.core_peer))
        ow_steps[-1].start()

    load_x.wait()

    def ln1(i, carry):
        filled, _ = filled_rows(i * 128, 128)
        norm, _, _ = norm_stats(filled, gain1, bias1)
        k.first[aligned(i * 128, 128), :] = norm.astype(bf16)
        return carry

    lax.fori_loop(0, ROWS // 128, ln1, 0)
    def key_bias_of(start, size):
        ids = lax.broadcasted_iota(jnp.int32, (size, 1), 0) + start
        return jnp.where(ids < k.lengths[...].reshape(1, 1), 0.0, NEG).astype(f32)

    key_bias = key_bias_of(0, ROWS)

    def mix_copy(p):
        strip = k.mix.at[:, aligned(k.t * LOCAL + p * 128, 128)]
        return k.copy(SEM_MIX + p, strip, strip, k.y_peer)

    sub = lax.broadcasted_iota(jnp.int32, (128, 1), 0)

    def forward_pair(p):
        cols = pl.ds(p * 128, 128)
        q_pair = k.qkv[0, :, cols].astype(f32) * HEAD_DIM ** (-0.5)
        k_pair = k.qkv[1, :, cols].astype(f32)
        v_turn = k.qkv[2, :, cols].astype(f32).T
        keys, values = [], []
        for h in range(2):
            half = (lane < 64) if h == 0 else (lane >= 64)
            rows = (sub < 64) if h == 0 else (sub >= 64)
            extra = 64 - 64 * h
            tail = jnp.where(lane == extra, key_bias, 0.0)
            keys.append(jnp.where(half, k_pair, tail).astype(bf16))
            tail = jnp.where(sub == extra, 1.0, 0.0)
            values.append(jnp.where(rows, v_turn, tail).astype(bf16))
        for start in range(0, ROWS, 128):
            span = slice(start, start + 128)
            made = []
            for h in range(2):
                half = (lane < 64) if h == 0 else (lane >= 64)
                extra = 64 - 64 * h
                tail = jnp.where(lane == extra, 1.0, 0.0)
                query = jnp.where(half, q_pair[span], tail).astype(bf16)
                scores = dot_nt(keys[h], query)
                peak = jnp.max(scores, axis=0, keepdims=True)
                weights = jnp.exp(scores - peak).astype(bf16)
                both = dot(values[h], weights)
                total = both[extra : extra + 1, :]
                made.append(both / total)
                k.lse[2 * p + h : 2 * p + h + 1, span] = peak + jnp.log(total)
            k.mix[span, aligned(k.t * LOCAL + p * 128, 128)] = (
                jnp.where(sub < 64, made[0], made[1]).T.astype(bf16)
            )
        mix_copy(p).start()

    load_wqkv.wait()
    k.lse[...] = jnp.zeros_like(k.lse)
    for half in range(2):
        cols = pl.ds(half * 256, 256)
        for m in range(3):
            bias = None if m == 1 else k.vec[7 + m // 2 : 8 + m // 2, cols]

            def project(i, carry, m=m, bias=bias, cols=cols):
                rows = aligned(i * 448, 448)
                value = dot(k.first[rows, :], k.wqkv[m, :, cols])
                k.qkv[m, rows, cols] = (value if bias is None else value + bias).astype(bf16)
                return carry

            lax.fori_loop(0, ROWS // 448, project, 0)
        if half == 0:
            ow_z()
        forward_pair(2 * half)
        if half == 0:
            ow_x()
        forward_pair(2 * half + 1)
        if half == 0:
            ow_core()

    def turn_rows(src, dst):
        def body(i, carry):
            cols = aligned(i * 128, 128)
            dst[cols, :] = src[:, cols].T
            return carry

        lax.fori_loop(0, WIDTH // 128, body, 0)

    turn_rows(k.first, k.first_t)
    pick = lax.broadcasted_iota(jnp.int32, (CHARS, 128), 0)
    spot = lax.broadcasted_iota(jnp.int32, (CHARS, 128), 1)
    once = jnp.where(pick == spot, 1.0, 0.0).astype(bf16)
    twice = jnp.where((pick == spot) | (pick + CHARS == spot), 1.0, 0.0).astype(bf16)
    k.hw1[...] = dot_tn(k.head_w[...], once).astype(bf16)
    k.hw2[...] = dot_tn(k.head_w[...], twice).astype(bf16)
    k.gd[...] = dot_tn(k.logit_grad[...], twice).astype(bf16)
    load_big.wait()

    def fold(i, carry):
        rows = aligned(i * 512, 512)
        value = dot(k.big[rows, :], k.hw2[...])
        high = value.astype(bf16).astype(f32)
        k.dh[rows, :] = jnp.where(lane < CHARS, high, value - high).astype(bf16)
        return carry

    lax.fori_loop(0, 4, fold, 0)
    k.nt[...] = jnp.zeros_like(k.nt)
    k.hh[...] = jnp.zeros_like(k.hh)
    k.ub[...] = jnp.zeros_like(k.ub)
    k.cs[...] = jnp.zeros_like(k.cs)
    ow_steps[5].wait()
    for handle in load_upw:
        handle.wait()

    def mix_wait(p, carry):
        mix_copy(p).wait()
        return carry

    lax.fori_loop(0, 4, mix_wait, 0)

    def pm_copy(i):
        rows = aligned(i * CHUNK, CHUNK)
        return k.copy(SEM_PM + i, k.first.at[rows, pl.ds(0, LOCAL)], k.pm_recv.at[rows, :], k.y_peer)

    def hidden_rows(i, carry):
        start = i * CHUNK
        rows = aligned(start, CHUNK)
        k.work[0:CHUNK, :] = dot(k.mix[rows, :], k.ow[...])
        for n in range(0, CHUNK, PIECE):
            piece = aligned(start + n, PIECE)
            filled, _ = filled_rows(start + n, PIECE)
            hidden = filled + k.work[n : n + PIECE, :] + out_bias
            second, unit, inverse = norm_stats(hidden, gain2, bias2)
            k.second[piece, :] = second.astype(bf16)
            k.unit[piece, :] = unit.astype(bf16)
            k.lp[piece, :] = jnp.broadcast_to(inverse, (PIECE, 128))
            k.pb[piece, :] = (hidden + down_bias).astype(bf16)
        down = k.pb[rows, :]
        head = dot(down, k.hw1[...]) * 0.5
        k.lp[rows, :] = jnp.where(lane == 64, k.lp[rows, :], head)
        k.hh[...] += dot_tn(k.gd[rows, :], down)[:CHARS] * first_share
        return carry

    lax.fori_loop(0, ROWS // CHUNK, hidden_rows, 0)
    turn_rows(k.second, k.turn)

    def feed(j):
        again = load(12 + j % 2, k.down_w.at[pl.ds(j * 512, 512), :], k.pb.at[pl.ds(0, 512), :])
        cols = pl.ds(j * 512, 512)
        bias = k.vec[9 + j // 2 : 10 + j // 2, pl.ds((j % 2) * 512, 512)]

        def body(i, carry):
            rows = aligned(i * FEED, FEED)
            grad = k.gd[rows, :]
            up = dot(k.second[rows, :], k.upw[pl.ds(j * 1024, 1024), :]) + bias
            act, slope = gelu_parts(up)
            act = act.astype(bf16)
            k.lp[rows, :] += dot(act, k.dh[cols, :])
            k.nt[:, cols] += dot_tn(grad, act)[:CHARS]
            grad_up = (dot_nt(grad, k.dh[cols, :]) * slope).astype(bf16)
            k.gu[rows, cols] = grad_up
            k.ub[0:1, cols] += col_sum(grad_up.astype(f32))
            return carry

        lax.fori_loop(0, ROWS // FEED, body, 0)
        again.wait()
        turned = k.nt[:, cols]
        high = turned.astype(bf16)
        rest = (turned - high.astype(f32)).astype(bf16)
        k.hh[...] += dot(high, k.pb[0:512, :]) + dot(rest, k.pb[0:512, :])

    def norm2_back(i):
        rows = pl.ds(i * CHUNK, CHUNK)
        k.work[0:CHUNK, :] = dot_nt(k.gu[rows, 0:512], k.upw[0:1024, :])
        for j in range(1, 4):
            k.work[0:CHUNK, :] += dot_nt(
                k.gu[rows, pl.ds(j * 512, 512)], k.upw[pl.ds(j * 1024, 1024), :]
            )
        sums2 = [jnp.zeros((8, WIDTH), f32)] * 3
        for n in range(0, CHUNK, PIECE):
            piece = pl.ds(i * CHUNK + n, PIECE)
            grad_second = k.work[n : n + PIECE, :]
            unit = k.unit[piece, :].astype(f32)
            spread = norm_back(grad_second, unit, k.lp[piece, 64:65], gain2)
            spread += dot_nt(k.gd[piece, :], k.hw1[...]) * first_share
            k.pb[piece, :] = spread.astype(bf16)
            sums2 = [
                total + fold_rows(term)
                for total, term in zip(sums2, (grad_second * unit, grad_second, spread))
            ]
        for n in range(3):
            k.cs[3 + n : 4 + n, :] += jnp.sum(sums2[n], axis=0, keepdims=True)
        low = k.pb[rows, :]
        k.first[rows, 0:LOCAL] = dot_nt(low, k.ow[other, :]).astype(bf16)
        pm_copy(i).start()
        k.pm_own[rows, :] = dot_nt(low, k.ow[mine, :]).astype(bf16)

    found = places(k)
    sums = SimpleNamespace(
        **{
            name: Sum(k, PARTS[name], found[name], landing[3 * n : 3 * n + 3], SEM_SUM + 11 * n)
            for n, name in enumerate(PARTS)
        }
    )
    sums.o.rc = None
    def up_grad(j):
        for n in range(2):
            k.big[pl.ds((j // 2) * 1024, 1024), pl.ds((j % 2) * 512 + n * 256, 256)] = dot(
                k.turn[...], k.gu[:, pl.ds(j * 512 + n * 256, 256)]
            ).astype(bf16)

    og_core, y_sums = [], []

    def out_grad():
        turn_rows(k.mix, k.turn)

        def out_block(i, carry):
            cols = aligned(i * 256, 256)
            k.og[:, cols] = dot(k.turn[...], k.pb[:, cols]).astype(bf16)
            return carry

        lax.fori_loop(0, 4, out_block, 0)
        for part in range(2):
            handle = k.copy(
                SEM_OG + part,
                k.og.at[aligned(part * LOCAL + (1 - k.c) * 256, 256), :],
                k.og_rc.at[part],
                k.core_peer,
            )
            handle.start()
            og_core.append(handle)
        k.sy[0:32, :] = k.hh[...]
        k.sy[32:48, :] = k.cs[...]
        sy_copy = k.copy(SEM_OG + 2, k.sy, k.sy_r, k.y_peer)
        sy_copy.start()
        y_sums.append(sy_copy)
        k.lpt[...] = (k.lp[...] + pltpu.roll(k.lp[...], 96, 1)).T[:CHARS]
        lp_copy = k.copy(SEM_OG + 3, k.lpt, k.lpr, k.y_peer)
        lp_copy.start()
        y_sums.append(lp_copy)

    def og_add(base, other):
        def body(i, carry):
            rows = aligned(base + i * 64, 64)
            total = k.og[rows, :].astype(f32) + other[aligned(i * 64, 64), :].astype(f32)
            k.og[rows, :] = total.astype(bf16)
            return carry

        lax.fori_loop(0, 4, body, 0)

    def og_pair():
        for part in range(2):
            og_core[part].wait()
            og_add(part * LOCAL + k.c * 256, k.og_rc.at[part])
        handle = k.copy(
            SEM_OG + 4,
            k.og.at[aligned((1 - k.t) * LOCAL + k.c * 256, 256), :],
            k.og_ry,
            k.y_peer,
        )
        handle.start()
        og_core.append(handle)

    def og_cross():
        og_core[2].wait()
        og_add(k.t * LOCAL + k.c * 256, k.og_ry)
        sums.o.x()

    def small():
        for handle in y_sums:
            handle.wait()
        k.logits[...] = k.lpt[...] + k.lpr[...] + k.head_b[...].astype(f32).reshape(CHARS, 1)
        k.sy[...] += k.sy_r[...]
        for j in range(4):
            k.sm[j * 32 : j * 32 + 32, :] = k.nt[:, j * 512 : (j + 1) * 512].astype(bf16)
        for j in range(2):
            cols = slice(j * 512, (j + 1) * 512)
            k.sm[128 + j * 32 : 160 + j * 32, :] = k.sy[0:32, cols].astype(bf16)
            k.sm[192 + j * 16 : 208 + j * 16, :] = k.sy[32:48, cols].astype(bf16)
        sub = lax.broadcasted_iota(jnp.int32, (16, 1), 0)
        total = jnp.sum(k.gd[...].astype(f32), axis=0, keepdims=True)
        total = jnp.concatenate([total, jnp.zeros((1, 384), f32)], axis=1)
        last_rows = jnp.where(sub == 4, total, 0.0)
        for j in range(4):
            last_rows = jnp.where(sub == j, k.ub[0:1, j * 512 : (j + 1) * 512], last_rows)
        k.sm[224:240, :] = last_rows.astype(bf16)
        k.sm[240:256, :] = jnp.zeros((16, LOCAL), bf16)
        sums.s.core()

    def pm_wait(i, carry):
        pm_copy(i).wait()
        return carry

    def heads_ready(n, carry):
        rows = aligned(n * 128, 128)
        shifts = -k.lse[:, rows].T
        for p in range(4):
            pair_ready(p, rows, shifts, key_bias_of(n * 128, 128))
        return carry

    def pair_ready(p, rows, shifts, bias):
        cols = pl.ds(p * 128, 128)
        mixed = k.mix[rows, aligned(k.t * LOCAL + p * 128, 128)].astype(f32)
        grad_pair = k.pm_own[rows, cols].astype(f32) + k.pm_recv[rows, cols].astype(f32)
        grad_pair = grad_pair.astype(bf16).astype(f32)
        q_pair = k.qkv[0, rows, cols].astype(f32) * HEAD_DIM ** (-0.5)
        k_pair = k.qkv[1, rows, cols].astype(f32)
        v_pair = k.qkv[2, rows, cols].astype(f32)
        for h in range(2):
            head = pl.ds((2 * p + h) * 128, 128)
            half = (lane < 64) if h == 0 else (lane >= 64)
            e = 64 - 64 * h
            shift = shifts[:, 2 * p + h : 2 * p + h + 1]
            one = shift.astype(bf16).astype(f32)
            two = (shift - one).astype(bf16).astype(f32)
            tail = jnp.where(lane == e + 3, shift - one - two, 0.0)
            tail = jnp.where(lane == e + 1, one, jnp.where(lane == e + 2, two, tail))
            tail = jnp.where(lane == e, 1.0, tail)
            k.second[rows, head] = jnp.where(half, q_pair, tail).astype(bf16)
            tail = jnp.where((lane > e) & (lane < e + 4), 1.0, 0.0)
            tail = jnp.where(lane == e, bias, tail)
            k.unit[rows, head] = jnp.where(half, k_pair, tail).astype(bf16)
            tail = jnp.where((lane >= e) & (lane < e + 2), 1.0, 0.0)
            k.ow[rows, head] = jnp.where(half, v_pair, tail).astype(bf16)
            total = -jnp.sum(jnp.where(half, grad_pair * mixed, 0.0), axis=1, keepdims=True)
            one = total.astype(bf16).astype(f32)
            tail = jnp.where(lane == e, one, jnp.where(lane == e + 1, total - one, 0.0))
            k.first[rows, head] = jnp.where(half, grad_pair, tail).astype(bf16)

    def prepare():
        lax.fori_loop(0, ROWS // CHUNK, pm_wait, 0)
        lax.fori_loop(0, ROWS // 128, heads_ready, 0)

    def backward_block(p, key_rows, query_rows, assign):
        made = []
        for h in range(2):
            head = pl.ds((2 * p + h) * 128, 128)
            query, key = k.second[query_rows, head], k.unit[key_rows, head]
            value, grad = k.ow[key_rows, head], k.first[query_rows, head]
            probs = jnp.exp(dot_nt(key, query))
            change = (probs * dot_nt(value, grad)).astype(bf16)
            made.append(
                (dot(change, query), dot(probs.astype(bf16), grad), dot_tn(key, change))
            )
        cols = pl.ds((p % 2) * 128, 128)
        for dst, at, n, low in (
            (k.gk, (key_rows, cols), 0, lane < 64),
            (k.gv, (key_rows, cols), 1, lane < 64),
            (k.gqt, (cols, query_rows), 2, sub < 64),
        ):
            total = jnp.where(low, made[0][n], made[1][n])
            if n == 2 and assign[1] or n < 2 and assign[0]:
                dst[at] = total
            else:
                dst[at] += total

    BLOCKS = ((0, 256), (256, 256), (512, 256), (768, 128))

    def backward_half(p, half):
        for start in range(half * 448, half * 448 + 448, 224):
            backward_block(p, pl.ds(start, 224), pl.ds(0, ROWS), (True, start == 0))

    def backward_step(i, p):
        start, size = BLOCKS[i]
        rows = pl.ds(start, size)
        rest = ROWS - start - size
        whole = ROWS - start
        first = 512 if whole > 512 else whole
        backward_block(p, pl.ds(start, first), rows, (i == 0, i == 0))
        if whole > first:
            backward_block(p, pl.ds(start + first, whole - first), rows, (i == 0, False))
        if rest:
            backward_block(p, rows, pl.ds(start + size, rest), (False, i == 0))

    def backward_end(pair, width, start, size):
        rows = pl.ds(start, size)
        own, at = pl.ds((pair % 2) * 128, width), pair * 128
        k.gu[rows, pl.ds(at, width)] = (k.gqt[own, rows] * HEAD_DIM ** (-0.5)).T.astype(bf16)
        k.gu[rows, pl.ds(LOCAL + at, width)] = k.gk[rows, own].astype(bf16)
        k.gu[rows, pl.ds(2 * LOCAL + at, width)] = k.gv[rows, own].astype(bf16)

    def qkv_grad(m, pair, width):
        k.upw[pl.ds(m * 1024, 1024), pl.ds(pair * 128, width)] = dot(
            k.first_t[...], k.gu[:, pl.ds(m * LOCAL + pair * 128, width)]
        ).astype(bf16)

    def f_copy(i):
        rows = pl.ds(*BLOCKS[i])
        return k.copy(SEM_F + i, k.mix.at[rows, :], k.f_recv.at[rows, :], k.y_peer)

    def f_out(i):
        rows = pl.ds(*BLOCKS[i])
        return pltpu.make_async_copy(
            k.mix.at[rows, :], k.frames_grad.at[rows, :], k.sem.at[SEM_LOCAL + 8 + i]
        )

    def frames_part(i):
        start, size = BLOCKS[i]
        rows = pl.ds(start, size)
        k.work[0:size, :] = dot_nt(k.gu[rows, 0:LOCAL], k.wqkv[0])
        for m in range(1, 3):
            k.work[0:size, :] += dot_nt(k.gu[rows, pl.ds(m * LOCAL, LOCAL)], k.wqkv[m])
        sums1 = [jnp.zeros((8, WIDTH), f32)] * 3
        for n in range(0, size, PIECE):
            piece = pl.ds(start + n, PIECE)
            filled, flag = filled_rows(start + n, PIECE)
            _, unit, inverse = norm_stats(filled, gain1, bias1)
            grad = k.work[n : n + PIECE, :]
            total = k.pb[piece, :].astype(f32) + norm_back(grad, unit, inverse, gain1)
            k.mix[piece, :] = jnp.where(flag, 0.0, total).astype(bf16)
            sums1 = [
                total_n + fold_rows(term)
                for total_n, term in zip(sums1, (jnp.where(flag, total, 0.0), grad * unit, grad))
            ]
        for n in range(3):
            k.cs[n : n + 1, :] += jnp.sum(sums1[n], axis=0, keepdims=True)
        f_copy(i).start()

    tiny = []

    row = lax.broadcasted_iota(jnp.int32, (16, 1), 0)

    def tiny_core():
        raw = jnp.concatenate(
            [col_sum(k.gu[:, pl.ds(m * LOCAL, LOCAL)].astype(f32)) for m in (0, 2)], axis=1
        )
        k.ty[0] = jnp.where(row == 8, raw, k.cs[...])
        tiny.append(k.copy(SEM_TINY, k.ty.at[0], k.tc, k.core_peer))
        tiny[0].start()

    def tiny_x():
        tiny[0].wait()
        k.cs[...] = k.ty[0] + k.tc[...]
        tiny.append(k.copy(SEM_TINY + 1, k.cs, k.tx, k.x_peer))
        tiny[1].start()

    def tiny_z():
        tiny[1].wait()
        k.ty[1] = k.cs[...] + k.tx[...]
        for n in range(1, 4):
            tiny.append(k.copy(SEM_TINY + 1 + n, k.ty.at[1], k.tz.at[n], k.z_peer(n)))
            tiny[-1].start()
        k.tz[0] = k.ty[1]

    def tiny_y():
        for handle in tiny[2:]:
            handle.wait()
        total = None
        for zz in range(4):
            term = k.tz[lax.rem(k.z - zz + 4, 4)]
            total = term if total is None else total + term
        k.tt[...] = total
        tiny.append(k.copy(SEM_TINY + 5, k.tt, k.ty_r, k.y_peer))
        tiny[-1].start()

    def tiny_end():
        tiny[-1].wait()
        k.tiny_o[...] = k.tt[...] + jnp.where(row == 8, 0.0, k.ty_r[...])

    def frames_end(i):
        f_copy(i).wait()
        rows = pl.ds(*BLOCKS[i])
        k.mix[rows, :] = (k.mix[rows, :].astype(f32) + k.f_recv[rows, :].astype(f32)).astype(bf16)
        f_out(i).start()

    feed(0)
    up_grad(0)
    sums.u0.core()
    feed(1)
    sums.u0.x()
    up_grad(1)
    sums.u1.core()
    feed(2)
    sums.u1.x()
    feed(3)
    sums.u0.spread()
    norm2_back(0)
    up_grad(2)
    sums.u2.core()
    sums.u1.spread()
    norm2_back(1)
    sums.u0.gather()
    sums.u2.x()
    up_grad(3)
    sums.u3.core()
    norm2_back(2)
    sums.u1.gather()
    sums.u3.x()
    norm2_back(3)
    out_grad()
    sums.u2.spread()
    sums.u0.x_back()
    prepare()
    k.cs[...] = jnp.zeros_like(k.cs)
    sums.u3.spread()
    sums.u1.x_back()
    sums.u0.core_back()
    backward_half(0, 0)
    og_pair()
    sums.u2.gather()
    backward_half(0, 1)
    small()
    backward_half(1, 0)
    sums.u3.gather()
    sums.s.x()
    sums.u1.core_back()
    backward_half(1, 1)
    backward_end(0, 256, 0, ROWS)
    qkv_grad(0, 0, 256)
    sums.q00.core()
    sums.s.spread()
    qkv_grad(1, 0, 256)
    sums.q10.core()
    qkv_grad(2, 0, 256)
    sums.q20.core()
    sums.u2.x_back()
    backward_half(2, 0)
    sums.q10.x()
    backward_half(2, 1)
    sums.q00.x()
    backward_end(2, 128, 0, ROWS)
    qkv_grad(0, 2, 128)
    sums.q02.core()
    sums.q20.x()
    qkv_grad(1, 2, 128)
    sums.q12.core()
    sums.s.gather()
    sums.u2.core_back()
    qkv_grad(2, 2, 128)
    sums.q22.core()
    backward_step(0, 3)
    sums.q10.spread()
    sums.s.x_back()
    sums.q02.x()
    backward_end(3, 128, *BLOCKS[0])
    frames_part(0)
    sums.q22.x()
    sums.q00.spread()
    sums.q12.x()
    backward_step(1, 3)
    og_cross()
    sums.q10.gather()
    sums.q20.spread()
    backward_end(3, 128, *BLOCKS[1])
    frames_part(1)
    sums.s.core_back()
    backward_step(2, 3)
    sums.q00.gather()
    backward_end(3, 128, *BLOCKS[2])
    frames_part(2)
    sums.q22.spread()
    sums.q10.x_back()
    backward_step(3, 3)
    sums.q12.spread()
    backward_end(3, 128, *BLOCKS[3])
    qkv_grad(0, 3, 128)
    sums.q03.core()
    qkv_grad(1, 3, 128)
    sums.q13.core()
    sums.q02.spread()
    qkv_grad(2, 3, 128)
    sums.q23.core()
    sums.u3.x_back()
    frames_part(3)
    tiny_core()
    sums.q20.gather()
    frames_end(0)
    sums.o.spread()
    sums.q00.x_back()
    sums.q10.core_back()
    tiny_x()
    sums.q03.x()
    sums.q02.gather()
    sums.q13.x()
    sums.q12.gather()
    sums.q23.x()
    tiny_z()
    sums.q22.gather()
    sums.u3.core_back()
    sums.q20.x_back()
    frames_end(1)
    sums.q00.core_back()
    sums.o.gather()
    tiny_y()
    sums.q02.x_back()
    sums.q03.spread()
    sums.q12.x_back()
    sums.q22.x_back()
    sums.q13.spread()
    tiny_end()
    sums.q23.spread()
    sums.q20.core_back()
    sums.q12.core_back()
    sums.o.x_back()
    frames_end(2)
    sums.q22.core_back()
    sums.q03.gather()
    sums.q13.gather()
    sums.q23.gather()
    sums.q03.x_back()
    frames_end(3)
    sums.q13.x_back()
    sums.o.core_back()
    sums.q23.x_back()
    sums.q03.core_back()
    sums.q13.core_back()
    sums.q02.core_back()
    sums.q23.core_back()
    for name in PARTS:
        vars(sums)[name].end()
    for i in range(4):
        f_out(i).wait()


def local_fused(
    frames,
    lengths,
    span_starts,
    mask_embedding,
    norm1_gain,
    norm1_bias,
    qkv_weight,
    qv_bias,
    out_weight,
    out_bias,
    norm2_gain,
    norm2_bias,
    up_weight,
    up_bias,
    down_weight,
    down_bias,
    head_weight,
    head_bias,
    logit_grad,
):
    inputs = dict(
        frames=frames,
        lengths=lengths,
        starts=span_starts,
        mask_embedding=mask_embedding,
        norm1_gain=norm1_gain,
        norm1_bias=norm1_bias,
        out_bias=out_bias,
        norm2_gain=norm2_gain,
        norm2_bias=norm2_bias,
        down_bias=down_bias,
        qv_bias=qv_bias,
        up_bias=up_bias,
        qkv_w=jnp.transpose(qkv_weight, (1, 0, 2)),
        out_w=out_weight,
        up_w=up_weight,
        down_w=down_weight,
        head_w=head_weight.T,
        head_b=head_bias,
        logit_grad=logit_grad.T,
    )
    outs = pl.pallas_call(
        fused,
        out_shape=[jax.ShapeDtypeStruct(o[0], o[1]) for o in OUTPUTS.values()],
        in_specs=[pl.BlockSpec(memory_space=m or pl.ANY) for m in INPUTS.values()],
        out_specs=[pl.BlockSpec(memory_space=o[2] or pl.ANY) for o in OUTPUTS.values()],
        scratch_shapes=[MEM(*item) for item in SCRATCH.values()]
        + [MEM(shape, bf16) for shape in landing_shapes()]
        + [pltpu.SemaphoreType.DMA((SEM_COUNT,)), pltpu.SemaphoreType.DMA((SEM_COUNT,))],
        compiler_params=pltpu.CompilerParams(
            collective_id=0, has_side_effects=True, vmem_limit_bytes=63 * 2**20
        ),
    )(*[inputs[name] for name in INPUTS])
    logits, frames_grad, up_o, out_o, qkv_o, small_o, tiny = outs
    wide = widen(frames_grad, up_o, out_o, qkv_o, small_o, tiny, head_weight.T)
    frames_grad, up_grad, out_grad, qkv_grad, down_grad, head_grad, qv_grad = wide[:7]
    up_bias_grad, down_bias_grad, head_bias_grad = wide[7:10]
    mask_grad, gain1_grad, bias1_grad, gain2_grad, bias2_grad, out_bias_grad = wide[10:]
    return (
        logits.T,
        frames_grad,
        mask_grad,
        gain1_grad,
        bias1_grad,
        jnp.transpose(qkv_grad.reshape(3, WIDTH, LOCAL), (1, 0, 2)),
        qv_grad,
        out_grad,
        out_bias_grad,
        gain2_grad,
        bias2_grad,
        up_grad,
        up_bias_grad,
        down_grad,
        down_bias_grad,
        head_grad.T,
        head_bias_grad,
    )


STEPS = 8


def widen_kernel(fg, uo, oo, qo, so, ti, hw, fg_w, u_w, o_w, q_w, d_w, hg, qv, ub, db, hb, *vectors):
    step = pl.program_id(0)
    fg_w[...] = fg[...].astype(f32)
    u_w[...] = uo[...].astype(f32)
    o_w[...] = oo[...].astype(f32)
    q_w[...] = qo[...].astype(f32)
    for j in range(4):

        @pl.when(step // 2 == j)
        def _(j=j):
            for n in range(2):

                @pl.when(lax.rem(step, 2) == n)
                def _(n=n):
                    d_w[...] = dot_tn(
                        so[j * 32 : j * 32 + 32, n * 256 : (n + 1) * 256], hw[...]
                    )

    @pl.when(step == 0)
    def _():
        for j in range(2):
            cols = slice(j * 512, (j + 1) * 512)
            hg[:, cols] = so[128 + j * 32 : 160 + j * 32, :].astype(f32)
            qv[j : j + 1, :] = ti[8:9, cols]
        tail = so[224:240, :].astype(f32)
        for j in range(4):
            ub[pl.ds(j * 512, 512)] = tail[j : j + 1, :].reshape(512)
        hb[...] = tail[4:5, 0:CHARS].reshape(CHARS)
        grads = tail[4:5, 0:CHARS].reshape(CHARS, 1)
        db[...] = jnp.sum(hw[...].astype(f32) * grads, axis=0, keepdims=True).reshape(WIDTH)
        for number in range(3):
            vectors[number][...] = ti[number : number + 1, :].reshape(WIDTH)
        for number in range(3):
            for j in range(2):
                block = so[192 + j * 16 : 208 + j * 16, :].astype(f32)
                vectors[3 + number][pl.ds(j * 512, 512)] = block[3 + number : 4 + number, :].reshape(512)


def widen(frames_grad, up_o, out_o, qkv_o, small_o, tiny, head_t):
    def strip(array):
        return pl.BlockSpec((array.shape[0] // STEPS, array.shape[1]), lambda i: (i, 0))

    def whole(*shape):
        return pl.BlockSpec(shape, lambda i: (0,) * len(shape))

    def shaped(*shape):
        return jax.ShapeDtypeStruct(shape, f32)

    large = (frames_grad, up_o, out_o, qkv_o)
    down = shaped(FFL, WIDTH)
    rest = [shaped(CHARS, WIDTH), shaped(2, LOCAL), shaped(FFL), shaped(WIDTH), shaped(CHARS)]
    rest += [shaped(WIDTH)] * 6
    return pl.pallas_call(
        widen_kernel,
        grid=(STEPS,),
        out_shape=[shaped(*a.shape) for a in large] + [down] + rest,
        in_specs=[strip(a) for a in large]
        + [whole(*small_o.shape), whole(*tiny.shape), whole(*head_t.shape)],
        out_specs=[strip(a) for a in large] + [strip(down)] + [whole(*r.shape) for r in rest],
        compiler_params=pltpu.CompilerParams(vmem_limit_bytes=60 * 2**20),
    )(*large, small_o, tiny, head_t)


def solution(mesh):
    placed = (
        P("dp", None),
        P("dp"),
        P("dp", None),
        P(),
        P(),
        P(),
        P(None, None, "tensor"),
        P(None, "tensor"),
        P("tensor", None),
        P(),
        P(),
        P(),
        P(None, "tensor"),
        P("tensor"),
        P("tensor", None),
        P(),
        P(),
        P(),
        P("dp", None),
    )
    fits = mesh.shape["dp"] == 16 and mesh.shape["tensor"] == 2
    return jax.shard_map(
        local_fused if fits else local,
        mesh=mesh,
        in_specs=placed,
        out_specs=(
            P("dp", None),
            P("dp", None),
            P(),
            P(),
            P(),
            P(None, None, "tensor"),
            P(None, "tensor"),
            P("tensor", None),
            P(),
            P(),
            P(),
            P(None, "tensor"),
            P("tensor"),
            P("tensor", None),
            P(),
            P(),
            P(),
        ),
        check_vma=False,
    )
```

```python
from functools import partial
from types import SimpleNamespace

import jax
import jax.numpy as jnp
from jax import lax
from jax.experimental import pallas as pl
from jax.experimental.pallas import tpu as pltpu
from jax.sharding import PartitionSpec as P

HEAD_DIM = 64
MASK_SPAN = 10


EPS = 1e-05
NEG = -1e30


def norm_stats(row_block, gain, shift):
    center = row_block - jnp.mean(row_block, axis=-1, keepdims=True)
    spread = jnp.mean(center * center, axis=-1, keepdims=True)
    inverse = lax.rsqrt(spread + EPS)
    unit_rows = center * inverse
    return (unit_rows * gain + shift, unit_rows, inverse)


def norm_back(grad_rows, unit_rows, inverse, gain):
    grad_unit = grad_rows * gain
    first_mean = jnp.mean(grad_unit, axis=-1, keepdims=True)
    second_mean = jnp.mean(grad_unit * unit_rows, axis=-1, keepdims=True)
    return inverse * (grad_unit - first_mean - unit_rows * second_mean)


def masked_scores(queries, key_rows, key_valid):
    factor = HEAD_DIM ** (-0.5)
    scores = (
        jnp.einsum("qhd,khd->hqk", queries, key_rows, preferred_element_type=jnp.float32) * factor
    )
    return jnp.where(key_valid[None, None, :], scores, NEG)


def attend_forward(packed):
    queries, key_rows, values, key_valid = packed
    scores = masked_scores(queries, key_rows, key_valid)
    row_peak = jnp.max(scores, axis=-1, keepdims=True)
    exp_scores = jnp.exp(scores - row_peak)
    row_total = jnp.sum(exp_scores, axis=-1, keepdims=True)
    prob_rows = (exp_scores / row_total).astype(jnp.bfloat16)
    mixture = jnp.einsum("hqk,khd->qhd", prob_rows, values, preferred_element_type=jnp.float32)
    return (mixture, row_peak + jnp.log(row_total))


def attend_backward(packed):
    queries, key_rows, values, key_valid, log_total, grad_mixture = packed
    factor = HEAD_DIM ** (-0.5)
    scores = masked_scores(queries, key_rows, key_valid)
    prob_rows = jnp.exp(scores - log_total)
    grad_values = jnp.einsum(
        "hqk,qhd->khd",
        prob_rows.astype(jnp.bfloat16),
        grad_mixture,
        preferred_element_type=jnp.float32,
    )
    grad_probs = jnp.einsum(
        "qhd,khd->hqk", grad_mixture, values, preferred_element_type=jnp.float32
    )
    row_dot = jnp.sum(prob_rows * grad_probs, axis=-1, keepdims=True)
    grad_scores = (prob_rows * (grad_probs - row_dot)).astype(jnp.bfloat16)
    grad_queries = (
        jnp.einsum("hqk,khd->qhd", grad_scores, key_rows, preferred_element_type=jnp.float32)
        * factor
    )
    grad_keys = (
        jnp.einsum("hqk,qhd->khd", grad_scores, queries, preferred_element_type=jnp.float32)
        * factor
    )
    return (grad_queries, grad_keys, grad_values)


def local(
    frames,
    lengths,
    span_starts,
    mask_embedding,
    norm1_gain,
    norm1_bias,
    qkv_weight,
    qv_bias,
    out_weight,
    out_bias,
    norm2_gain,
    norm2_bias,
    up_weight,
    up_bias,
    down_weight,
    down_bias,
    head_weight,
    head_bias,
    logit_grad,
):
    utterances_here, span_count = span_starts.shape
    row_count, model_width = frames.shape
    frame_count = row_count // utterances_here
    local_width = qkv_weight.shape[2]
    heads_here = local_width // HEAD_DIM
    f32, bf16 = jnp.float32, jnp.bfloat16
    first_share = lax.axis_index("tensor") == 0

    def mm(spec, left, right):
        return jnp.einsum(spec, left, right, preferred_element_type=f32)

    def split(wide):
        high = wide.astype(bf16)
        return jnp.concatenate([high, (wide - high.astype(f32)).astype(bf16)], axis=-1)

    places = jnp.arange(frame_count, dtype=jnp.int32)
    covered = (places[None, None, :] >= span_starts[:, :, None]) & (
        places[None, None, :] < span_starts[:, :, None] + MASK_SPAN
    )
    masked = jnp.any(covered, axis=1).reshape(row_count, 1)
    key_valid = places[None, :] < lengths[:, None]
    gain_one = norm1_gain.astype(f32)
    gain_two = norm2_gain.astype(f32)
    filled = jnp.where(masked, mask_embedding.astype(f32)[None, :], frames.astype(f32))
    first_norm, first_unit, first_inverse = norm_stats(filled, gain_one, norm1_bias.astype(f32))
    first_low = first_norm.astype(bf16)
    weight_flat = qkv_weight.reshape(model_width, 3 * local_width)
    bias_full = jnp.stack(
        [qv_bias[0].astype(f32), jnp.zeros((local_width,), f32), qv_bias[1].astype(f32)]
    ).reshape(3 * local_width)
    projected = (mm("rd,dc->rc", first_low, weight_flat) + bias_full).astype(bf16)
    triple = projected.reshape(utterances_here, frame_count, 3, heads_here, HEAD_DIM)
    queries = triple[:, :, 0]
    key_rows = triple[:, :, 1]
    values = triple[:, :, 2]
    mixture, log_total = lax.map(attend_forward, (queries, key_rows, values, key_valid))
    mixture_low = mixture.astype(bf16).reshape(row_count, local_width)
    mixture_all = lax.all_gather(mixture_low, "tensor", axis=1, tiled=True)
    out_all = lax.all_gather(out_weight, "tensor", axis=0, tiled=True)
    hidden = filled + mm("rl,ld->rd", mixture_all, out_all) + out_bias.astype(f32)
    second_norm, second_unit, second_inverse = norm_stats(hidden, gain_two, norm2_bias.astype(f32))
    second_low = second_norm.astype(bf16)
    up_rows = mm("rd,df->rf", second_low, up_weight) + up_bias.astype(f32)
    activ, gelu_pull = jax.vjp(partial(jax.nn.gelu, approximate=False), up_rows)
    activ_low = activ.astype(bf16)
    down_head = split(mm("fd,dv->fv", down_weight, head_weight))
    characters = head_weight.shape[1]
    own_logits = mm("rf,fv->rv", activ_low, down_head)
    own_logits = own_logits[:, :characters] + own_logits[:, characters:]
    hidden_down = (hidden + down_bias.astype(f32)).astype(bf16)
    logits = (
        lax.psum(own_logits, "tensor")
        + mm("rd,dv->rv", hidden_down, head_weight)
        + head_bias.astype(f32)
    )
    twice = jnp.concatenate([logit_grad, logit_grad], axis=1)
    grad_activ = mm("rv,fv->rf", twice, down_head)
    grad_up = gelu_pull(grad_activ)[0].astype(bf16)
    activ_head = mm("rf,rv->fv", activ_low, logit_grad)
    hidden_head = mm("rd,rv->dv", hidden_down, logit_grad)
    head_bias_grad = jnp.sum(logit_grad.astype(f32), axis=0)
    up_grad = mm("rd,rf->df", second_low, grad_up)
    up_bias_grad = jnp.sum(grad_up.astype(f32), axis=0)
    grad_second = mm("rf,df->rd", grad_up, up_weight)
    norm2_gain_grad = jnp.sum(grad_second * second_unit, axis=0)
    norm2_bias_grad = jnp.sum(grad_second, axis=0)
    grad_output = mm("rv,dv->rd", logit_grad, head_weight)
    grad_hidden = norm_back(grad_second, second_unit, second_inverse, gain_two) + jnp.where(
        first_share, grad_output, 0.0
    )
    grad_attn = grad_hidden.astype(bf16)
    out_bias_grad = jnp.sum(grad_hidden, axis=0)
    grad_mixture = lax.psum_scatter(
        mm("rd,ld->rl", grad_attn, out_all).astype(bf16), "tensor", scatter_dimension=1, tiled=True
    )
    out_grad = lax.psum_scatter(
        mm("rl,rd->ld", mixture_all, grad_attn).astype(bf16),
        "tensor",
        scatter_dimension=0,
        tiled=True,
    )
    grad_mixture = grad_mixture.reshape(utterances_here, frame_count, heads_here, HEAD_DIM)
    grad_queries, grad_keys, grad_values = lax.map(
        attend_backward, (queries, key_rows, values, key_valid, log_total, grad_mixture)
    )
    grad_triple = (
        jnp.stack([grad_queries, grad_keys, grad_values], axis=2)
        .astype(bf16)
        .reshape(row_count, 3 * local_width)
    )
    qkv_grad = mm("rd,rc->dc", first_low, grad_triple).reshape(model_width, 3, local_width)
    column_sums = jnp.sum(grad_triple.astype(f32), axis=0).reshape(3, local_width)
    qv_bias_grad = jnp.stack([column_sums[0], column_sums[2]])
    grad_first = mm("rc,dc->rd", grad_triple, weight_flat)
    norm1_gain_grad = jnp.sum(grad_first * first_unit, axis=0)
    norm1_bias_grad = jnp.sum(grad_first, axis=0)
    grad_filled = grad_hidden + norm_back(grad_first, first_unit, first_inverse, gain_one)
    mask_grad = jnp.sum(jnp.where(masked, grad_filled, 0.0), axis=0)
    frames_grad = jnp.where(masked, 0.0, grad_filled).astype(bf16)
    frames_grad = lax.all_gather(
        lax.psum_scatter(frames_grad, "tensor", scatter_dimension=0, tiled=True),
        "tensor",
        axis=0,
        tiled=True,
    ).astype(f32)
    up_grad = lax.psum(up_grad.astype(bf16), "dp").astype(f32)
    out_grad = lax.psum(out_grad, "dp").astype(f32)
    qkv_grad = lax.psum(qkv_grad.astype(bf16), "dp").astype(f32)
    activ_head, up_bias_grad, qv_bias_grad, head_bias_grad, hidden_head = lax.psum(
        (activ_head, up_bias_grad, qv_bias_grad, head_bias_grad, hidden_head), "dp"
    )
    activ_split = split(activ_head)
    head_twice = jnp.concatenate([head_weight, head_weight], axis=1)
    down_grad = mm("fv,dv->fd", activ_split, head_twice)
    down_head_grad = mm("fd,fv->dv", down_weight, activ_split)
    down_head_grad = down_head_grad[:, :characters] + down_head_grad[:, characters:]
    down_bias_grad = jnp.dot(
        head_weight.astype(f32), head_bias_grad, precision=lax.Precision.HIGHEST
    )
    mask_grad, norm1_gain_grad, norm1_bias_grad, norm2_gain_grad, norm2_bias_grad, out_bias_grad = (
        lax.psum(
            (
                mask_grad,
                norm1_gain_grad,
                norm1_bias_grad,
                norm2_gain_grad,
                norm2_bias_grad,
                out_bias_grad,
            ),
            ("dp", "tensor"),
        )
    )
    head_grad = hidden_head + lax.psum(down_head_grad, "tensor")
    return (
        logits,
        frames_grad,
        mask_grad,
        norm1_gain_grad,
        norm1_bias_grad,
        qkv_grad,
        qv_bias_grad,
        out_grad,
        out_bias_grad,
        norm2_gain_grad,
        norm2_bias_grad,
        up_grad,
        up_bias_grad,
        down_grad,
        down_bias_grad,
        head_grad,
        head_bias_grad,
    )


f32, bf16 = jnp.float32, jnp.bfloat16
WIDTH = 1024
LOCAL = 512
FFL = 2048
ROWS = 896
CHARS = 32
CHUNK = 224
PIECE = 32
FEED = 448


def dot(left, right):
    return lax.dot_general(left, right, (((1,), (0,)), ((), ())), preferred_element_type=f32)


def dot_nt(left, right):
    return lax.dot_general(left, right, (((1,), (1,)), ((), ())), preferred_element_type=f32)


def dot_tn(left, right):
    return lax.dot_general(left, right, (((0,), (0,)), ((), ())), preferred_element_type=f32)


def aligned(start, size):
    return pl.ds(pl.multiple_of(start, size), size)


def fold_rows(block):
    rows, width = block.shape
    return jnp.sum(block.reshape(rows // 8, 8, width), axis=0)


def col_sum(block):
    return jnp.sum(fold_rows(block), axis=0, keepdims=True)


def gelu_parts(block):
    bell = jnp.exp(block * block * -0.5)
    cdf = 0.5 + 0.5 * lax.erf(block * (0.5**0.5))
    return block * cdf, cdf + block * bell * 0.3989422804014327


MEM = pltpu.VMEM
INPUTS = dict(
    frames=None,
    lengths=MEM,
    starts=MEM,
    mask_embedding=MEM,
    norm1_gain=MEM,
    norm1_bias=MEM,
    out_bias=MEM,
    norm2_gain=MEM,
    norm2_bias=MEM,
    down_bias=MEM,
    qv_bias=MEM,
    up_bias=MEM,
    qkv_w=None,
    out_w=None,
    up_w=None,
    down_w=None,
    head_w=MEM,
    head_b=MEM,
    logit_grad=MEM,
)
OUTPUTS = dict(
    logits=((CHARS, ROWS), f32, MEM),
    frames_grad=((ROWS, WIDTH), bf16, None),
    up_o=((WIDTH, FFL), bf16, None),
    out_o=((LOCAL, WIDTH), bf16, None),
    qkv_o=((3 * WIDTH, LOCAL), bf16, None),
    small_o=((256, LOCAL), bf16, None),
    tiny_o=((16, WIDTH), f32, MEM),
)
SCRATCH = dict(
    vec=((16, WIDTH), f32),
    x=((ROWS, WIDTH), bf16),
    wqkv=((3, WIDTH, LOCAL), bf16),
    first=((ROWS, WIDTH), bf16),
    first_t=((WIDTH, ROWS), bf16),
    qkv=((3, ROWS, LOCAL), bf16),
    mix=((ROWS, WIDTH), bf16),
    ow=((WIDTH, WIDTH), bf16),
    upw=((4 * WIDTH, LOCAL), bf16),
    big=((2 * WIDTH, WIDTH), bf16),
    lse=((128, ROWS), f32),
    dh=((FFL, 128), bf16),
    hw2=((WIDTH, 128), bf16),
    hw1=((WIDTH, 128), bf16),
    gd=((ROWS, 128), bf16),
    lp=((ROWS, 128), f32),
    lpt=((CHARS, ROWS), f32),
    lpr=((CHARS, ROWS), f32),
    second=((ROWS, WIDTH), bf16),
    work=((256, WIDTH), f32),
    unit=((ROWS, WIDTH), bf16),
    gu=((ROWS, FFL), bf16),
    pb=((ROWS, WIDTH), bf16),
    pm_own=((ROWS, LOCAL), bf16),
    pm_recv=((ROWS, LOCAL), bf16),
    nt=((CHARS, FFL), f32),
    hh=((CHARS, WIDTH), f32),
    ub=((8, FFL), f32),
    cs=((16, WIDTH), f32),
    gqt=((256, ROWS), f32),
    gk=((ROWS, 256), f32),
    gv=((ROWS, 256), f32),
    turn=((WIDTH, ROWS), bf16),
    og=((WIDTH, WIDTH), bf16),
    og_rc=((2, 256, WIDTH), bf16),
    og_ry=((256, WIDTH), bf16),
    sy=((48, WIDTH), f32),
    sy_r=((48, WIDTH), f32),
    sm=((256, LOCAL), bf16),
    f_recv=((ROWS, WIDTH), bf16),
    ty=((2, 16, WIDTH), f32),
    tc=((16, WIDTH), f32),
    tt=((16, WIDTH), f32),
    ty_r=((16, WIDTH), f32),
    tx=((16, WIDTH), f32),
    tz=((4, 16, WIDTH), f32),
)
PARTS = dict(
    u0=(1024, 512),
    u1=(1024, 512),
    u2=(1024, 512),
    u3=(1024, 512),
    o=(512, 1024),
    s=(256, 512),
    q00=(1024, 256),
    q10=(1024, 256),
    q20=(1024, 256),
    q02=(1024, 128),
    q12=(1024, 128),
    q22=(1024, 128),
    q03=(1024, 128),
    q13=(1024, 128),
    q23=(1024, 128),
)


def places(k):
    found = dict(
        o=(k.og, k.t * LOCAL, 0, k.out_o, 0, 0),
        s=(k.sm, 0, 0, k.small_o, 0, 0),
        q00=(k.upw, 0, 0, k.qkv_o, 0, 0),
        q10=(k.upw, 1024, 0, k.qkv_o, 1024, 0),
        q20=(k.upw, 2048, 0, k.qkv_o, 2048, 0),
        q02=(k.upw, 0, 256, k.qkv_o, 0, 256),
        q12=(k.upw, 1024, 256, k.qkv_o, 1024, 256),
        q22=(k.upw, 2048, 256, k.qkv_o, 2048, 256),
        q03=(k.upw, 0, 384, k.qkv_o, 0, 384),
        q13=(k.upw, 1024, 384, k.qkv_o, 1024, 384),
        q23=(k.upw, 2048, 384, k.qkv_o, 2048, 384),
        u0=(k.big, 0, 0, k.up_o, 0, 0),
        u1=(k.big, 0, 512, k.up_o, 0, 512),
        u2=(k.big, 1024, 0, k.up_o, 0, 1024),
        u3=(k.big, 1024, 512, k.up_o, 0, 1536),
    )
    return found


class Sum:
    def __init__(self, k, shape, place, landing, base):
        self.k = k
        self.rows, self.width = rows, _ = shape
        self.src, self.row0, self.col0, self.out, self.orow0, self.ocol0 = place
        self.rx, self.rz, self.rc = landing
        self.base = base
        self.half, self.quarter, self.piece = rows // 2, rows // 4, rows // 16
        self.b1 = k.c * self.half
        self.b2 = self.b1 + k.x_ * self.quarter
        self.b3 = self.b2 + k.z * self.piece

    def at(self, start, size):
        return self.src.at[aligned(self.row0 + start, size), pl.ds(self.col0, self.width)]

    def out_at(self, start, size):
        return self.out.at[aligned(self.orow0 + start, size), pl.ds(self.ocol0, self.width)]

    def add(self, start, size, others):
        step = min(size, 64 if size % 64 == 0 else 96 if size % 96 == 0 else 32)

        def body(i, carry):
            rows = aligned(self.row0 + start + i * step, step)
            cols = pl.ds(self.col0, self.width)
            total = self.src[rows, cols].astype(f32)
            for other in others:
                total += other[aligned(i * step, step), :].astype(f32)
            self.src[rows, cols] = total.astype(bf16)
            return carry

        lax.fori_loop(0, size // step, body, 0)

    def core(self):
        k = self.k
        self.h_core = k.copy(self.base, self.at((1 - k.c) * self.half, self.half), self.rc, k.core_peer)
        self.h_core.start()

    def x(self):
        k = self.k
        if self.rc is not None:
            self.h_core.wait()
            self.add(self.b1, self.half, [self.rc])
        self.h_x = k.copy(
            self.base + 1,
            self.at(self.b1 + (1 - k.x_) * self.quarter, self.quarter),
            self.rx,
            k.x_peer,
        )
        self.h_x.start()

    def spread(self):
        k = self.k
        self.h_x.wait()
        self.add(self.b2, self.quarter, [self.rx])
        self.h_z = []
        for s in range(1, 4):
            there = lax.rem(k.z + s, 4)
            handle = k.copy(
                self.base + 1 + s,
                self.at(self.b2 + there * self.piece, self.piece),
                self.rz.at[s - 1],
                k.z_peer(s),
            )
            handle.start()
            self.h_z.append(handle)

    def gather(self):
        k = self.k
        for handle in self.h_z:
            handle.wait()
        self.add(self.b3, self.piece, [self.rz.at[s] for s in range(3)])
        mine = self.out_at(self.b3, self.piece)
        self.h_own = pltpu.make_async_copy(self.at(self.b3, self.piece), mine, k.sem.at[self.base + 10])
        self.h_own.start()
        self.h_zg = []
        for s in range(1, 4):
            handle = k.copy(self.base + 4 + s, self.at(self.b3, self.piece), mine, k.z_peer(s))
            handle.start()
            self.h_zg.append(handle)

    def x_back(self):
        k = self.k
        self.h_own.wait()
        for handle in self.h_zg:
            handle.wait()
        block = self.out_at(self.b2, self.quarter)
        self.h_xg = k.copy(self.base + 8, block, block, k.x_peer)
        self.h_xg.start()

    def core_back(self):
        k = self.k
        self.h_xg.wait()
        block = self.out_at(self.b1, self.half)
        self.h_cg = k.copy(self.base + 9, block, block, k.core_peer)
        self.h_cg.start()

    def end(self):
        self.h_cg.wait()


SEM_LOCAL, SEM_OW, SEM_MIX, SEM_PM, SEM_OG, SEM_F, SEM_TINY, SEM_SUM = 0, 16, 32, 36, 40, 48, 52, 60
SEM_COUNT = SEM_SUM + 11 * len(PARTS)


def landing_shapes():
    shapes = []
    for rows, width in PARTS.values():
        shapes += [(rows // 4, width), (3, rows // 16, width), (rows // 2, width)]
    return shapes


def fused(*refs):
    names = list(INPUTS) + list(OUTPUTS) + list(SCRATCH)
    k = SimpleNamespace(**dict(zip(names, refs)))
    landing = refs[len(names) : -2]
    k.sem, k.rsem = refs[-2:]
    place = lax.axis_index("dp")
    k.t = lax.axis_index("tensor")
    k.z, k.x_, k.c = place // 4, lax.rem(place // 2, 2), lax.rem(place, 2)
    k.core_peer = {"dp": place + 1 - 2 * k.c}
    k.x_peer = {"dp": place + 2 - 4 * k.x_}
    k.y_peer = {"tensor": 1 - k.t}
    k.z_peer = lambda s: {"dp": lax.rem(k.z + s, 4) * 4 + k.x_ * 2 + k.c}

    def copy(number, src, dst, device):
        return pltpu.make_async_remote_copy(
            src_ref=src,
            dst_ref=dst,
            send_sem=k.sem.at[number],
            recv_sem=k.rsem.at[number],
            device_id=device,
            device_id_type=pl.DeviceIdType.MESH,
        )

    k.copy = copy
    mine = aligned(k.t * LOCAL, LOCAL)
    other = aligned((1 - k.t) * LOCAL, LOCAL)

    def load(number, src, dst):
        handle = pltpu.make_async_copy(src, dst, k.sem.at[SEM_LOCAL + number])
        handle.start()
        return handle

    load_x = load(0, k.frames, k.x)
    load_wqkv = load(1, k.qkv_w, k.wqkv)
    load_ow = load(2, k.out_w, k.ow.at[mine, :])
    load_big = load(3, k.down_w, k.big)
    load_upw = [
        load(4 + j, k.up_w.at[:, pl.ds(j * 512, 512)], k.upw.at[pl.ds(j * 1024, 1024), :])
        for j in range(4)
    ]
    barrier = pltpu.get_barrier_semaphore()
    peers = [k.core_peer, k.x_peer, k.y_peer, k.z_peer(1), k.z_peer(2), k.z_peer(3)]
    for peer in peers:
        pl.semaphore_signal(barrier, inc=1, device_id=peer, device_id_type=pl.DeviceIdType.MESH)

    for number, ref in enumerate(
        (
            k.mask_embedding,
            k.norm1_gain,
            k.norm1_bias,
            k.out_bias,
            k.norm2_gain,
            k.norm2_bias,
            k.down_bias,
        )
    ):
        k.vec[number : number + 1, :] = ref[...].astype(f32).reshape(1, WIDTH)
    k.vec[7:9, 0:LOCAL] = k.qv_bias[...].astype(f32)
    k.vec[9:11, :] = k.up_bias[...].astype(f32).reshape(2, WIDTH)
    emb, gain1, bias1, out_bias, gain2, bias2, down_bias = (
        k.vec[i : i + 1, :] for i in range(7)
    )
    lane = lax.broadcasted_iota(jnp.int32, (1, 128), 1)
    first_share = jnp.where(k.t == 0, 1.0, 0.0).astype(f32)

    def filled_rows(start, size):
        ids = lax.broadcasted_iota(jnp.int32, (size, k.starts.shape[1]), 0) + start
        begin = k.starts[...]
        inside = jnp.where((ids >= begin) & (ids < begin + MASK_SPAN), 1.0, 0.0)
        column = jnp.max(inside, axis=1, keepdims=True)
        flag = jnp.broadcast_to(column, (size, WIDTH)) > 0.5
        if isinstance(start, int):
            rows = pl.ds(start, size)
        else:
            rows = aligned(start, size)
        return jnp.where(flag, emb, k.x[rows, :].astype(f32)), flag

    load_x.wait()

    def ln1(i, carry):
        for n in range(0, CHUNK, PIECE):
            piece = aligned(i * CHUNK + n, PIECE)
            filled, _ = filled_rows(i * CHUNK + n, PIECE)
            norm, _, _ = norm_stats(filled, gain1, bias1)
            k.first[piece, :] = norm.astype(bf16)
        return carry

    lax.fori_loop(0, ROWS // CHUNK, ln1, 0)
    pl.semaphore_wait(barrier, len(peers))
    load_ow.wait()

    def ow_rows(tensor, x, z, size):
        return k.ow.at[aligned(tensor * LOCAL + k.c * 256 + x * 128 + z * 32, size), :]

    strip = ow_rows(k.t, k.x_, k.z, 32)
    ow_steps = [k.copy(SEM_OW, strip, strip, k.y_peer)]
    ow_steps[0].start()

    def ow_z():
        ow_steps[0].wait()
        strip = ow_rows(1 - k.t, k.x_, k.z, 32)
        for n in range(1, 4):
            ow_steps.append(k.copy(SEM_OW + n, strip, strip, k.z_peer(n)))
            ow_steps[-1].start()

    def ow_x():
        for handle in ow_steps[1:4]:
            handle.wait()
        strip = ow_rows(1 - k.t, k.x_, 0, 128)
        ow_steps.append(k.copy(SEM_OW + 4, strip, strip, k.x_peer))
        ow_steps[-1].start()

    def ow_core():
        ow_steps[4].wait()
        strip = ow_rows(1 - k.t, 0, 0, 256)
        ow_steps.append(k.copy(SEM_OW + 5, strip, strip, k.core_peer))
        ow_steps[-1].start()

    def key_bias_of(start, size):
        ids = lax.broadcasted_iota(jnp.int32, (size, 1), 0) + start
        return jnp.where(ids < k.lengths[...].reshape(1, 1), 0.0, NEG).astype(f32)

    key_bias = key_bias_of(0, ROWS)

    def mix_copy(p):
        strip = k.mix.at[:, aligned(k.t * LOCAL + p * 128, 128)]
        return k.copy(SEM_MIX + p, strip, strip, k.y_peer)

    sub = lax.broadcasted_iota(jnp.int32, (128, 1), 0)

    def forward_pair(p):
        cols = pl.ds(p * 128, 128)
        q_pair = k.qkv[0, :, cols].astype(f32) * HEAD_DIM ** (-0.5)
        k_pair = k.qkv[1, :, cols].astype(f32)
        v_turn = k.qkv[2, :, cols].astype(f32).T
        keys, values = [], []
        for h in range(2):
            half = (lane < 64) if h == 0 else (lane >= 64)
            rows = (sub < 64) if h == 0 else (sub >= 64)
            extra = 64 - 64 * h
            tail = jnp.where(lane == extra, key_bias, 0.0)
            keys.append(jnp.where(half, k_pair, tail).astype(bf16))
            tail = jnp.where(sub == extra, 1.0, 0.0)
            values.append(jnp.where(rows, v_turn, tail).astype(bf16))
        for start in range(0, ROWS, 128):
            span = slice(start, start + 128)
            made = []
            for h in range(2):
                half = (lane < 64) if h == 0 else (lane >= 64)
                extra = 64 - 64 * h
                tail = jnp.where(lane == extra, 1.0, 0.0)
                query = jnp.where(half, q_pair[span], tail).astype(bf16)
                scores = dot_nt(keys[h], query)
                peak = jnp.max(scores, axis=0, keepdims=True)
                weights = jnp.exp(scores - peak).astype(bf16)
                both = dot(values[h], weights)
                total = both[extra : extra + 1, :]
                made.append(both / total)
                k.lse[2 * p + h : 2 * p + h + 1, span] = peak + jnp.log(total)
            k.mix[span, aligned(k.t * LOCAL + p * 128, 128)] = (
                jnp.where(sub < 64, made[0], made[1]).T.astype(bf16)
            )
        mix_copy(p).start()

    load_wqkv.wait()
    k.lse[...] = jnp.zeros_like(k.lse)
    for half in range(2):
        cols = pl.ds(half * 256, 256)
        for m in range(3):
            bias = None if m == 1 else k.vec[7 + m // 2 : 8 + m // 2, cols]

            def project(i, carry, m=m, bias=bias, cols=cols):
                rows = aligned(i * 448, 448)
                value = dot(k.first[rows, :], k.wqkv[m, :, cols])
                k.qkv[m, rows, cols] = (value if bias is None else value + bias).astype(bf16)
                return carry

            lax.fori_loop(0, ROWS // 448, project, 0)
        if half == 0:
            ow_z()
        forward_pair(2 * half)
        if half == 1:
            ow_x()
        forward_pair(2 * half + 1)
        if half == 1:
            ow_core()

    def turn_rows(src, dst):
        def body(i, carry):
            cols = aligned(i * 128, 128)
            dst[cols, :] = src[:, cols].T
            return carry

        lax.fori_loop(0, WIDTH // 128, body, 0)

    turn_rows(k.first, k.first_t)
    pick = lax.broadcasted_iota(jnp.int32, (CHARS, 128), 0)
    spot = lax.broadcasted_iota(jnp.int32, (CHARS, 128), 1)
    once = jnp.where(pick == spot, 1.0, 0.0).astype(bf16)
    twice = jnp.where((pick == spot) | (pick + CHARS == spot), 1.0, 0.0).astype(bf16)
    k.hw1[...] = dot_tn(k.head_w[...], once).astype(bf16)
    k.hw2[...] = dot_tn(k.head_w[...], twice).astype(bf16)
    k.gd[...] = dot_tn(k.logit_grad[...], twice).astype(bf16)
    load_big.wait()

    def fold(i, carry):
        rows = aligned(i * 512, 512)
        value = dot(k.big[rows, :], k.hw2[...])
        high = value.astype(bf16).astype(f32)
        k.dh[rows, :] = jnp.where(lane < CHARS, high, value - high).astype(bf16)
        return carry

    lax.fori_loop(0, 4, fold, 0)
    k.nt[...] = jnp.zeros_like(k.nt)
    k.hh[...] = jnp.zeros_like(k.hh)
    k.ub[...] = jnp.zeros_like(k.ub)
    k.cs[...] = jnp.zeros_like(k.cs)
    ow_steps[5].wait()
    for handle in load_upw:
        handle.wait()

    def mix_wait(p, carry):
        mix_copy(p).wait()
        return carry

    lax.fori_loop(0, 4, mix_wait, 0)

    def pm_copy(i):
        rows = aligned(i * CHUNK, CHUNK)
        return k.copy(SEM_PM + i, k.first.at[rows, pl.ds(0, LOCAL)], k.pm_recv.at[rows, :], k.y_peer)

    def hidden_rows(i, carry):
        start = i * CHUNK
        rows = aligned(start, CHUNK)
        k.work[0:CHUNK, :] = dot(k.mix[rows, :], k.ow[...])
        for n in range(0, CHUNK, PIECE):
            piece = aligned(start + n, PIECE)
            filled, _ = filled_rows(start + n, PIECE)
            hidden = filled + k.work[n : n + PIECE, :] + out_bias
            second, unit, inverse = norm_stats(hidden, gain2, bias2)
            k.second[piece, :] = second.astype(bf16)
            k.unit[piece, :] = unit.astype(bf16)
            k.lp[piece, :] = jnp.broadcast_to(inverse, (PIECE, 128))
            k.pb[piece, :] = (hidden + down_bias).astype(bf16)
        down = k.pb[rows, :]
        head = dot(down, k.hw1[...]) * 0.5
        k.lp[rows, :] = jnp.where(lane == 64, k.lp[rows, :], head)
        k.hh[...] += dot_tn(k.gd[rows, :], down)[:CHARS] * first_share
        return carry

    lax.fori_loop(0, ROWS // CHUNK, hidden_rows, 0)
    turn_rows(k.second, k.turn)

    def feed(j):
        again = load(12 + j % 2, k.down_w.at[pl.ds(j * 512, 512), :], k.pb.at[pl.ds(0, 512), :])
        cols = pl.ds(j * 512, 512)
        bias = k.vec[9 + j // 2 : 10 + j // 2, pl.ds((j % 2) * 512, 512)]

        def body(i, carry):
            rows = aligned(i * FEED, FEED)
            grad = k.gd[rows, :]
            up = dot(k.second[rows, :], k.upw[pl.ds(j * 1024, 1024), :]) + bias
            act, slope = gelu_parts(up)
            act = act.astype(bf16)
            k.lp[rows, :] += dot(act, k.dh[cols, :])
            k.nt[:, cols] += dot_tn(grad, act)[:CHARS]
            grad_up = (dot_nt(grad, k.dh[cols, :]) * slope).astype(bf16)
            k.gu[rows, cols] = grad_up
            k.ub[0:1, cols] += col_sum(grad_up.astype(f32))
            return carry

        lax.fori_loop(0, ROWS // FEED, body, 0)
        again.wait()
        turned = k.nt[:, cols]
        high = turned.astype(bf16)
        rest = (turned - high.astype(f32)).astype(bf16)
        k.hh[...] += dot(high, k.pb[0:512, :]) + dot(rest, k.pb[0:512, :])

    def norm2_back(i):
        rows = pl.ds(i * CHUNK, CHUNK)
        k.work[0:CHUNK, :] = dot_nt(k.gu[rows, 0:512], k.upw[0:1024, :])
        for j in range(1, 4):
            k.work[0:CHUNK, :] += dot_nt(
                k.gu[rows, pl.ds(j * 512, 512)], k.upw[pl.ds(j * 1024, 1024), :]
            )
        sums2 = [jnp.zeros((8, WIDTH), f32)] * 3
        for n in range(0, CHUNK, PIECE):
            piece = pl.ds(i * CHUNK + n, PIECE)
            grad_second = k.work[n : n + PIECE, :]
            unit = k.unit[piece, :].astype(f32)
            spread = norm_back(grad_second, unit, k.lp[piece, 64:65], gain2)
            spread += dot_nt(k.gd[piece, :], k.hw1[...]) * first_share
            k.pb[piece, :] = spread.astype(bf16)
            sums2 = [
                total + fold_rows(term)
                for total, term in zip(sums2, (grad_second * unit, grad_second, spread))
            ]
        for n in range(3):
            k.cs[3 + n : 4 + n, :] += jnp.sum(sums2[n], axis=0, keepdims=True)
        low = k.pb[rows, :]
        k.first[rows, 0:LOCAL] = dot_nt(low, k.ow[other, :]).astype(bf16)
        pm_copy(i).start()
        k.pm_own[rows, :] = dot_nt(low, k.ow[mine, :]).astype(bf16)

    found = places(k)
    sums = SimpleNamespace(
        **{
            name: Sum(k, PARTS[name], found[name], landing[3 * n : 3 * n + 3], SEM_SUM + 11 * n)
            for n, name in enumerate(PARTS)
        }
    )
    sums.o.rc = None
    def up_grad(j):
        for n in range(2):
            k.big[pl.ds((j // 2) * 1024, 1024), pl.ds((j % 2) * 512 + n * 256, 256)] = dot(
                k.turn[...], k.gu[:, pl.ds(j * 512 + n * 256, 256)]
            ).astype(bf16)

    og_core, y_sums = [], []

    def out_grad():
        turn_rows(k.mix, k.turn)

        def out_block(i, carry):
            cols = aligned(i * 256, 256)
            k.og[:, cols] = dot(k.turn[...], k.pb[:, cols]).astype(bf16)
            return carry

        lax.fori_loop(0, 4, out_block, 0)
        for part in range(2):
            handle = k.copy(
                SEM_OG + part,
                k.og.at[aligned(part * LOCAL + (1 - k.c) * 256, 256), :],
                k.og_rc.at[part],
                k.core_peer,
            )
            handle.start()
            og_core.append(handle)
        k.sy[0:32, :] = k.hh[...]
        k.sy[32:48, :] = k.cs[...]
        sy_copy = k.copy(SEM_OG + 2, k.sy, k.sy_r, k.y_peer)
        sy_copy.start()
        y_sums.append(sy_copy)
        k.lpt[...] = (k.lp[...] + pltpu.roll(k.lp[...], 96, 1)).T[:CHARS]
        lp_copy = k.copy(SEM_OG + 3, k.lpt, k.lpr, k.y_peer)
        lp_copy.start()
        y_sums.append(lp_copy)

    def og_add(base, other):
        def body(i, carry):
            rows = aligned(base + i * 64, 64)
            total = k.og[rows, :].astype(f32) + other[aligned(i * 64, 64), :].astype(f32)
            k.og[rows, :] = total.astype(bf16)
            return carry

        lax.fori_loop(0, 4, body, 0)

    def og_pair():
        for part in range(2):
            og_core[part].wait()
            og_add(part * LOCAL + k.c * 256, k.og_rc.at[part])
        handle = k.copy(
            SEM_OG + 4,
            k.og.at[aligned((1 - k.t) * LOCAL + k.c * 256, 256), :],
            k.og_ry,
            k.y_peer,
        )
        handle.start()
        og_core.append(handle)

    def og_cross():
        og_core[2].wait()
        og_add(k.t * LOCAL + k.c * 256, k.og_ry)
        sums.o.x()

    def small():
        for handle in y_sums:
            handle.wait()
        k.logits[...] = k.lpt[...] + k.lpr[...] + k.head_b[...].astype(f32).reshape(CHARS, 1)
        k.sy[...] += k.sy_r[...]
        for j in range(4):
            k.sm[j * 32 : j * 32 + 32, :] = k.nt[:, j * 512 : (j + 1) * 512].astype(bf16)
        for j in range(2):
            cols = slice(j * 512, (j + 1) * 512)
            k.sm[128 + j * 32 : 160 + j * 32, :] = k.sy[0:32, cols].astype(bf16)
            k.sm[192 + j * 16 : 208 + j * 16, :] = k.sy[32:48, cols].astype(bf16)
        sub = lax.broadcasted_iota(jnp.int32, (16, 1), 0)
        total = jnp.sum(k.gd[...].astype(f32), axis=0, keepdims=True)
        total = jnp.concatenate([total, jnp.zeros((1, 384), f32)], axis=1)
        last_rows = jnp.where(sub == 4, total, 0.0)
        for j in range(4):
            last_rows = jnp.where(sub == j, k.ub[0:1, j * 512 : (j + 1) * 512], last_rows)
        k.sm[224:240, :] = last_rows.astype(bf16)
        k.sm[240:256, :] = jnp.zeros((16, LOCAL), bf16)
        sums.s.core()

    def pm_wait(i, carry):
        pm_copy(i).wait()
        return carry

    def heads_ready(n, carry):
        rows = aligned(n * 128, 128)
        shifts = -k.lse[:, rows].T
        for p in range(4):
            pair_ready(p, rows, shifts, key_bias_of(n * 128, 128))
        return carry

    def pair_ready(p, rows, shifts, bias):
        cols = pl.ds(p * 128, 128)
        mixed = k.mix[rows, aligned(k.t * LOCAL + p * 128, 128)].astype(f32)
        grad_pair = k.pm_own[rows, cols].astype(f32) + k.pm_recv[rows, cols].astype(f32)
        grad_pair = grad_pair.astype(bf16).astype(f32)
        q_pair = k.qkv[0, rows, cols].astype(f32) * HEAD_DIM ** (-0.5)
        k_pair = k.qkv[1, rows, cols].astype(f32)
        v_pair = k.qkv[2, rows, cols].astype(f32)
        for h in range(2):
            head = pl.ds((2 * p + h) * 128, 128)
            half = (lane < 64) if h == 0 else (lane >= 64)
            e = 64 - 64 * h
            shift = shifts[:, 2 * p + h : 2 * p + h + 1]
            one = shift.astype(bf16).astype(f32)
            two = (shift - one).astype(bf16).astype(f32)
            tail = jnp.where(lane == e + 3, shift - one - two, 0.0)
            tail = jnp.where(lane == e + 1, one, jnp.where(lane == e + 2, two, tail))
            tail = jnp.where(lane == e, 1.0, tail)
            k.second[rows, head] = jnp.where(half, q_pair, tail).astype(bf16)
            tail = jnp.where((lane > e) & (lane < e + 4), 1.0, 0.0)
            tail = jnp.where(lane == e, bias, tail)
            k.unit[rows, head] = jnp.where(half, k_pair, tail).astype(bf16)
            tail = jnp.where((lane >= e) & (lane < e + 2), 1.0, 0.0)
            k.ow[rows, head] = jnp.where(half, v_pair, tail).astype(bf16)
            total = -jnp.sum(jnp.where(half, grad_pair * mixed, 0.0), axis=1, keepdims=True)
            one = total.astype(bf16).astype(f32)
            tail = jnp.where(lane == e, one, jnp.where(lane == e + 1, total - one, 0.0))
            k.first[rows, head] = jnp.where(half, grad_pair, tail).astype(bf16)

    def prepare():
        lax.fori_loop(0, ROWS // CHUNK, pm_wait, 0)
        lax.fori_loop(0, ROWS // 128, heads_ready, 0)

    def backward_block(p, key_rows, query_rows, assign):
        made = []
        for h in range(2):
            head = pl.ds((2 * p + h) * 128, 128)
            query, key = k.second[query_rows, head], k.unit[key_rows, head]
            value, grad = k.ow[key_rows, head], k.first[query_rows, head]
            probs = jnp.exp(dot_nt(key, query))
            change = (probs * dot_nt(value, grad)).astype(bf16)
            made.append(
                (dot(change, query), dot(probs.astype(bf16), grad), dot_tn(key, change))
            )
        cols = pl.ds((p % 2) * 128, 128)
        for dst, at, n, low in (
            (k.gk, (key_rows, cols), 0, lane < 64),
            (k.gv, (key_rows, cols), 1, lane < 64),
            (k.gqt, (cols, query_rows), 2, sub < 64),
        ):
            total = jnp.where(low, made[0][n], made[1][n])
            if n == 2 and assign[1] or n < 2 and assign[0]:
                dst[at] = total
            else:
                dst[at] += total

    BLOCKS = ((0, 256), (256, 256), (512, 256), (768, 128))

    def backward_half(p, half):
        for start in range(half * 448, half * 448 + 448, 224):
            backward_block(p, pl.ds(start, 224), pl.ds(0, ROWS), (True, start == 0))

    def backward_step(i, p):
        start, size = BLOCKS[i]
        rows = pl.ds(start, size)
        rest = ROWS - start - size
        whole = ROWS - start
        first = 512 if whole > 512 else whole
        backward_block(p, pl.ds(start, first), rows, (i == 0, i == 0))
        if whole > first:
            backward_block(p, pl.ds(start + first, whole - first), rows, (i == 0, False))
        if rest:
            backward_block(p, rows, pl.ds(start + size, rest), (False, i == 0))

    def backward_end(pair, width, start, size):
        rows = pl.ds(start, size)
        own, at = pl.ds((pair % 2) * 128, width), pair * 128
        k.gu[rows, pl.ds(at, width)] = (k.gqt[own, rows] * HEAD_DIM ** (-0.5)).T.astype(bf16)
        k.gu[rows, pl.ds(LOCAL + at, width)] = k.gk[rows, own].astype(bf16)
        k.gu[rows, pl.ds(2 * LOCAL + at, width)] = k.gv[rows, own].astype(bf16)

    def qkv_grad(m, pair, width):
        k.upw[pl.ds(m * 1024, 1024), pl.ds(pair * 128, width)] = dot(
            k.first_t[...], k.gu[:, pl.ds(m * LOCAL + pair * 128, width)]
        ).astype(bf16)

    def f_copy(i):
        rows = pl.ds(*BLOCKS[i])
        return k.copy(SEM_F + i, k.mix.at[rows, :], k.f_recv.at[rows, :], k.y_peer)

    def f_out(i):
        rows = pl.ds(*BLOCKS[i])
        return pltpu.make_async_copy(
            k.mix.at[rows, :], k.frames_grad.at[rows, :], k.sem.at[SEM_LOCAL + 8 + i]
        )

    def frames_part(i):
        start, size = BLOCKS[i]
        rows = pl.ds(start, size)
        k.work[0:size, :] = dot_nt(k.gu[rows, 0:LOCAL], k.wqkv[0])
        for m in range(1, 3):
            k.work[0:size, :] += dot_nt(k.gu[rows, pl.ds(m * LOCAL, LOCAL)], k.wqkv[m])
        sums1 = [jnp.zeros((8, WIDTH), f32)] * 3
        for n in range(0, size, PIECE):
            piece = pl.ds(start + n, PIECE)
            filled, flag = filled_rows(start + n, PIECE)
            _, unit, inverse = norm_stats(filled, gain1, bias1)
            grad = k.work[n : n + PIECE, :]
            total = k.pb[piece, :].astype(f32) + norm_back(grad, unit, inverse, gain1)
            k.mix[piece, :] = jnp.where(flag, 0.0, total).astype(bf16)
            sums1 = [
                total_n + fold_rows(term)
                for total_n, term in zip(sums1, (jnp.where(flag, total, 0.0), grad * unit, grad))
            ]
        for n in range(3):
            k.cs[n : n + 1, :] += jnp.sum(sums1[n], axis=0, keepdims=True)
        f_copy(i).start()

    tiny = []

    row = lax.broadcasted_iota(jnp.int32, (16, 1), 0)

    def tiny_core():
        raw = jnp.concatenate(
            [col_sum(k.gu[:, pl.ds(m * LOCAL, LOCAL)].astype(f32)) for m in (0, 2)], axis=1
        )
        k.ty[0] = jnp.where(row == 8, raw, k.cs[...])
        tiny.append(k.copy(SEM_TINY, k.ty.at[0], k.tc, k.core_peer))
        tiny[0].start()

    def tiny_x():
        tiny[0].wait()
        k.cs[...] = k.ty[0] + k.tc[...]
        tiny.append(k.copy(SEM_TINY + 1, k.cs, k.tx, k.x_peer))
        tiny[1].start()

    def tiny_z():
        tiny[1].wait()
        k.ty[1] = k.cs[...] + k.tx[...]
        for n in range(1, 4):
            tiny.append(k.copy(SEM_TINY + 1 + n, k.ty.at[1], k.tz.at[n], k.z_peer(n)))
            tiny[-1].start()
        k.tz[0] = k.ty[1]

    def tiny_y():
        for handle in tiny[2:]:
            handle.wait()
        total = None
        for zz in range(4):
            term = k.tz[lax.rem(k.z - zz + 4, 4)]
            total = term if total is None else total + term
        k.tt[...] = total
        tiny.append(k.copy(SEM_TINY + 5, k.tt, k.ty_r, k.y_peer))
        tiny[-1].start()

    def tiny_end():
        tiny[-1].wait()
        k.tiny_o[...] = k.tt[...] + jnp.where(row == 8, 0.0, k.ty_r[...])

    def frames_end(i):
        f_copy(i).wait()
        rows = pl.ds(*BLOCKS[i])
        k.mix[rows, :] = (k.mix[rows, :].astype(f32) + k.f_recv[rows, :].astype(f32)).astype(bf16)
        f_out(i).start()

    feed(0)
    up_grad(0)
    sums.u0.core()
    feed(1)
    up_grad(1)
    sums.u1.core()
    sums.u0.x()
    feed(2)
    feed(3)
    sums.u1.x()
    norm2_back(0)
    sums.u0.spread()
    up_grad(2)
    sums.u2.core()
    norm2_back(1)
    up_grad(3)
    sums.u3.core()
    sums.u2.x()
    sums.u1.spread()
    norm2_back(2)
    sums.u0.gather()
    norm2_back(3)
    sums.u3.x()
    out_grad()
    sums.u1.gather()
    prepare()
    k.cs[...] = jnp.zeros_like(k.cs)
    sums.u2.spread()
    sums.u0.x_back()
    backward_half(0, 0)
    og_pair()
    sums.u3.spread()
    sums.u1.x_back()
    backward_half(0, 1)
    small()
    backward_half(1, 0)
    backward_half(1, 1)
    sums.u2.gather()
    sums.s.x()
    sums.u0.core_back()
    backward_end(0, 256, 0, ROWS)
    qkv_grad(0, 0, 256)
    sums.q00.core()
    qkv_grad(1, 0, 256)
    sums.q10.core()
    qkv_grad(2, 0, 256)
    sums.q20.core()
    backward_half(2, 0)
    sums.s.spread()
    sums.q00.x()
    sums.q10.x()
    sums.u3.gather()
    sums.u1.core_back()
    backward_half(2, 1)
    sums.q20.x()
    backward_end(2, 128, 0, ROWS)
    qkv_grad(0, 2, 128)
    sums.q02.core()
    qkv_grad(1, 2, 128)
    sums.q12.core()
    og_cross()
    qkv_grad(2, 2, 128)
    sums.q22.core()
    sums.s.gather()
    sums.q00.spread()
    backward_step(0, 3)
    sums.q10.spread()
    backward_end(3, 128, *BLOCKS[0])
    frames_part(0)
    sums.q02.x()
    backward_step(1, 3)
    sums.q20.spread()
    sums.q12.x()
    backward_end(3, 128, *BLOCKS[1])
    frames_part(1)
    sums.u2.x_back()
    backward_step(2, 3)
    sums.q00.gather()
    backward_end(3, 128, *BLOCKS[2])
    frames_part(2)
    sums.o.spread()
    backward_step(3, 3)
    backward_end(3, 128, *BLOCKS[3])
    qkv_grad(0, 3, 128)
    sums.q03.core()
    sums.u3.x_back()
    qkv_grad(1, 3, 128)
    sums.q13.core()
    qkv_grad(2, 3, 128)
    sums.q23.core()
    frames_part(3)
    tiny_core()
    sums.q20.gather()
    sums.q03.x()
    sums.q02.spread()
    sums.q13.x()
    tiny_x()
    sums.u2.core_back()
    sums.q12.spread()
    sums.q23.x()
    sums.q10.gather()
    sums.q00.x_back()
    tiny_z()
    sums.o.gather()
    sums.s.x_back()
    sums.u3.core_back()
    sums.q20.x_back()
    sums.q03.spread()
    tiny_y()
    sums.q22.x()
    sums.q13.spread()
    sums.q10.x_back()
    sums.q00.core_back()
    sums.q23.spread()
    sums.s.core_back()
    sums.q02.gather()
    sums.q12.gather()
    sums.q20.core_back()
    sums.o.x_back()
    sums.q22.spread()
    sums.q03.gather()
    sums.q13.gather()
    sums.q10.core_back()
    sums.q23.gather()
    sums.q02.x_back()
    sums.q12.x_back()
    sums.q22.gather()
    sums.o.core_back()
    sums.q03.x_back()
    sums.q02.core_back()
    sums.q13.x_back()
    sums.q12.core_back()
    sums.q23.x_back()
    sums.q22.x_back()
    sums.q03.core_back()
    sums.q13.core_back()
    sums.q23.core_back()
    sums.q22.core_back()
    frames_end(0)
    frames_end(1)
    frames_end(2)
    frames_end(3)
    tiny_end()
    for name in PARTS:
        vars(sums)[name].end()
    for i in range(4):
        f_out(i).wait()


def local_fused(
    frames,
    lengths,
    span_starts,
    mask_embedding,
    norm1_gain,
    norm1_bias,
    qkv_weight,
    qv_bias,
    out_weight,
    out_bias,
    norm2_gain,
    norm2_bias,
    up_weight,
    up_bias,
    down_weight,
    down_bias,
    head_weight,
    head_bias,
    logit_grad,
):
    inputs = dict(
        frames=frames,
        lengths=lengths,
        starts=span_starts,
        mask_embedding=mask_embedding,
        norm1_gain=norm1_gain,
        norm1_bias=norm1_bias,
        out_bias=out_bias,
        norm2_gain=norm2_gain,
        norm2_bias=norm2_bias,
        down_bias=down_bias,
        qv_bias=qv_bias,
        up_bias=up_bias,
        qkv_w=jnp.transpose(qkv_weight, (1, 0, 2)),
        out_w=out_weight,
        up_w=up_weight,
        down_w=down_weight,
        head_w=head_weight.T,
        head_b=head_bias,
        logit_grad=logit_grad.T,
    )
    outs = pl.pallas_call(
        fused,
        out_shape=[jax.ShapeDtypeStruct(o[0], o[1]) for o in OUTPUTS.values()],
        in_specs=[pl.BlockSpec(memory_space=m or pl.ANY) for m in INPUTS.values()],
        out_specs=[pl.BlockSpec(memory_space=o[2] or pl.ANY) for o in OUTPUTS.values()],
        scratch_shapes=[MEM(*item) for item in SCRATCH.values()]
        + [MEM(shape, bf16) for shape in landing_shapes()]
        + [pltpu.SemaphoreType.DMA((SEM_COUNT,)), pltpu.SemaphoreType.DMA((SEM_COUNT,))],
        compiler_params=pltpu.CompilerParams(
            collective_id=0, has_side_effects=True, vmem_limit_bytes=63 * 2**20
        ),
    )(*[inputs[name] for name in INPUTS])
    logits, frames_grad, up_o, out_o, qkv_o, small_o, tiny = outs
    wide = widen(frames_grad, up_o, out_o, qkv_o, small_o, tiny, head_weight.T)
    frames_grad, up_grad, out_grad, qkv_grad, down_grad, head_grad, qv_grad = wide[:7]
    up_bias_grad, down_bias_grad, head_bias_grad = wide[7:10]
    mask_grad, gain1_grad, bias1_grad, gain2_grad, bias2_grad, out_bias_grad = wide[10:]
    return (
        logits.T,
        frames_grad,
        mask_grad,
        gain1_grad,
        bias1_grad,
        jnp.transpose(qkv_grad.reshape(3, WIDTH, LOCAL), (1, 0, 2)),
        qv_grad,
        out_grad,
        out_bias_grad,
        gain2_grad,
        bias2_grad,
        up_grad,
        up_bias_grad,
        down_grad,
        down_bias_grad,
        head_grad.T,
        head_bias_grad,
    )


STEPS = 4


def widen_kernel(fg, uo, oo, qo, so, ti, hw, fg_w, u_w, o_w, q_w, d_w, hg, qv, ub, db, hb, *vectors):
    step = pl.program_id(0)
    fg_w[...] = fg[...].astype(f32)
    u_w[...] = uo[...].astype(f32)
    o_w[...] = oo[...].astype(f32)
    q_w[...] = qo[...].astype(f32)
    d_w[...] = dot_tn(so[aligned(step * 32, 32), :], hw[...])

    @pl.when(step == 0)
    def _():
        for j in range(2):
            cols = slice(j * 512, (j + 1) * 512)
            hg[:, cols] = so[128 + j * 32 : 160 + j * 32, :].astype(f32)
            qv[j : j + 1, :] = ti[8:9, cols]
        tail = so[224:240, :].astype(f32)
        for j in range(4):
            ub[pl.ds(j * 512, 512)] = tail[j : j + 1, :].reshape(512)
        hb[...] = tail[4:5, 0:CHARS].reshape(CHARS)
        grads = tail[4:5, 0:CHARS].reshape(CHARS, 1)
        db[...] = jnp.sum(hw[...].astype(f32) * grads, axis=0, keepdims=True).reshape(WIDTH)
        for number in range(3):
            vectors[number][...] = ti[number : number + 1, :].reshape(WIDTH)
        for number in range(3):
            for j in range(2):
                block = so[192 + j * 16 : 208 + j * 16, :].astype(f32)
                vectors[3 + number][pl.ds(j * 512, 512)] = block[3 + number : 4 + number, :].reshape(512)


def widen(frames_grad, up_o, out_o, qkv_o, small_o, tiny, head_t):
    def strip(array):
        return pl.BlockSpec((array.shape[0] // STEPS, array.shape[1]), lambda i: (i, 0))

    def whole(*shape):
        return pl.BlockSpec(shape, lambda i: (0,) * len(shape))

    def shaped(*shape):
        return jax.ShapeDtypeStruct(shape, f32)

    large = (frames_grad, up_o, out_o, qkv_o)
    down = shaped(FFL, WIDTH)
    rest = [shaped(CHARS, WIDTH), shaped(2, LOCAL), shaped(FFL), shaped(WIDTH), shaped(CHARS)]
    rest += [shaped(WIDTH)] * 6
    return pl.pallas_call(
        widen_kernel,
        grid=(STEPS,),
        out_shape=[shaped(*a.shape) for a in large] + [down] + rest,
        in_specs=[strip(a) for a in large]
        + [whole(*small_o.shape), whole(*tiny.shape), whole(*head_t.shape)],
        out_specs=[strip(a) for a in large] + [strip(down)] + [whole(*r.shape) for r in rest],
        compiler_params=pltpu.CompilerParams(vmem_limit_bytes=60 * 2**20),
    )(*large, small_o, tiny, head_t)


def solution(mesh):
    placed = (
        P("dp", None),
        P("dp"),
        P("dp", None),
        P(),
        P(),
        P(),
        P(None, None, "tensor"),
        P(None, "tensor"),
        P("tensor", None),
        P(),
        P(),
        P(),
        P(None, "tensor"),
        P("tensor"),
        P("tensor", None),
        P(),
        P(),
        P(),
        P("dp", None),
    )
    fits = mesh.shape["dp"] == 16 and mesh.shape["tensor"] == 2
    return jax.shard_map(
        local_fused if fits else local,
        mesh=mesh,
        in_specs=placed,
        out_specs=(
            P("dp", None),
            P("dp", None),
            P(),
            P(),
            P(),
            P(None, None, "tensor"),
            P(None, "tensor"),
            P("tensor", None),
            P(),
            P(),
            P(),
            P(None, "tensor"),
            P("tensor"),
            P("tensor", None),
            P(),
            P(),
            P(),
        ),
        check_vma=False,
    )
```

```python
from functools import partial
from types import SimpleNamespace

import jax
import jax.numpy as jnp
from jax import lax
from jax.experimental import pallas as pl
from jax.experimental.pallas import tpu as pltpu
from jax.sharding import PartitionSpec as P

HEAD_DIM = 64
MASK_SPAN = 10


EPS = 1e-05
NEG = -1e30


def norm_stats(row_block, gain, shift):
    center = row_block - jnp.mean(row_block, axis=-1, keepdims=True)
    spread = jnp.mean(center * center, axis=-1, keepdims=True)
    inverse = lax.rsqrt(spread + EPS)
    unit_rows = center * inverse
    return (unit_rows * gain + shift, unit_rows, inverse)


def norm_back(grad_rows, unit_rows, inverse, gain):
    grad_unit = grad_rows * gain
    first_mean = jnp.mean(grad_unit, axis=-1, keepdims=True)
    second_mean = jnp.mean(grad_unit * unit_rows, axis=-1, keepdims=True)
    return inverse * (grad_unit - first_mean - unit_rows * second_mean)


def masked_scores(queries, key_rows, key_valid):
    factor = HEAD_DIM ** (-0.5)
    scores = (
        jnp.einsum("qhd,khd->hqk", queries, key_rows, preferred_element_type=jnp.float32) * factor
    )
    return jnp.where(key_valid[None, None, :], scores, NEG)


def attend_forward(packed):
    queries, key_rows, values, key_valid = packed
    scores = masked_scores(queries, key_rows, key_valid)
    row_peak = jnp.max(scores, axis=-1, keepdims=True)
    exp_scores = jnp.exp(scores - row_peak)
    row_total = jnp.sum(exp_scores, axis=-1, keepdims=True)
    prob_rows = (exp_scores / row_total).astype(jnp.bfloat16)
    mixture = jnp.einsum("hqk,khd->qhd", prob_rows, values, preferred_element_type=jnp.float32)
    return (mixture, row_peak + jnp.log(row_total))


def attend_backward(packed):
    queries, key_rows, values, key_valid, log_total, grad_mixture = packed
    factor = HEAD_DIM ** (-0.5)
    scores = masked_scores(queries, key_rows, key_valid)
    prob_rows = jnp.exp(scores - log_total)
    grad_values = jnp.einsum(
        "hqk,qhd->khd",
        prob_rows.astype(jnp.bfloat16),
        grad_mixture,
        preferred_element_type=jnp.float32,
    )
    grad_probs = jnp.einsum(
        "qhd,khd->hqk", grad_mixture, values, preferred_element_type=jnp.float32
    )
    row_dot = jnp.sum(prob_rows * grad_probs, axis=-1, keepdims=True)
    grad_scores = (prob_rows * (grad_probs - row_dot)).astype(jnp.bfloat16)
    grad_queries = (
        jnp.einsum("hqk,khd->qhd", grad_scores, key_rows, preferred_element_type=jnp.float32)
        * factor
    )
    grad_keys = (
        jnp.einsum("hqk,qhd->khd", grad_scores, queries, preferred_element_type=jnp.float32)
        * factor
    )
    return (grad_queries, grad_keys, grad_values)


def local(
    frames,
    lengths,
    span_starts,
    mask_embedding,
    norm1_gain,
    norm1_bias,
    qkv_weight,
    qv_bias,
    out_weight,
    out_bias,
    norm2_gain,
    norm2_bias,
    up_weight,
    up_bias,
    down_weight,
    down_bias,
    head_weight,
    head_bias,
    logit_grad,
):
    utterances_here, span_count = span_starts.shape
    row_count, model_width = frames.shape
    frame_count = row_count // utterances_here
    local_width = qkv_weight.shape[2]
    heads_here = local_width // HEAD_DIM
    f32, bf16 = jnp.float32, jnp.bfloat16
    first_share = lax.axis_index("tensor") == 0

    def mm(spec, left, right):
        return jnp.einsum(spec, left, right, preferred_element_type=f32)

    def split(wide):
        high = wide.astype(bf16)
        return jnp.concatenate([high, (wide - high.astype(f32)).astype(bf16)], axis=-1)

    places = jnp.arange(frame_count, dtype=jnp.int32)
    covered = (places[None, None, :] >= span_starts[:, :, None]) & (
        places[None, None, :] < span_starts[:, :, None] + MASK_SPAN
    )
    masked = jnp.any(covered, axis=1).reshape(row_count, 1)
    key_valid = places[None, :] < lengths[:, None]
    gain_one = norm1_gain.astype(f32)
    gain_two = norm2_gain.astype(f32)
    filled = jnp.where(masked, mask_embedding.astype(f32)[None, :], frames.astype(f32))
    first_norm, first_unit, first_inverse = norm_stats(filled, gain_one, norm1_bias.astype(f32))
    first_low = first_norm.astype(bf16)
    weight_flat = qkv_weight.reshape(model_width, 3 * local_width)
    bias_full = jnp.stack(
        [qv_bias[0].astype(f32), jnp.zeros((local_width,), f32), qv_bias[1].astype(f32)]
    ).reshape(3 * local_width)
    projected = (mm("rd,dc->rc", first_low, weight_flat) + bias_full).astype(bf16)
    triple = projected.reshape(utterances_here, frame_count, 3, heads_here, HEAD_DIM)
    queries = triple[:, :, 0]
    key_rows = triple[:, :, 1]
    values = triple[:, :, 2]
    mixture, log_total = lax.map(attend_forward, (queries, key_rows, values, key_valid))
    mixture_low = mixture.astype(bf16).reshape(row_count, local_width)
    mixture_all = lax.all_gather(mixture_low, "tensor", axis=1, tiled=True)
    out_all = lax.all_gather(out_weight, "tensor", axis=0, tiled=True)
    hidden = filled + mm("rl,ld->rd", mixture_all, out_all) + out_bias.astype(f32)
    second_norm, second_unit, second_inverse = norm_stats(hidden, gain_two, norm2_bias.astype(f32))
    second_low = second_norm.astype(bf16)
    up_rows = mm("rd,df->rf", second_low, up_weight) + up_bias.astype(f32)
    activ, gelu_pull = jax.vjp(partial(jax.nn.gelu, approximate=False), up_rows)
    activ_low = activ.astype(bf16)
    down_head = split(mm("fd,dv->fv", down_weight, head_weight))
    characters = head_weight.shape[1]
    own_logits = mm("rf,fv->rv", activ_low, down_head)
    own_logits = own_logits[:, :characters] + own_logits[:, characters:]
    hidden_down = (hidden + down_bias.astype(f32)).astype(bf16)
    logits = (
        lax.psum(own_logits, "tensor")
        + mm("rd,dv->rv", hidden_down, head_weight)
        + head_bias.astype(f32)
    )
    twice = jnp.concatenate([logit_grad, logit_grad], axis=1)
    grad_activ = mm("rv,fv->rf", twice, down_head)
    grad_up = gelu_pull(grad_activ)[0].astype(bf16)
    activ_head = mm("rf,rv->fv", activ_low, logit_grad)
    hidden_head = mm("rd,rv->dv", hidden_down, logit_grad)
    head_bias_grad = jnp.sum(logit_grad.astype(f32), axis=0)
    up_grad = mm("rd,rf->df", second_low, grad_up)
    up_bias_grad = jnp.sum(grad_up.astype(f32), axis=0)
    grad_second = mm("rf,df->rd", grad_up, up_weight)
    norm2_gain_grad = jnp.sum(grad_second * second_unit, axis=0)
    norm2_bias_grad = jnp.sum(grad_second, axis=0)
    grad_output = mm("rv,dv->rd", logit_grad, head_weight)
    grad_hidden = norm_back(grad_second, second_unit, second_inverse, gain_two) + jnp.where(
        first_share, grad_output, 0.0
    )
    grad_attn = grad_hidden.astype(bf16)
    out_bias_grad = jnp.sum(grad_hidden, axis=0)
    grad_mixture = lax.psum_scatter(
        mm("rd,ld->rl", grad_attn, out_all).astype(bf16), "tensor", scatter_dimension=1, tiled=True
    )
    out_grad = lax.psum_scatter(
        mm("rl,rd->ld", mixture_all, grad_attn).astype(bf16),
        "tensor",
        scatter_dimension=0,
        tiled=True,
    )
    grad_mixture = grad_mixture.reshape(utterances_here, frame_count, heads_here, HEAD_DIM)
    grad_queries, grad_keys, grad_values = lax.map(
        attend_backward, (queries, key_rows, values, key_valid, log_total, grad_mixture)
    )
    grad_triple = (
        jnp.stack([grad_queries, grad_keys, grad_values], axis=2)
        .astype(bf16)
        .reshape(row_count, 3 * local_width)
    )
    qkv_grad = mm("rd,rc->dc", first_low, grad_triple).reshape(model_width, 3, local_width)
    column_sums = jnp.sum(grad_triple.astype(f32), axis=0).reshape(3, local_width)
    qv_bias_grad = jnp.stack([column_sums[0], column_sums[2]])
    grad_first = mm("rc,dc->rd", grad_triple, weight_flat)
    norm1_gain_grad = jnp.sum(grad_first * first_unit, axis=0)
    norm1_bias_grad = jnp.sum(grad_first, axis=0)
    grad_filled = grad_hidden + norm_back(grad_first, first_unit, first_inverse, gain_one)
    mask_grad = jnp.sum(jnp.where(masked, grad_filled, 0.0), axis=0)
    frames_grad = jnp.where(masked, 0.0, grad_filled).astype(bf16)
    frames_grad = lax.all_gather(
        lax.psum_scatter(frames_grad, "tensor", scatter_dimension=0, tiled=True),
        "tensor",
        axis=0,
        tiled=True,
    ).astype(f32)
    up_grad = lax.psum(up_grad.astype(bf16), "dp").astype(f32)
    out_grad = lax.psum(out_grad, "dp").astype(f32)
    qkv_grad = lax.psum(qkv_grad.astype(bf16), "dp").astype(f32)
    activ_head, up_bias_grad, qv_bias_grad, head_bias_grad, hidden_head = lax.psum(
        (activ_head, up_bias_grad, qv_bias_grad, head_bias_grad, hidden_head), "dp"
    )
    activ_split = split(activ_head)
    head_twice = jnp.concatenate([head_weight, head_weight], axis=1)
    down_grad = mm("fv,dv->fd", activ_split, head_twice)
    down_head_grad = mm("fd,fv->dv", down_weight, activ_split)
    down_head_grad = down_head_grad[:, :characters] + down_head_grad[:, characters:]
    down_bias_grad = jnp.dot(
        head_weight.astype(f32), head_bias_grad, precision=lax.Precision.HIGHEST
    )
    mask_grad, norm1_gain_grad, norm1_bias_grad, norm2_gain_grad, norm2_bias_grad, out_bias_grad = (
        lax.psum(
            (
                mask_grad,
                norm1_gain_grad,
                norm1_bias_grad,
                norm2_gain_grad,
                norm2_bias_grad,
                out_bias_grad,
            ),
            ("dp", "tensor"),
        )
    )
    head_grad = hidden_head + lax.psum(down_head_grad, "tensor")
    return (
        logits,
        frames_grad,
        mask_grad,
        norm1_gain_grad,
        norm1_bias_grad,
        qkv_grad,
        qv_bias_grad,
        out_grad,
        out_bias_grad,
        norm2_gain_grad,
        norm2_bias_grad,
        up_grad,
        up_bias_grad,
        down_grad,
        down_bias_grad,
        head_grad,
        head_bias_grad,
    )


f32, bf16 = jnp.float32, jnp.bfloat16
WIDTH = 1024
LOCAL = 512
FFL = 2048
ROWS = 896
CHARS = 32
CHUNK = 224
PIECE = 32
FEED = 448


def dot(left, right):
    return lax.dot_general(left, right, (((1,), (0,)), ((), ())), preferred_element_type=f32)


def dot_nt(left, right):
    return lax.dot_general(left, right, (((1,), (1,)), ((), ())), preferred_element_type=f32)


def dot_tn(left, right):
    return lax.dot_general(left, right, (((0,), (0,)), ((), ())), preferred_element_type=f32)


def aligned(start, size):
    return pl.ds(pl.multiple_of(start, size), size)


def fold_rows(block):
    rows, width = block.shape
    return jnp.sum(block.reshape(rows // 8, 8, width), axis=0)


def col_sum(block):
    return jnp.sum(fold_rows(block), axis=0, keepdims=True)


def gelu_parts(block):
    bell = jnp.exp(block * block * -0.5)
    cdf = 0.5 + 0.5 * lax.erf(block * (0.5**0.5))
    return block * cdf, cdf + block * bell * 0.3989422804014327


MEM = pltpu.VMEM
INPUTS = dict(
    frames=None,
    lengths=MEM,
    starts=MEM,
    mask_embedding=MEM,
    norm1_gain=MEM,
    norm1_bias=MEM,
    out_bias=MEM,
    norm2_gain=MEM,
    norm2_bias=MEM,
    down_bias=MEM,
    qv_bias=MEM,
    up_bias=MEM,
    qkv_w=None,
    out_w=None,
    up_w=None,
    down_w=None,
    head_w=MEM,
    head_b=MEM,
    logit_grad=MEM,
)
OUTPUTS = dict(
    logits=((CHARS, ROWS), f32, MEM),
    frames_grad=((ROWS, WIDTH), bf16, None),
    up_o=((WIDTH, FFL), bf16, None),
    out_o=((LOCAL, WIDTH), bf16, None),
    qkv_o=((3 * WIDTH, LOCAL), bf16, None),
    small_o=((256, LOCAL), bf16, None),
    tiny_o=((16, WIDTH), f32, MEM),
)
SCRATCH = dict(
    vec=((16, WIDTH), f32),
    x=((ROWS, WIDTH), bf16),
    wqkv=((3, WIDTH, LOCAL), bf16),
    first=((ROWS, WIDTH), bf16),
    first_t=((WIDTH, ROWS), bf16),
    qkv=((3, ROWS, LOCAL), bf16),
    mix=((ROWS, WIDTH), bf16),
    ow=((WIDTH, WIDTH), bf16),
    upw=((4 * WIDTH, LOCAL), bf16),
    big=((2 * WIDTH, WIDTH), bf16),
    lse=((128, ROWS), f32),
    dh=((FFL, 128), bf16),
    hw2=((WIDTH, 128), bf16),
    hw1=((WIDTH, 128), bf16),
    gd=((ROWS, 128), bf16),
    lp=((ROWS, 128), f32),
    lpt=((CHARS, ROWS), f32),
    lpr=((CHARS, ROWS), f32),
    second=((ROWS, WIDTH), bf16),
    work=((256, WIDTH), f32),
    unit=((ROWS, WIDTH), bf16),
    gu=((ROWS, FFL), bf16),
    pb=((ROWS, WIDTH), bf16),
    pm_own=((ROWS, LOCAL), bf16),
    pm_recv=((ROWS, LOCAL), bf16),
    nt=((CHARS, FFL), f32),
    hh=((CHARS, WIDTH), f32),
    ub=((8, FFL), f32),
    cs=((16, WIDTH), f32),
    gqt=((256, ROWS), f32),
    gk=((ROWS, 256), f32),
    gv=((ROWS, 256), f32),
    turn=((WIDTH, ROWS), bf16),
    og=((WIDTH, WIDTH), bf16),
    og_rc=((2, 256, WIDTH), bf16),
    og_ry=((256, WIDTH), bf16),
    sy=((48, WIDTH), f32),
    sy_r=((48, WIDTH), f32),
    sm=((256, LOCAL), bf16),
    f_recv=((ROWS, WIDTH), bf16),
    ty=((2, 16, WIDTH), f32),
    tc=((16, WIDTH), f32),
    tt=((16, WIDTH), f32),
    ty_r=((16, WIDTH), f32),
    tx=((16, WIDTH), f32),
    tz=((4, 16, WIDTH), f32),
)
PARTS = dict(
    u0=(1024, 512),
    u1=(1024, 512),
    u2=(1024, 512),
    u3=(1024, 512),
    o=(512, 1024),
    s=(256, 512),
    q00=(1024, 256),
    q10=(1024, 256),
    q20=(1024, 256),
    q02=(1024, 128),
    q12=(1024, 128),
    q22=(1024, 128),
    q03=(1024, 128),
    q13=(1024, 128),
    q23=(1024, 128),
)


def places(k):
    found = dict(
        o=(k.og, k.t * LOCAL, 0, k.out_o, 0, 0),
        s=(k.sm, 0, 0, k.small_o, 0, 0),
        q00=(k.upw, 0, 0, k.qkv_o, 0, 0),
        q10=(k.upw, 1024, 0, k.qkv_o, 1024, 0),
        q20=(k.upw, 2048, 0, k.qkv_o, 2048, 0),
        q02=(k.upw, 0, 256, k.qkv_o, 0, 256),
        q12=(k.upw, 1024, 256, k.qkv_o, 1024, 256),
        q22=(k.upw, 2048, 256, k.qkv_o, 2048, 256),
        q03=(k.upw, 0, 384, k.qkv_o, 0, 384),
        q13=(k.upw, 1024, 384, k.qkv_o, 1024, 384),
        q23=(k.upw, 2048, 384, k.qkv_o, 2048, 384),
        u0=(k.big, 0, 0, k.up_o, 0, 0),
        u1=(k.big, 0, 512, k.up_o, 0, 512),
        u2=(k.big, 1024, 0, k.up_o, 0, 1024),
        u3=(k.big, 1024, 512, k.up_o, 0, 1536),
    )
    return found


class Sum:
    def __init__(self, k, shape, place, landing, base):
        self.k = k
        self.rows, self.width = rows, _ = shape
        self.src, self.row0, self.col0, self.out, self.orow0, self.ocol0 = place
        self.rx, self.rz, self.rc = landing
        self.base = base
        self.half, self.quarter, self.piece = rows // 2, rows // 4, rows // 16
        self.b1 = k.c * self.half
        self.b2 = self.b1 + k.x_ * self.quarter
        self.b3 = self.b2 + k.z * self.piece

    def at(self, start, size):
        return self.src.at[aligned(self.row0 + start, size), pl.ds(self.col0, self.width)]

    def out_at(self, start, size):
        return self.out.at[aligned(self.orow0 + start, size), pl.ds(self.ocol0, self.width)]

    def add(self, start, size, others):
        step = min(size, 64 if size % 64 == 0 else 96 if size % 96 == 0 else 32)

        def body(i, carry):
            rows = aligned(self.row0 + start + i * step, step)
            cols = pl.ds(self.col0, self.width)
            total = self.src[rows, cols].astype(f32)
            for other in others:
                total += other[aligned(i * step, step), :].astype(f32)
            self.src[rows, cols] = total.astype(bf16)
            return carry

        lax.fori_loop(0, size // step, body, 0)

    def core(self):
        k = self.k
        self.h_core = k.copy(self.base, self.at((1 - k.c) * self.half, self.half), self.rc, k.core_peer)
        self.h_core.start()

    def x(self):
        k = self.k
        if self.rc is not None:
            self.h_core.wait()
            self.add(self.b1, self.half, [self.rc])
        self.h_x = k.copy(
            self.base + 1,
            self.at(self.b1 + (1 - k.x_) * self.quarter, self.quarter),
            self.rx,
            k.x_peer,
        )
        self.h_x.start()

    def spread(self):
        k = self.k
        self.h_x.wait()
        self.add(self.b2, self.quarter, [self.rx])
        self.h_z = []
        for s in range(1, 4):
            there = lax.rem(k.z + s, 4)
            handle = k.copy(
                self.base + 1 + s,
                self.at(self.b2 + there * self.piece, self.piece),
                self.rz.at[s - 1],
                k.z_peer(s),
            )
            handle.start()
            self.h_z.append(handle)

    def gather(self):
        k = self.k
        for handle in self.h_z:
            handle.wait()
        self.add(self.b3, self.piece, [self.rz.at[s] for s in range(3)])
        mine = self.out_at(self.b3, self.piece)
        self.h_own = pltpu.make_async_copy(self.at(self.b3, self.piece), mine, k.sem.at[self.base + 10])
        self.h_own.start()
        self.h_zg = []
        for s in range(1, 4):
            handle = k.copy(self.base + 4 + s, self.at(self.b3, self.piece), mine, k.z_peer(s))
            handle.start()
            self.h_zg.append(handle)

    def x_back(self):
        k = self.k
        self.h_own.wait()
        for handle in self.h_zg:
            handle.wait()
        block = self.out_at(self.b2, self.quarter)
        self.h_xg = k.copy(self.base + 8, block, block, k.x_peer)
        self.h_xg.start()

    def core_back(self):
        k = self.k
        self.h_xg.wait()
        block = self.out_at(self.b1, self.half)
        self.h_cg = k.copy(self.base + 9, block, block, k.core_peer)
        self.h_cg.start()

    def end(self):
        self.h_cg.wait()


SEM_LOCAL, SEM_OW, SEM_MIX, SEM_PM, SEM_OG, SEM_F, SEM_TINY, SEM_SUM = 0, 16, 32, 36, 40, 48, 52, 60
SEM_COUNT = SEM_SUM + 11 * len(PARTS)


def landing_shapes():
    shapes = []
    for rows, width in PARTS.values():
        shapes += [(rows // 4, width), (3, rows // 16, width), (rows // 2, width)]
    return shapes


def fused(*refs):
    names = list(INPUTS) + list(OUTPUTS) + list(SCRATCH)
    k = SimpleNamespace(**dict(zip(names, refs)))
    landing = refs[len(names) : -2]
    k.sem, k.rsem = refs[-2:]
    place = lax.axis_index("dp")
    k.t = lax.axis_index("tensor")
    k.z, k.x_, k.c = place // 4, lax.rem(place // 2, 2), lax.rem(place, 2)
    k.core_peer = {"dp": place + 1 - 2 * k.c}
    k.x_peer = {"dp": place + 2 - 4 * k.x_}
    k.y_peer = {"tensor": 1 - k.t}
    k.z_peer = lambda s: {"dp": lax.rem(k.z + s, 4) * 4 + k.x_ * 2 + k.c}

    def copy(number, src, dst, device):
        return pltpu.make_async_remote_copy(
            src_ref=src,
            dst_ref=dst,
            send_sem=k.sem.at[number],
            recv_sem=k.rsem.at[number],
            device_id=device,
            device_id_type=pl.DeviceIdType.MESH,
        )

    k.copy = copy
    mine = aligned(k.t * LOCAL, LOCAL)
    other = aligned((1 - k.t) * LOCAL, LOCAL)

    def load(number, src, dst):
        handle = pltpu.make_async_copy(src, dst, k.sem.at[SEM_LOCAL + number])
        handle.start()
        return handle

    load_x = load(0, k.frames, k.x)
    load_wqkv = load(1, k.qkv_w, k.wqkv)
    load_ow = load(2, k.out_w, k.ow.at[mine, :])
    load_big = load(3, k.down_w, k.big)
    load_upw = [
        load(4 + j, k.up_w.at[:, pl.ds(j * 512, 512)], k.upw.at[pl.ds(j * 1024, 1024), :])
        for j in range(4)
    ]
    barrier = pltpu.get_barrier_semaphore()
    peers = [k.core_peer, k.x_peer, k.y_peer, k.z_peer(1), k.z_peer(2), k.z_peer(3)]
    for peer in peers:
        pl.semaphore_signal(barrier, inc=1, device_id=peer, device_id_type=pl.DeviceIdType.MESH)

    for number, ref in enumerate(
        (
            k.mask_embedding,
            k.norm1_gain,
            k.norm1_bias,
            k.out_bias,
            k.norm2_gain,
            k.norm2_bias,
            k.down_bias,
        )
    ):
        k.vec[number : number + 1, :] = ref[...].astype(f32).reshape(1, WIDTH)
    k.vec[7:9, 0:LOCAL] = k.qv_bias[...].astype(f32)
    k.vec[9:11, :] = k.up_bias[...].astype(f32).reshape(2, WIDTH)
    emb, gain1, bias1, out_bias, gain2, bias2, down_bias = (
        k.vec[i : i + 1, :] for i in range(7)
    )
    lane = lax.broadcasted_iota(jnp.int32, (1, 128), 1)
    first_share = jnp.where(k.t == 0, 1.0, 0.0).astype(f32)

    def filled_rows(start, size):
        ids = lax.broadcasted_iota(jnp.int32, (size, k.starts.shape[1]), 0) + start
        begin = k.starts[...]
        inside = jnp.where((ids >= begin) & (ids < begin + MASK_SPAN), 1.0, 0.0)
        column = jnp.max(inside, axis=1, keepdims=True)
        flag = jnp.broadcast_to(column, (size, WIDTH)) > 0.5
        if isinstance(start, int):
            rows = pl.ds(start, size)
        else:
            rows = aligned(start, size)
        return jnp.where(flag, emb, k.x[rows, :].astype(f32)), flag

    load_x.wait()

    def ln1(i, carry):
        for n in range(0, CHUNK, PIECE):
            piece = aligned(i * CHUNK + n, PIECE)
            filled, _ = filled_rows(i * CHUNK + n, PIECE)
            norm, _, _ = norm_stats(filled, gain1, bias1)
            k.first[piece, :] = norm.astype(bf16)
        return carry

    lax.fori_loop(0, ROWS // CHUNK, ln1, 0)
    pl.semaphore_wait(barrier, len(peers))
    load_ow.wait()

    def ow_rows(tensor, x, z, size):
        return k.ow.at[aligned(tensor * LOCAL + k.c * 256 + x * 128 + z * 32, size), :]

    strip = ow_rows(k.t, k.x_, k.z, 32)
    ow_steps = [k.copy(SEM_OW, strip, strip, k.y_peer)]
    ow_steps[0].start()

    def ow_z():
        ow_steps[0].wait()
        strip = ow_rows(1 - k.t, k.x_, k.z, 32)
        for n in range(1, 4):
            ow_steps.append(k.copy(SEM_OW + n, strip, strip, k.z_peer(n)))
            ow_steps[-1].start()

    def ow_x():
        for handle in ow_steps[1:4]:
            handle.wait()
        strip = ow_rows(1 - k.t, k.x_, 0, 128)
        ow_steps.append(k.copy(SEM_OW + 4, strip, strip, k.x_peer))
        ow_steps[-1].start()

    def ow_core():
        ow_steps[4].wait()
        strip = ow_rows(1 - k.t, 0, 0, 256)
        ow_steps.append(k.copy(SEM_OW + 5, strip, strip, k.core_peer))
        ow_steps[-1].start()

    def key_bias_of(start, size):
        ids = lax.broadcasted_iota(jnp.int32, (size, 1), 0) + start
        return jnp.where(ids < k.lengths[...].reshape(1, 1), 0.0, NEG).astype(f32)

    key_bias = key_bias_of(0, ROWS)

    def mix_copy(p):
        strip = k.mix.at[:, aligned(k.t * LOCAL + p * 128, 128)]
        return k.copy(SEM_MIX + p, strip, strip, k.y_peer)

    sub = lax.broadcasted_iota(jnp.int32, (128, 1), 0)

    def forward_pair(p):
        cols = pl.ds(p * 128, 128)
        q_pair = k.qkv[0, :, cols].astype(f32) * HEAD_DIM ** (-0.5)
        k_pair = k.qkv[1, :, cols].astype(f32)
        v_turn = k.qkv[2, :, cols].astype(f32).T
        keys, values = [], []
        for h in range(2):
            half = (lane < 64) if h == 0 else (lane >= 64)
            rows = (sub < 64) if h == 0 else (sub >= 64)
            extra = 64 - 64 * h
            tail = jnp.where(lane == extra, key_bias, 0.0)
            keys.append(jnp.where(half, k_pair, tail).astype(bf16))
            tail = jnp.where(sub == extra, 1.0, 0.0)
            values.append(jnp.where(rows, v_turn, tail).astype(bf16))
        for start in range(0, ROWS, 128):
            span = slice(start, start + 128)
            made = []
            for h in range(2):
                half = (lane < 64) if h == 0 else (lane >= 64)
                extra = 64 - 64 * h
                tail = jnp.where(lane == extra, 1.0, 0.0)
                query = jnp.where(half, q_pair[span], tail).astype(bf16)
                scores = dot_nt(keys[h], query)
                peak = jnp.max(scores, axis=0, keepdims=True)
                weights = jnp.exp(scores - peak).astype(bf16)
                both = dot(values[h], weights)
                total = both[extra : extra + 1, :]
                made.append(both / total)
                k.lse[2 * p + h : 2 * p + h + 1, span] = peak + jnp.log(total)
            k.mix[span, aligned(k.t * LOCAL + p * 128, 128)] = (
                jnp.where(sub < 64, made[0], made[1]).T.astype(bf16)
            )
        mix_copy(p).start()

    load_wqkv.wait()
    k.lse[...] = jnp.zeros_like(k.lse)
    for half in range(2):
        cols = pl.ds(half * 256, 256)
        for m in range(3):
            bias = None if m == 1 else k.vec[7 + m // 2 : 8 + m // 2, cols]

            def project(i, carry, m=m, bias=bias, cols=cols):
                rows = aligned(i * 448, 448)
                value = dot(k.first[rows, :], k.wqkv[m, :, cols])
                k.qkv[m, rows, cols] = (value if bias is None else value + bias).astype(bf16)
                return carry

            lax.fori_loop(0, ROWS // 448, project, 0)
        if half == 0:
            ow_z()
        forward_pair(2 * half)
        if half == 1:
            ow_x()
        forward_pair(2 * half + 1)
        if half == 1:
            ow_core()

    def turn_rows(src, dst):
        def body(i, carry):
            cols = aligned(i * 128, 128)
            dst[cols, :] = src[:, cols].T
            return carry

        lax.fori_loop(0, WIDTH // 128, body, 0)

    turn_rows(k.first, k.first_t)
    pick = lax.broadcasted_iota(jnp.int32, (CHARS, 128), 0)
    spot = lax.broadcasted_iota(jnp.int32, (CHARS, 128), 1)
    once = jnp.where(pick == spot, 1.0, 0.0).astype(bf16)
    twice = jnp.where((pick == spot) | (pick + CHARS == spot), 1.0, 0.0).astype(bf16)
    k.hw1[...] = dot_tn(k.head_w[...], once).astype(bf16)
    k.hw2[...] = dot_tn(k.head_w[...], twice).astype(bf16)
    k.gd[...] = dot_tn(k.logit_grad[...], twice).astype(bf16)
    load_big.wait()

    def fold(i, carry):
        rows = aligned(i * 512, 512)
        value = dot(k.big[rows, :], k.hw2[...])
        high = value.astype(bf16).astype(f32)
        k.dh[rows, :] = jnp.where(lane < CHARS, high, value - high).astype(bf16)
        return carry

    lax.fori_loop(0, 4, fold, 0)
    k.nt[...] = jnp.zeros_like(k.nt)
    k.hh[...] = jnp.zeros_like(k.hh)
    k.ub[...] = jnp.zeros_like(k.ub)
    k.cs[...] = jnp.zeros_like(k.cs)
    ow_steps[5].wait()
    for handle in load_upw:
        handle.wait()

    def mix_wait(p, carry):
        mix_copy(p).wait()
        return carry

    lax.fori_loop(0, 4, mix_wait, 0)

    def pm_copy(i):
        rows = aligned(i * CHUNK, CHUNK)
        return k.copy(SEM_PM + i, k.first.at[rows, pl.ds(0, LOCAL)], k.pm_recv.at[rows, :], k.y_peer)

    def hidden_rows(i, carry):
        start = i * CHUNK
        rows = aligned(start, CHUNK)
        k.work[0:CHUNK, :] = dot(k.mix[rows, :], k.ow[...])
        for n in range(0, CHUNK, PIECE):
            piece = aligned(start + n, PIECE)
            filled, _ = filled_rows(start + n, PIECE)
            hidden = filled + k.work[n : n + PIECE, :] + out_bias
            second, unit, inverse = norm_stats(hidden, gain2, bias2)
            k.second[piece, :] = second.astype(bf16)
            k.unit[piece, :] = unit.astype(bf16)
            k.lp[piece, :] = jnp.broadcast_to(inverse, (PIECE, 128))
            k.pb[piece, :] = (hidden + down_bias).astype(bf16)
        down = k.pb[rows, :]
        head = dot(down, k.hw1[...]) * 0.5
        k.lp[rows, :] = jnp.where(lane == 64, k.lp[rows, :], head)
        k.hh[...] += dot_tn(k.gd[rows, :], down)[:CHARS] * first_share
        return carry

    lax.fori_loop(0, ROWS // CHUNK, hidden_rows, 0)
    turn_rows(k.second, k.turn)

    def feed(j):
        again = load(12 + j % 2, k.down_w.at[pl.ds(j * 512, 512), :], k.pb.at[pl.ds(0, 512), :])
        cols = pl.ds(j * 512, 512)
        bias = k.vec[9 + j // 2 : 10 + j // 2, pl.ds((j % 2) * 512, 512)]

        def body(i, carry):
            rows = aligned(i * FEED, FEED)
            grad = k.gd[rows, :]
            up = dot(k.second[rows, :], k.upw[pl.ds(j * 1024, 1024), :]) + bias
            act, slope = gelu_parts(up)
            act = act.astype(bf16)
            k.lp[rows, :] += dot(act, k.dh[cols, :])
            k.nt[:, cols] += dot_tn(grad, act)[:CHARS]
            grad_up = (dot_nt(grad, k.dh[cols, :]) * slope).astype(bf16)
            k.gu[rows, cols] = grad_up
            k.ub[0:1, cols] += col_sum(grad_up.astype(f32))
            return carry

        lax.fori_loop(0, ROWS // FEED, body, 0)
        again.wait()
        turned = k.nt[:, cols]
        high = turned.astype(bf16)
        rest = (turned - high.astype(f32)).astype(bf16)
        k.hh[...] += dot(high, k.pb[0:512, :]) + dot(rest, k.pb[0:512, :])

    def norm2_back(i):
        rows = pl.ds(i * CHUNK, CHUNK)
        k.work[0:CHUNK, :] = dot_nt(k.gu[rows, 0:512], k.upw[0:1024, :])
        for j in range(1, 4):
            k.work[0:CHUNK, :] += dot_nt(
                k.gu[rows, pl.ds(j * 512, 512)], k.upw[pl.ds(j * 1024, 1024), :]
            )
        sums2 = [jnp.zeros((8, WIDTH), f32)] * 3
        for n in range(0, CHUNK, PIECE):
            piece = pl.ds(i * CHUNK + n, PIECE)
            grad_second = k.work[n : n + PIECE, :]
            unit = k.unit[piece, :].astype(f32)
            spread = norm_back(grad_second, unit, k.lp[piece, 64:65], gain2)
            spread += dot_nt(k.gd[piece, :], k.hw1[...]) * first_share
            k.pb[piece, :] = spread.astype(bf16)
            sums2 = [
                total + fold_rows(term)
                for total, term in zip(sums2, (grad_second * unit, grad_second, spread))
            ]
        for n in range(3):
            k.cs[3 + n : 4 + n, :] += jnp.sum(sums2[n], axis=0, keepdims=True)
        low = k.pb[rows, :]
        k.first[rows, 0:LOCAL] = dot_nt(low, k.ow[other, :]).astype(bf16)
        pm_copy(i).start()
        k.pm_own[rows, :] = dot_nt(low, k.ow[mine, :]).astype(bf16)

    found = places(k)
    sums = SimpleNamespace(
        **{
            name: Sum(k, PARTS[name], found[name], landing[3 * n : 3 * n + 3], SEM_SUM + 11 * n)
            for n, name in enumerate(PARTS)
        }
    )
    sums.o.rc = None
    def up_grad(j):
        for n in range(2):
            k.big[pl.ds((j // 2) * 1024, 1024), pl.ds((j % 2) * 512 + n * 256, 256)] = dot(
                k.turn[...], k.gu[:, pl.ds(j * 512 + n * 256, 256)]
            ).astype(bf16)

    og_core, y_sums = [], []

    def out_grad():
        turn_rows(k.mix, k.turn)

        def out_block(i, carry):
            cols = aligned(i * 256, 256)
            k.og[:, cols] = dot(k.turn[...], k.pb[:, cols]).astype(bf16)
            return carry

        lax.fori_loop(0, 4, out_block, 0)
        for part in range(2):
            handle = k.copy(
                SEM_OG + part,
                k.og.at[aligned(part * LOCAL + (1 - k.c) * 256, 256), :],
                k.og_rc.at[part],
                k.core_peer,
            )
            handle.start()
            og_core.append(handle)
        k.sy[0:32, :] = k.hh[...]
        k.sy[32:48, :] = k.cs[...]
        sy_copy = k.copy(SEM_OG + 2, k.sy, k.sy_r, k.y_peer)
        sy_copy.start()
        y_sums.append(sy_copy)
        k.lpt[...] = (k.lp[...] + pltpu.roll(k.lp[...], 96, 1)).T[:CHARS]
        lp_copy = k.copy(SEM_OG + 3, k.lpt, k.lpr, k.y_peer)
        lp_copy.start()
        y_sums.append(lp_copy)

    def og_add(base, other):
        def body(i, carry):
            rows = aligned(base + i * 64, 64)
            total = k.og[rows, :].astype(f32) + other[aligned(i * 64, 64), :].astype(f32)
            k.og[rows, :] = total.astype(bf16)
            return carry

        lax.fori_loop(0, 4, body, 0)

    def og_pair():
        for part in range(2):
            og_core[part].wait()
            og_add(part * LOCAL + k.c * 256, k.og_rc.at[part])
        handle = k.copy(
            SEM_OG + 4,
            k.og.at[aligned((1 - k.t) * LOCAL + k.c * 256, 256), :],
            k.og_ry,
            k.y_peer,
        )
        handle.start()
        og_core.append(handle)

    def og_cross():
        og_core[2].wait()
        og_add(k.t * LOCAL + k.c * 256, k.og_ry)
        sums.o.x()

    def small():
        for handle in y_sums:
            handle.wait()
        k.logits[...] = k.lpt[...] + k.lpr[...] + k.head_b[...].astype(f32).reshape(CHARS, 1)
        k.sy[...] += k.sy_r[...]
        for j in range(4):
            k.sm[j * 32 : j * 32 + 32, :] = k.nt[:, j * 512 : (j + 1) * 512].astype(bf16)
        for j in range(2):
            cols = slice(j * 512, (j + 1) * 512)
            k.sm[128 + j * 32 : 160 + j * 32, :] = k.sy[0:32, cols].astype(bf16)
            k.sm[192 + j * 16 : 208 + j * 16, :] = k.sy[32:48, cols].astype(bf16)
        sub = lax.broadcasted_iota(jnp.int32, (16, 1), 0)
        total = jnp.sum(k.gd[...].astype(f32), axis=0, keepdims=True)
        total = jnp.concatenate([total, jnp.zeros((1, 384), f32)], axis=1)
        last_rows = jnp.where(sub == 4, total, 0.0)
        for j in range(4):
            last_rows = jnp.where(sub == j, k.ub[0:1, j * 512 : (j + 1) * 512], last_rows)
        k.sm[224:240, :] = last_rows.astype(bf16)
        k.sm[240:256, :] = jnp.zeros((16, LOCAL), bf16)
        sums.s.core()

    def pm_wait(i, carry):
        pm_copy(i).wait()
        return carry

    def heads_ready(n, carry):
        rows = aligned(n * 128, 128)
        shifts = -k.lse[:, rows].T
        for p in range(4):
            pair_ready(p, rows, shifts, key_bias_of(n * 128, 128))
        return carry

    def pair_ready(p, rows, shifts, bias):
        cols = pl.ds(p * 128, 128)
        mixed = k.mix[rows, aligned(k.t * LOCAL + p * 128, 128)].astype(f32)
        grad_pair = k.pm_own[rows, cols].astype(f32) + k.pm_recv[rows, cols].astype(f32)
        grad_pair = grad_pair.astype(bf16).astype(f32)
        q_pair = k.qkv[0, rows, cols].astype(f32) * HEAD_DIM ** (-0.5)
        k_pair = k.qkv[1, rows, cols].astype(f32)
        v_pair = k.qkv[2, rows, cols].astype(f32)
        for h in range(2):
            head = pl.ds((2 * p + h) * 128, 128)
            half = (lane < 64) if h == 0 else (lane >= 64)
            e = 64 - 64 * h
            shift = shifts[:, 2 * p + h : 2 * p + h + 1]
            one = shift.astype(bf16).astype(f32)
            two = (shift - one).astype(bf16).astype(f32)
            tail = jnp.where(lane == e + 3, shift - one - two, 0.0)
            tail = jnp.where(lane == e + 1, one, jnp.where(lane == e + 2, two, tail))
            tail = jnp.where(lane == e, 1.0, tail)
            k.second[rows, head] = jnp.where(half, q_pair, tail).astype(bf16)
            tail = jnp.where((lane > e) & (lane < e + 4), 1.0, 0.0)
            tail = jnp.where(lane == e, bias, tail)
            k.unit[rows, head] = jnp.where(half, k_pair, tail).astype(bf16)
            tail = jnp.where((lane >= e) & (lane < e + 2), 1.0, 0.0)
            k.ow[rows, head] = jnp.where(half, v_pair, tail).astype(bf16)
            total = -jnp.sum(jnp.where(half, grad_pair * mixed, 0.0), axis=1, keepdims=True)
            one = total.astype(bf16).astype(f32)
            tail = jnp.where(lane == e, one, jnp.where(lane == e + 1, total - one, 0.0))
            k.first[rows, head] = jnp.where(half, grad_pair, tail).astype(bf16)

    def prepare():
        lax.fori_loop(0, ROWS // CHUNK, pm_wait, 0)
        lax.fori_loop(0, ROWS // 128, heads_ready, 0)

    def backward_block(p, key_rows, query_rows, assign):
        made = []
        for h in range(2):
            head = pl.ds((2 * p + h) * 128, 128)
            query, key = k.second[query_rows, head], k.unit[key_rows, head]
            value, grad = k.ow[key_rows, head], k.first[query_rows, head]
            probs = jnp.exp(dot_nt(key, query))
            change = (probs * dot_nt(value, grad)).astype(bf16)
            made.append(
                (dot(change, query), dot(probs.astype(bf16), grad), dot_tn(key, change))
            )
        cols = pl.ds((p % 2) * 128, 128)
        for dst, at, n, low in (
            (k.gk, (key_rows, cols), 0, lane < 64),
            (k.gv, (key_rows, cols), 1, lane < 64),
            (k.gqt, (cols, query_rows), 2, sub < 64),
        ):
            total = jnp.where(low, made[0][n], made[1][n])
            if n == 2 and assign[1] or n < 2 and assign[0]:
                dst[at] = total
            else:
                dst[at] += total

    BLOCKS = ((0, 256), (256, 256), (512, 256), (768, 128))

    def backward_half(p, half):
        for start in range(half * 448, half * 448 + 448, 224):
            backward_block(p, pl.ds(start, 224), pl.ds(0, ROWS), (True, start == 0))

    def backward_step(i, p):
        start, size = BLOCKS[i]
        rows = pl.ds(start, size)
        rest = ROWS - start - size
        whole = ROWS - start
        first = 512 if whole > 512 else whole
        backward_block(p, pl.ds(start, first), rows, (i == 0, i == 0))
        if whole > first:
            backward_block(p, pl.ds(start + first, whole - first), rows, (i == 0, False))
        if rest:
            backward_block(p, rows, pl.ds(start + size, rest), (False, i == 0))

    def backward_end(pair, width, start, size):
        rows = pl.ds(start, size)
        own, at = pl.ds((pair % 2) * 128, width), pair * 128
        k.gu[rows, pl.ds(at, width)] = (k.gqt[own, rows] * HEAD_DIM ** (-0.5)).T.astype(bf16)
        k.gu[rows, pl.ds(LOCAL + at, width)] = k.gk[rows, own].astype(bf16)
        k.gu[rows, pl.ds(2 * LOCAL + at, width)] = k.gv[rows, own].astype(bf16)

    def qkv_grad(m, pair, width):
        k.upw[pl.ds(m * 1024, 1024), pl.ds(pair * 128, width)] = dot(
            k.first_t[...], k.gu[:, pl.ds(m * LOCAL + pair * 128, width)]
        ).astype(bf16)

    def f_copy(i):
        rows = pl.ds(*BLOCKS[i])
        return k.copy(SEM_F + i, k.mix.at[rows, :], k.f_recv.at[rows, :], k.y_peer)

    def f_out(i):
        rows = pl.ds(*BLOCKS[i])
        return pltpu.make_async_copy(
            k.mix.at[rows, :], k.frames_grad.at[rows, :], k.sem.at[SEM_LOCAL + 8 + i]
        )

    def frames_part(i):
        start, size = BLOCKS[i]
        rows = pl.ds(start, size)
        k.work[0:size, :] = dot_nt(k.gu[rows, 0:LOCAL], k.wqkv[0])
        for m in range(1, 3):
            k.work[0:size, :] += dot_nt(k.gu[rows, pl.ds(m * LOCAL, LOCAL)], k.wqkv[m])
        sums1 = [jnp.zeros((8, WIDTH), f32)] * 3
        for n in range(0, size, PIECE):
            piece = pl.ds(start + n, PIECE)
            filled, flag = filled_rows(start + n, PIECE)
            _, unit, inverse = norm_stats(filled, gain1, bias1)
            grad = k.work[n : n + PIECE, :]
            total = k.pb[piece, :].astype(f32) + norm_back(grad, unit, inverse, gain1)
            k.mix[piece, :] = jnp.where(flag, 0.0, total).astype(bf16)
            sums1 = [
                total_n + fold_rows(term)
                for total_n, term in zip(sums1, (jnp.where(flag, total, 0.0), grad * unit, grad))
            ]
        for n in range(3):
            k.cs[n : n + 1, :] += jnp.sum(sums1[n], axis=0, keepdims=True)
        f_copy(i).start()

    tiny = []

    row = lax.broadcasted_iota(jnp.int32, (16, 1), 0)

    def tiny_core():
        raw = jnp.concatenate(
            [col_sum(k.gu[:, pl.ds(m * LOCAL, LOCAL)].astype(f32)) for m in (0, 2)], axis=1
        )
        k.ty[0] = jnp.where(row == 8, raw, k.cs[...])
        tiny.append(k.copy(SEM_TINY, k.ty.at[0], k.tc, k.core_peer))
        tiny[0].start()

    def tiny_x():
        tiny[0].wait()
        k.cs[...] = k.ty[0] + k.tc[...]
        tiny.append(k.copy(SEM_TINY + 1, k.cs, k.tx, k.x_peer))
        tiny[1].start()

    def tiny_z():
        tiny[1].wait()
        k.ty[1] = k.cs[...] + k.tx[...]
        for n in range(1, 4):
            tiny.append(k.copy(SEM_TINY + 1 + n, k.ty.at[1], k.tz.at[n], k.z_peer(n)))
            tiny[-1].start()
        k.tz[0] = k.ty[1]

    def tiny_y():
        for handle in tiny[2:]:
            handle.wait()
        total = None
        for zz in range(4):
            term = k.tz[lax.rem(k.z - zz + 4, 4)]
            total = term if total is None else total + term
        k.tt[...] = total
        tiny.append(k.copy(SEM_TINY + 5, k.tt, k.ty_r, k.y_peer))
        tiny[-1].start()

    def tiny_end():
        tiny[-1].wait()
        k.tiny_o[...] = k.tt[...] + jnp.where(row == 8, 0.0, k.ty_r[...])

    def frames_end(i):
        f_copy(i).wait()
        rows = pl.ds(*BLOCKS[i])
        k.mix[rows, :] = (k.mix[rows, :].astype(f32) + k.f_recv[rows, :].astype(f32)).astype(bf16)
        f_out(i).start()

    feed(0)
    up_grad(0)
    sums.u0.core()
    feed(1)
    up_grad(1)
    sums.u1.core()
    sums.u0.x()
    feed(2)
    feed(3)
    sums.u1.x()
    norm2_back(0)
    sums.u0.spread()
    up_grad(2)
    sums.u2.core()
    norm2_back(1)
    up_grad(3)
    sums.u3.core()
    sums.u1.spread()
    sums.u2.x()
    norm2_back(2)
    sums.u0.gather()
    sums.u3.x()
    norm2_back(3)
    out_grad()
    sums.u1.gather()
    prepare()
    k.cs[...] = jnp.zeros_like(k.cs)
    sums.u2.spread()
    sums.u1.x_back()
    backward_half(0, 0)
    og_pair()
    sums.u3.spread()
    sums.u0.x_back()
    backward_half(0, 1)
    small()
    backward_half(1, 0)
    sums.u2.gather()
    sums.s.x()
    sums.u1.core_back()
    backward_half(1, 1)
    backward_end(0, 256, 0, ROWS)
    qkv_grad(0, 0, 256)
    sums.q00.core()
    qkv_grad(1, 0, 256)
    sums.q10.core()
    qkv_grad(2, 0, 256)
    sums.q20.core()
    backward_half(2, 0)
    sums.q00.x()
    sums.q10.x()
    sums.s.spread()
    sums.u3.gather()
    sums.u0.core_back()
    backward_half(2, 1)
    sums.q20.x()
    backward_end(2, 128, 0, ROWS)
    qkv_grad(0, 2, 128)
    sums.q02.core()
    qkv_grad(1, 2, 128)
    sums.q12.core()
    sums.s.gather()
    qkv_grad(2, 2, 128)
    sums.q22.core()
    og_cross()
    sums.q00.spread()
    backward_step(0, 3)
    sums.q10.spread()
    backward_end(3, 128, *BLOCKS[0])
    frames_part(0)
    backward_step(1, 3)
    sums.q20.spread()
    sums.q02.x()
    sums.q12.x()
    backward_end(3, 128, *BLOCKS[1])
    frames_part(1)
    sums.q00.gather()
    sums.q22.x()
    backward_step(2, 3)
    sums.u2.x_back()
    backward_end(3, 128, *BLOCKS[2])
    frames_part(2)
    sums.o.spread()
    backward_step(3, 3)
    backward_end(3, 128, *BLOCKS[3])
    qkv_grad(0, 3, 128)
    sums.q03.core()
    qkv_grad(1, 3, 128)
    sums.q13.core()
    qkv_grad(2, 3, 128)
    sums.q23.core()
    frames_part(3)
    tiny_core()
    sums.u3.x_back()
    sums.q20.gather()
    sums.q00.x_back()
    sums.q22.spread()
    tiny_x()
    sums.u2.core_back()
    sums.q02.spread()
    sums.q12.spread()
    sums.q03.x()
    sums.o.gather()
    tiny_z()
    sums.q13.x()
    sums.q02.gather()
    sums.q23.x()
    sums.q20.x_back()
    sums.u3.core_back()
    tiny_y()
    sums.q03.spread()
    sums.s.x_back()
    sums.q13.spread()
    sums.q10.gather()
    sums.q20.core_back()
    sums.o.x_back()
    sums.q23.spread()
    sums.q12.gather()
    sums.s.core_back()
    sums.q02.x_back()
    sums.q03.gather()
    sums.q13.gather()
    sums.q22.gather()
    sums.q10.x_back()
    sums.q02.core_back()
    sums.q23.gather()
    sums.q03.x_back()
    sums.q13.x_back()
    sums.q10.core_back()
    sums.q22.x_back()
    sums.q03.core_back()
    sums.q23.x_back()
    sums.q13.core_back()
    sums.o.core_back()
    sums.q12.x_back()
    sums.q22.core_back()
    sums.q23.core_back()
    sums.q00.core_back()
    sums.q12.core_back()
    frames_end(0)
    frames_end(1)
    frames_end(2)
    frames_end(3)
    tiny_end()
    for name in PARTS:
        vars(sums)[name].end()
    for i in range(4):
        f_out(i).wait()


def local_fused(
    frames,
    lengths,
    span_starts,
    mask_embedding,
    norm1_gain,
    norm1_bias,
    qkv_weight,
    qv_bias,
    out_weight,
    out_bias,
    norm2_gain,
    norm2_bias,
    up_weight,
    up_bias,
    down_weight,
    down_bias,
    head_weight,
    head_bias,
    logit_grad,
):
    inputs = dict(
        frames=frames,
        lengths=lengths,
        starts=span_starts,
        mask_embedding=mask_embedding,
        norm1_gain=norm1_gain,
        norm1_bias=norm1_bias,
        out_bias=out_bias,
        norm2_gain=norm2_gain,
        norm2_bias=norm2_bias,
        down_bias=down_bias,
        qv_bias=qv_bias,
        up_bias=up_bias,
        qkv_w=jnp.transpose(qkv_weight, (1, 0, 2)),
        out_w=out_weight,
        up_w=up_weight,
        down_w=down_weight,
        head_w=head_weight.T,
        head_b=head_bias,
        logit_grad=logit_grad.T,
    )
    outs = pl.pallas_call(
        fused,
        out_shape=[jax.ShapeDtypeStruct(o[0], o[1]) for o in OUTPUTS.values()],
        in_specs=[pl.BlockSpec(memory_space=m or pl.ANY) for m in INPUTS.values()],
        out_specs=[pl.BlockSpec(memory_space=o[2] or pl.ANY) for o in OUTPUTS.values()],
        scratch_shapes=[MEM(*item) for item in SCRATCH.values()]
        + [MEM(shape, bf16) for shape in landing_shapes()]
        + [pltpu.SemaphoreType.DMA((SEM_COUNT,)), pltpu.SemaphoreType.DMA((SEM_COUNT,))],
        compiler_params=pltpu.CompilerParams(
            collective_id=0, has_side_effects=True, vmem_limit_bytes=63 * 2**20
        ),
    )(*[inputs[name] for name in INPUTS])
    logits, frames_grad, up_o, out_o, qkv_o, small_o, tiny = outs
    wide = widen(frames_grad, up_o, out_o, qkv_o, small_o, tiny, head_weight.T)
    frames_grad, up_grad, out_grad, qkv_grad, down_grad, head_grad, qv_grad = wide[:7]
    up_bias_grad, down_bias_grad, head_bias_grad = wide[7:10]
    mask_grad, gain1_grad, bias1_grad, gain2_grad, bias2_grad, out_bias_grad = wide[10:]
    return (
        logits.T,
        frames_grad,
        mask_grad,
        gain1_grad,
        bias1_grad,
        jnp.transpose(qkv_grad.reshape(3, WIDTH, LOCAL), (1, 0, 2)),
        qv_grad,
        out_grad,
        out_bias_grad,
        gain2_grad,
        bias2_grad,
        up_grad,
        up_bias_grad,
        down_grad,
        down_bias_grad,
        head_grad.T,
        head_bias_grad,
    )


STEPS = 4


def widen_kernel(fg, uo, oo, qo, so, ti, hw, fg_w, u_w, o_w, q_w, d_w, hg, qv, ub, db, hb, *vectors):
    step = pl.program_id(0)
    fg_w[...] = fg[...].astype(f32)
    u_w[...] = uo[...].astype(f32)
    o_w[...] = oo[...].astype(f32)
    q_w[...] = qo[...].astype(f32)
    d_w[...] = dot_tn(so[aligned(step * 32, 32), :], hw[...])

    @pl.when(step == 0)
    def _():
        for j in range(2):
            cols = slice(j * 512, (j + 1) * 512)
            hg[:, cols] = so[128 + j * 32 : 160 + j * 32, :].astype(f32)
            qv[j : j + 1, :] = ti[8:9, cols]
        tail = so[224:240, :].astype(f32)
        for j in range(4):
            ub[pl.ds(j * 512, 512)] = tail[j : j + 1, :].reshape(512)
        hb[...] = tail[4:5, 0:CHARS].reshape(CHARS)
        grads = tail[4:5, 0:CHARS].reshape(CHARS, 1)
        db[...] = jnp.sum(hw[...].astype(f32) * grads, axis=0, keepdims=True).reshape(WIDTH)
        for number in range(3):
            vectors[number][...] = ti[number : number + 1, :].reshape(WIDTH)
        for number in range(3):
            for j in range(2):
                block = so[192 + j * 16 : 208 + j * 16, :].astype(f32)
                vectors[3 + number][pl.ds(j * 512, 512)] = block[3 + number : 4 + number, :].reshape(512)


def widen(frames_grad, up_o, out_o, qkv_o, small_o, tiny, head_t):
    def strip(array):
        return pl.BlockSpec((array.shape[0] // STEPS, array.shape[1]), lambda i: (i, 0))

    def whole(*shape):
        return pl.BlockSpec(shape, lambda i: (0,) * len(shape))

    def shaped(*shape):
        return jax.ShapeDtypeStruct(shape, f32)

    large = (frames_grad, up_o, out_o, qkv_o)
    down = shaped(FFL, WIDTH)
    rest = [shaped(CHARS, WIDTH), shaped(2, LOCAL), shaped(FFL), shaped(WIDTH), shaped(CHARS)]
    rest += [shaped(WIDTH)] * 6
    return pl.pallas_call(
        widen_kernel,
        grid=(STEPS,),
        out_shape=[shaped(*a.shape) for a in large] + [down] + rest,
        in_specs=[strip(a) for a in large]
        + [whole(*small_o.shape), whole(*tiny.shape), whole(*head_t.shape)],
        out_specs=[strip(a) for a in large] + [strip(down)] + [whole(*r.shape) for r in rest],
        compiler_params=pltpu.CompilerParams(vmem_limit_bytes=60 * 2**20),
    )(*large, small_o, tiny, head_t)


def solution(mesh):
    placed = (
        P("dp", None),
        P("dp"),
        P("dp", None),
        P(),
        P(),
        P(),
        P(None, None, "tensor"),
        P(None, "tensor"),
        P("tensor", None),
        P(),
        P(),
        P(),
        P(None, "tensor"),
        P("tensor"),
        P("tensor", None),
        P(),
        P(),
        P(),
        P("dp", None),
    )
    fits = mesh.shape["dp"] == 16 and mesh.shape["tensor"] == 2
    return jax.shard_map(
        local_fused if fits else local,
        mesh=mesh,
        in_specs=placed,
        out_specs=(
            P("dp", None),
            P("dp", None),
            P(),
            P(),
            P(),
            P(None, None, "tensor"),
            P(None, "tensor"),
            P("tensor", None),
            P(),
            P(),
            P(),
            P(None, "tensor"),
            P("tensor"),
            P("tensor", None),
            P(),
            P(),
            P(),
        ),
        check_vma=False,
    )
```
